32 devices in a mesh: expert: 16 (over z, y, x), tensor: 2 (over core).
Axes of the slice: x: 2, y: 2, z: 4, core: 2. Of those that a mesh axis runs over, the one named last changes fastest.
Arguments:
- inputs: bfloat16 [4096, 2048], P(('expert', 'tensor')), may hold values from -6 to 6
- norm_attn: float32 [2048], replicated, may hold values from 0.5 to 1.5
- w_query: bfloat16 [2048, 3072], P(None, 'tensor'), may hold values from -0.125 to 0.125
- w_latent: bfloat16 [2048, 576], replicated, may hold values from -0.125 to 0.125
- norm_latent: float32 [512], replicated, may hold values from 0.5 to 1.5
- w_expand: bfloat16 [512, 4096], P(None, 'tensor'), may hold values from -0.25 to 0.25
- w_output: bfloat16 [2048, 2048], P(None, 'tensor'), may hold values from -1 to 1
- norm_moe: float32 [2048], replicated, may hold values from 0.5 to 1.5
- w_router: bfloat16 [2048, 32], replicated, may hold values from -0.0625 to 0.0625
- w_shared_gate: bfloat16 [2048, 2816], P(None, 'tensor'), may hold values from -0.125 to 0.125
- w_shared_up: bfloat16 [2048, 2816], P(None, 'tensor'), may hold values from -0.125 to 0.125
- w_shared_down: bfloat16 [2048, 2816], P(None, 'tensor'), may hold values from -0.21875 to 0.21875
- w_expert_gate: bfloat16 [32, 2048, 1408], P('expert', None, 'tensor'), may hold values from -0.125 to 0.125
- w_expert_up: bfloat16 [32, 2048, 1408], P('expert', None, 'tensor'), may hold values from -0.125 to 0.125
- w_expert_down: bfloat16 [32, 2048, 1408], P('expert', None, 'tensor'), may hold values from -0.3125 to 0.3125
- routes: int32 [4096, 6], P(('expert', 'tensor')), may hold values from 0 to 31, all different within a row; in each aligned block of 128 rows (0 to 127, 128 to 255, ...) at most 32 rows name the same one
- cotangent: bfloat16 [4096, 2048], P(('expert', 'tensor')), may hold values from -6 to 6
Outputs:
- output: bfloat16 [4096, 2048], P(('expert', 'tensor'))
- grad_inputs: float32 [4096, 2048], P(('expert', 'tensor'))
- grad_norm_attn: float32 [2048], P(('expert', 'tensor'))
- grad_query: float32 [2048, 3072], P('expert', 'tensor')
- grad_latent: float32 [2048, 576], P(('expert', 'tensor'))
- grad_norm_latent: float32 [512], P(('expert', 'tensor'))
- grad_expand: float32 [512, 4096], P('expert', 'tensor')
- grad_output: float32 [2048, 2048], P('expert', 'tensor')
- grad_norm_moe: float32 [2048], P(('expert', 'tensor'))
- grad_router: float32 [2048, 32], P(('expert', 'tensor'))
- grad_shared_gate: float32 [2048, 2816], P('expert', 'tensor')
- grad_shared_up: float32 [2048, 2816], P('expert', 'tensor')
- grad_shared_down: float32 [2048, 2816], P('expert', 'tensor')
- grad_expert_gate: float32 [32, 2048, 1408], P('expert', None, 'tensor')
- grad_expert_up: float32 [32, 2048, 1408], P('expert', None, 'tensor')
- grad_expert_down: float32 [32, 2048, 1408], P('expert', None, 'tensor')
The draws below stay inside these ranges and needn't reach their ends.
Inputs may be any that keep to these rules, and one draw needn't show every extreme that they name: `routes`: each row names 6 different experts; among the 128 rows of one device no expert is named by more than 32 rows, and in every draw some expert is named by exactly 32 rows of some device.
All inputs are finite; a program needn't handle non-finite values.
Results may differ from the reference program's by a relative error of at most 0.025.
Values may be sent and summed in bfloat16 or wider, within the bound.
A program may use at most 320 MiB of HBM per device.

```python
import math
import jax
import jax.numpy as jnp
import numpy as np
from jax import lax

D = 2048
HEADS = 16
NOPE = 128
ROPE = 64
VD = 128
LATENT = 512
FF = 1408
SHARED_FF = 2816
TOPK = 6
TOK_DEV = 128
SEQ = 256
TOKENS = 4096
EXPERTS = 32
CAP = 32
N_TENSOR = 2


def steps_of(own_key, dims, split, least, largest):
    def one(dim, shards_of):
        draws = jax.random.uniform(jax.random.fold_in(jax.random.fold_in(own_key, 6), dim), (shards_of,), jnp.float32, least / len(split), largest / len(split))
        return jnp.repeat(jnp.exp(draws), dims[dim] // shards_of).reshape((-1,) + (1,) * (len(dims) - dim - 1))

    loudness = one(*split[0])
    for cut in split[1:]:
        loudness = loudness * one(*cut)
    return loudness


def deal_out(own_key, own, number, rows, number_of, top, reach, lean):
    order = jax.random.permutation(own_key, number_of)
    crowded, usual = portions_of(number_of, rows * top, reach, lean, True), portions_of(number_of, rows * top, reach, lean, False)
    places = jnp.arange(number_of)

    def named(sizes, offset_by):
        used = int((sizes > 0).sum())
        fixed = max(1, used // 4)
        moved = fixed + (places - fixed + offset_by * (used - fixed)) % max(1, number_of - fixed)
        return jnp.zeros((number_of,), jnp.int32).at[order[jnp.where(places < fixed, places, moved)]].set(jnp.asarray(sizes, jnp.int32))

    sizes = jnp.where(number % 4 == 0, named(crowded, number // 4), named(usual, number - number // 4 - 1))
    mixed = jax.random.permutation(jax.random.fold_in(own, 3), number_of)
    source_of, sink = mixed[0:number_of // 2 * 2:2], mixed[1:number_of // 2 * 2:2]
    room = jnp.minimum(sizes[source_of] - 1, reach - sizes[sink]) // 2
    room = jnp.where((source_of == order[0]) | (sink == order[0]) | (sizes[sink] == 0), 0, jnp.maximum(room, 0))
    moved = jax.random.randint(jax.random.fold_in(own, 4), (number_of // 2,), 0, 1 << 20) % (room + 1)
    sizes = sizes.at[source_of].add(-moved).at[sink].add(moved)
    members = jnp.searchsorted(jnp.cumsum(sizes), jnp.arange(rows * top), side="right").astype(jnp.int32)
    listing = members.reshape(top, rows).T
    listing = listing[jax.random.permutation(jax.random.fold_in(own, 1), rows)]
    offset_by = jax.random.randint(jax.random.fold_in(own, 2), (rows, 1), 0, top)
    return jnp.take_along_axis(listing, (jnp.arange(top)[None, :] + offset_by) % top, axis=1)


def portions_of(number_of, total, most, skew, full):
    weights = [(1 << 20) // math.isqrt(rank ** skew) + 1 for rank in range(1, number_of + 1)]
    largest = most if full else min(most, max(-(-total // number_of), total * weights[0] // sum(weights)))
    least = 1 if total - largest >= number_of - 1 else 0
    given, spare = [largest] + [least] * (number_of - 1), total - largest - least * (number_of - 1)
    while spare > 0:
        movable = [i for i in range(1, number_of) if given[i] < largest] or [i for i in range(1, number_of) if given[i] < most]
        whole, remaining = sum([weights[i] for i in movable]), spare
        for i in movable:
            addition = min(most - given[i], max(1, remaining * weights[i] // whole), spare)
            given[i] = given[i] + addition
            spare = spare - addition
    return np.array(given)


def bell_draw(key, shape, deviation, reach, split=(), kind=jnp.bfloat16):
    factor_of = steps_of(key, shape, split, -0.22, 0.18) if split else 1.0
    entries = jax.random.normal(key, shape, jnp.float32) * deviation * factor_of
    return jnp.minimum(jnp.maximum(entries, -reach), reach).astype(kind)


def setup_inputs(seed: int = 0) -> dict:
    keys = jax.random.split(jax.random.key(seed), 18)
    inputs = bell_draw(keys[0], (TOKENS, D), 1.0, 6.0, ((0, 32),))
    norm_attn = jnp.clip(1.0 + 0.1 * jax.random.normal(keys[1], (D,), jnp.float32), 0.5, 1.5)
    w_query = bell_draw(keys[2], (D, HEADS * (NOPE + ROPE)), D ** -0.5, 0.125, ((1, 2),))
    w_latent = bell_draw(keys[3], (D, LATENT + ROPE), D ** -0.5, 0.125)
    norm_latent = jnp.clip(1.0 + 0.1 * jax.random.normal(keys[4], (LATENT,), jnp.float32), 0.5, 1.5)
    w_expand = bell_draw(keys[5], (LATENT, HEADS * (NOPE + VD)), LATENT ** -0.5, 0.25, ((1, 2),))
    w_output = bell_draw(keys[6], (D, HEADS * VD), (HEADS * VD // 64) ** -0.5, 1.0, ((1, 2),))
    norm_moe = jnp.clip(1.0 + 0.1 * jax.random.normal(keys[7], (D,), jnp.float32), 0.5, 1.5)
    w_router = bell_draw(keys[8], (D, EXPERTS), (4 * D) ** -0.5, 0.0625)
    w_shared_gate = bell_draw(keys[9], (D, SHARED_FF), D ** -0.5, 0.125, ((1, 2),))
    w_shared_up = bell_draw(keys[10], (D, SHARED_FF), D ** -0.5, 0.125, ((1, 2),))
    w_shared_down = bell_draw(keys[11], (D, SHARED_FF), (SHARED_FF // 4) ** -0.5, 0.21875, ((1, 2),))
    w_expert_gate = bell_draw(keys[12], (EXPERTS, D, FF), D ** -0.5, 0.125, ((0, 16), (2, 2)))
    w_expert_up = bell_draw(keys[13], (EXPERTS, D, FF), D ** -0.5, 0.125, ((0, 16), (2, 2)))
    w_expert_down = bell_draw(keys[14], (EXPERTS, D, FF), (FF // 4) ** -0.5, 0.3125, ((0, 16), (2, 2)))
    routes_keys = jax.random.split(jax.random.fold_in(keys[15], 1), TOKENS // TOK_DEV)
    routes_turns = jax.random.permutation(jax.random.fold_in(keys[15], 3), TOKENS // TOK_DEV)
    routes = jax.vmap(lambda own, number: deal_out(jax.random.fold_in(keys[15], 2), own, number, TOK_DEV, EXPERTS, TOPK, CAP, 1))(routes_keys, routes_turns).reshape((TOKENS, TOPK))
    cotangent = bell_draw(keys[16], (TOKENS, D), 1.0, 6.0, ((0, 32),))
    return {"inputs": inputs, "norm_attn": norm_attn, "w_query": w_query, "w_latent": w_latent, "norm_latent": norm_latent, "w_expand": w_expand, "w_output": w_output, "norm_moe": norm_moe, "w_router": w_router, "w_shared_gate": w_shared_gate, "w_shared_up": w_shared_up, "w_shared_down": w_shared_down, "w_expert_gate": w_expert_gate, "w_expert_up": w_expert_up, "w_expert_down": w_expert_down, "routes": routes, "cotangent": cotangent}


@jax.custom_vjp
def low(v):
    return lax.optimization_barrier(v.astype(jnp.bfloat16)).astype(jnp.float32)

@jax.custom_vjp
def low_back(v):
    return v

def low_keep(v):
    return (low(v), None)

def low_pass(kept, grad):
    return (grad,)

def back_keep(v):
    return (v, None)

def back_low(kept, grad):
    return (low(grad),)
low.defvjp(low_keep, low_pass)
low_back.defvjp(back_keep, back_low)
HIGHEST = lax.Precision.HIGHEST
EPS = 1e-06

def matmul(left, right):
    return jnp.dot(left, right, precision=HIGHEST)

def rms_scale(values):
    return lax.rsqrt(lax.optimization_barrier(jnp.mean(values * values, axis=-1, keepdims=True)) + EPS)

def rotary(values, positions):
    width = values.shape[-1]
    half = width // 2
    freq = 10000.0 ** (-(jnp.arange(half, dtype=jnp.float32) * 2.0) / width)
    angle = positions.astype(jnp.float32)[:, None] * freq[None, :]
    cosine = jnp.cos(angle)
    sine = jnp.sin(angle)
    if values.ndim == 3:
        cosine = cosine[:, None, :]
        sine = sine[:, None, :]
    first = values[..., :half]
    second = values[..., half:]
    return jnp.concatenate([first * cosine - second * sine, first * sine + second * cosine], axis=-1)

def attend(query, key, value):
    length = query.shape[0]
    scores = jnp.einsum('qhd,khd->hqk', query, key, precision=HIGHEST) * (1.0 / math.sqrt(NOPE + ROPE))
    scores = low_back(scores)
    places = jnp.arange(length, dtype=jnp.int32)
    causal = places[None, :, None] >= places[None, None, :]
    scores = jnp.where(causal, scores, -1e+30)
    probs = low(jax.nn.softmax(scores, axis=-1))
    return jnp.einsum('hqk,khd->qhd', probs, value, precision=HIGHEST)

def attend_item(item):
    return attend(item[0], item[1], item[2])

def expert_apply(rows, w_gate, w_up, w_down):
    width = w_gate.shape[1] // N_TENSOR
    total = jnp.zeros(rows.shape, jnp.float32)
    for block_index in range(N_TENSOR):
        first = block_index * width
        own = low_back(rows)
        gate_act = low_back(matmul(own, w_gate[:, first:first + width]))
        up_act = low_back(matmul(own, w_up[:, first:first + width]))
        hidden = low(jax.nn.silu(gate_act) * up_act)
        total = total + low(jnp.dot(hidden, w_down[:, first:first + width].T, precision=HIGHEST))
    return low_back(total)

def expert_item(item):
    return expert_apply(item[0], item[1], item[2], item[3])

def place_table(routes):
    blocks = routes.reshape(-1, TOK_DEV * TOPK)
    expert_ids = jnp.arange(EXPERTS, dtype=jnp.int32)
    hot = (blocks[:, :, None] == expert_ids[None, None, :]).astype(jnp.int32)
    earlier = jnp.cumsum(hot, axis=1, dtype=jnp.int32) - hot
    place = lax.optimization_barrier(jnp.sum(earlier * hot, axis=2, dtype=jnp.int32))
    return blocks * CAP + place

def layer(inputs, norm_attn, w_query, w_latent, norm_latent, w_expand, w_output, norm_moe, w_router, w_shared_gate, w_shared_up, w_shared_down, w_expert_gate, w_expert_up, w_expert_down, routes):
    positions = jnp.arange(TOKENS, dtype=jnp.int32) % SEQ
    normed = low(inputs * rms_scale(inputs) * norm_attn)
    query_raw = low_back(matmul(normed, w_query)).reshape(TOKENS, HEADS, NOPE + ROPE)
    query = low(jnp.concatenate([query_raw[..., :NOPE], rotary(query_raw[..., NOPE:], positions)], axis=-1))
    compressed = low_back(matmul(normed, w_latent))
    lat_raw = compressed[:, :LATENT]
    latent = low(lat_raw * rms_scale(lat_raw) * norm_latent)
    key_rope = low(rotary(compressed[:, LATENT:], positions))
    expanded = low(low_back(matmul(latent, w_expand))).reshape(TOKENS, HEADS, NOPE + VD)
    key = jnp.concatenate([expanded[..., :NOPE], jnp.broadcast_to(key_rope[:, None, :], (TOKENS, HEADS, ROPE))], axis=-1)
    value = expanded[..., NOPE:]
    nseq = TOKENS // SEQ
    attended = lax.map(jax.checkpoint(attend_item), (query.reshape(nseq, SEQ, HEADS, NOPE + ROPE), key.reshape(nseq, SEQ, HEADS, NOPE + ROPE), value.reshape(nseq, SEQ, HEADS, VD)))
    attended = low(low_back(attended.reshape(TOKENS, HEADS * VD)))
    after_attn = inputs + low_back(jnp.dot(attended, w_output.T, precision=HIGHEST))
    h_moe = low(after_attn * rms_scale(after_attn) * norm_moe)
    logits = low_back(matmul(h_moe, w_router))
    gates = jax.nn.softmax(jnp.take_along_axis(logits, routes, axis=1), axis=-1)
    blocks_count = TOKENS // TOK_DEV
    slots = place_table(routes)
    block_ids = jnp.arange(blocks_count, dtype=jnp.int32)[:, None]
    source = jnp.repeat(h_moe.reshape(blocks_count, TOK_DEV, D), TOPK, axis=1)
    grid = jnp.zeros((blocks_count, EXPERTS * CAP, D), jnp.float32).at[block_ids, slots].add(source)
    per_expert = grid.reshape(blocks_count, EXPERTS, CAP, D).transpose(1, 0, 2, 3).reshape(EXPERTS, blocks_count * CAP, D)
    results = lax.map(jax.checkpoint(expert_item), (per_expert, w_expert_gate, w_expert_up, w_expert_down))
    back = results.reshape(EXPERTS, blocks_count, CAP, D).transpose(1, 0, 2, 3).reshape(blocks_count, EXPERTS * CAP, D)
    picked = back[block_ids, slots].reshape(TOKENS, TOPK, D)
    routed = lax.optimization_barrier(jnp.sum(gates[:, :, None] * picked, axis=1))
    shared = expert_apply(h_moe, w_shared_gate, w_shared_up, w_shared_down)
    return after_attn + routed + shared

def reference(inputs, norm_attn, w_query, w_latent, norm_latent, w_expand, w_output, norm_moe, w_router, w_shared_gate, w_shared_up, w_shared_down, w_expert_gate, w_expert_up, w_expert_down, routes, cotangent):
    floats = tuple((item.astype(jnp.float32) for item in (inputs, norm_attn, w_query, w_latent, norm_latent, w_expand, w_output, norm_moe, w_router, w_shared_gate, w_shared_up, w_shared_down, w_expert_gate, w_expert_up, w_expert_down)))

    def forward(*params):
        return layer(*params, routes)
    result, pull = jax.vjp(forward, *floats)
    grads = pull(cotangent.astype(jnp.float32))
    return (result.astype(jnp.bfloat16), grads[0], grads[1], grads[2], grads[3], grads[4], grads[5], grads[6], grads[7], grads[8], grads[9], grads[10], grads[11], grads[12], grads[13], grads[14])
```

```python
import functools
import math

import jax
import jax.numpy as jnp
from jax import lax
from jax.experimental import pallas as pl
from jax.experimental.pallas import tpu as pltpu
from jax.sharding import PartitionSpec as P

EXPERT = "expert"
TENSOR = "tensor"
NOPE = 128
ROPE = 64
VD = 128
LATENT = 512
TOPK = 6


EPS = 1e-06


def rope_tables(positions, width):
    half = width // 2
    freq = 10000.0 ** (-(jnp.arange(half, dtype=jnp.float32) * 2.0) / width)
    angle = positions.astype(jnp.float32)[:, None] * freq[None, :]
    return (jnp.cos(angle), jnp.sin(angle))


def rotate(values, cosine, sine):
    half = values.shape[-1] // 2
    first = values[..., :half]
    second = values[..., half:]
    return jnp.concatenate(
        [first * cosine - second * sine, first * sine + second * cosine], axis=-1
    )


def unrotate(grads, cosine, sine):
    half = grads.shape[-1] // 2
    first = grads[..., :half]
    second = grads[..., half:]
    return jnp.concatenate(
        [first * cosine + second * sine, second * cosine - first * sine], axis=-1
    )


def norm_back(grad_out, normed, scale, gain):
    scaled = grad_out * gain
    grad_in = scale * (scaled - normed * jnp.mean(scaled * normed, axis=-1, keepdims=True))
    return (grad_in, jnp.sum(grad_out * normed, axis=0))


def masked_scores(rows_query, key_full, first_row, scale):
    block = rows_query.shape[0]
    scores = (
        jnp.einsum("qhd,khd->hqk", rows_query, key_full, preferred_element_type=jnp.float32) * scale
    )
    allowed = (first_row + jnp.arange(block))[:, None] >= jnp.arange(key_full.shape[0])[None, :]
    return jnp.where(allowed[None], scores, -1e30)


def attention_forward(query, key_full, value, scale):
    seq_rows = query.shape[0]
    block = min(seq_rows, 512)

    def one_block(index):
        first_row = index * block
        scores = masked_scores(query, key_full, first_row, scale)
        peak = jnp.max(scores, axis=-1, keepdims=True)
        weights = jnp.exp(scores - peak)
        total = jnp.sum(weights, axis=-1, keepdims=True)
        probs = (weights / total).astype(jnp.bfloat16)
        result = jnp.einsum("hqk,khd->qhd", probs, value, preferred_element_type=jnp.float32)
        return (result.astype(jnp.bfloat16), (peak + jnp.log(total))[..., 0])

    results, log_totals = lax.map(one_block, jnp.arange(seq_rows // block))
    return (results.reshape(seq_rows, query.shape[1], value.shape[2]), log_totals)


def attention_backward(query, key_full, value, grad_attended, log_totals, scale):
    seq_rows = query.shape[0]
    block = min(seq_rows, 512)

    def one_block(carry, index):
        grad_key, grad_value = carry
        first_row = index * block
        scores = masked_scores(query, key_full, first_row, scale)
        probs = jnp.exp(scores - log_totals[index][..., None])
        grad_probs = jnp.einsum(
            "qhv,khv->hqk", grad_attended, value, preferred_element_type=jnp.float32
        )
        centre = jnp.sum(probs * grad_probs, axis=-1, keepdims=True)
        grad_scores = (probs * (grad_probs - centre)).astype(jnp.bfloat16)
        grad_rows = (
            jnp.einsum("hqk,khd->qhd", grad_scores, key_full, preferred_element_type=jnp.float32)
            * scale
        )
        grad_key = (
            grad_key
            + jnp.einsum("hqk,qhd->khd", grad_scores, query, preferred_element_type=jnp.float32)
            * scale
        )
        grad_value = grad_value + jnp.einsum(
            "hqk,qhv->khv",
            probs.astype(jnp.bfloat16),
            grad_attended,
            preferred_element_type=jnp.float32,
        )
        return ((grad_key, grad_value), grad_rows)

    start_key = jnp.zeros(key_full.shape, jnp.float32)
    start_value = jnp.zeros(value.shape, jnp.float32)
    (grad_key, grad_value), grad_query = lax.scan(
        one_block, (start_key, start_value), jnp.arange(seq_rows // block)
    )
    return (grad_query.reshape(query.shape), grad_key, grad_value)


def to_experts(grid, rows):
    gathered, rows_all = (
        lax.all_gather(grid, TENSOR, axis=0, tiled=True),
        lax.all_gather(rows, TENSOR, axis=0, tiled=True),
    )
    received = lax.all_to_all(gathered, EXPERT, split_axis=1, concat_axis=1, tiled=True)
    return (received, rows_all)


def from_experts(expert_part, shared_part):
    returned = lax.all_to_all(expert_part, EXPERT, split_axis=1, concat_axis=1, tiled=True)
    summed, shared_sum = (
        lax.psum_scatter(returned, TENSOR, scatter_dimension=0, tiled=True).astype(jnp.float32),
        lax.psum_scatter(shared_part, TENSOR, scatter_dimension=0, tiled=True).astype(
            jnp.float32
        ),
    )
    return (summed, shared_sum)


def per_device_exchanged(
    inputs,
    norm_attn,
    w_query,
    w_latent,
    norm_latent,
    w_expand,
    w_output,
    norm_moe,
    w_router,
    w_shared_gate,
    w_shared_up,
    w_shared_down,
    w_expert_gate,
    w_expert_up,
    w_expert_down,
    routes,
    cotangent,
):
    own_rows = inputs.shape[0]
    width = inputs.shape[1]
    tensor_size = lax.axis_size(TENSOR)
    expert_size = lax.axis_size(EXPERT)
    tensor_index = lax.axis_index(TENSOR)
    seq_rows = own_rows * tensor_size
    local_heads = w_query.shape[1] // (NOPE + ROPE)
    experts = w_router.shape[1]
    local_experts = experts // expert_size
    capacity = own_rows * TOPK * 4 // (3 * experts)
    scale = 1.0 / math.sqrt(NOPE + ROPE)
    flat_in = inputs.astype(jnp.float32)
    scale_one = lax.rsqrt(jnp.mean(flat_in * flat_in, axis=-1, keepdims=True) + EPS)
    normed_one = flat_in * scale_one
    h_own = (normed_one * norm_attn).astype(jnp.bfloat16)
    compressed = jnp.dot(h_own, w_latent, preferred_element_type=jnp.float32)
    lat_raw = compressed[:, :LATENT]
    scale_lat = lax.rsqrt(jnp.mean(lat_raw * lat_raw, axis=-1, keepdims=True) + EPS)
    normed_lat = lat_raw * scale_lat
    lat_own = (normed_lat * norm_latent).astype(jnp.bfloat16)
    cos_own, sin_own = rope_tables(tensor_index * own_rows + jnp.arange(own_rows), ROPE)
    rope_own = rotate(compressed[:, LATENT:], cos_own, sin_own).astype(jnp.bfloat16)
    h_all, lat_all, rope_all = (
        lax.all_gather(h_own, TENSOR, axis=0, tiled=True),
        lax.all_gather(lat_own, TENSOR, axis=0, tiled=True),
        lax.all_gather(rope_own, TENSOR, axis=0, tiled=True),
    )
    cos_all, sin_all = rope_tables(jnp.arange(seq_rows), ROPE)
    cos_all = cos_all[:, None, :]
    sin_all = sin_all[:, None, :]
    query_raw = jnp.dot(h_all, w_query, preferred_element_type=jnp.float32).reshape(
        seq_rows, local_heads, NOPE + ROPE
    )
    query = jnp.concatenate(
        [query_raw[..., :NOPE], rotate(query_raw[..., NOPE:], cos_all, sin_all)], axis=-1
    ).astype(jnp.bfloat16)
    expanded = jnp.dot(lat_all, w_expand, preferred_element_type=jnp.float32).astype(jnp.bfloat16)
    expanded = expanded.reshape(seq_rows, local_heads, NOPE + VD)
    key_full = jnp.concatenate(
        [
            expanded[..., :NOPE],
            jnp.broadcast_to(rope_all[:, None, :], (seq_rows, local_heads, ROPE)),
        ],
        axis=-1,
    )
    value = expanded[..., NOPE:]
    attended, log_totals = attention_forward(query, key_full, value, scale)
    attended_flat = attended.reshape(seq_rows, local_heads * VD)
    attn_terms = jnp.einsum(
        "sv,dv->sd", attended_flat, w_output, preferred_element_type=jnp.float32
    )
    after_attn = flat_in + lax.psum_scatter(
        attn_terms.astype(jnp.bfloat16), TENSOR, scatter_dimension=0, tiled=True
    ).astype(jnp.float32)
    scale_two = lax.rsqrt(jnp.mean(after_attn * after_attn, axis=-1, keepdims=True) + EPS)
    normed_two = after_attn * scale_two
    h_moe = (normed_two * norm_moe).astype(jnp.bfloat16)
    logits = jnp.dot(h_moe, w_router, preferred_element_type=jnp.float32)
    expert_ids = jnp.arange(experts, dtype=jnp.int32)
    route_hot = (routes[:, :, None] == expert_ids[None, None, :]).astype(jnp.float32)
    gates = jax.nn.softmax(jnp.sum(route_hot * logits[:, None, :], axis=-1), axis=-1)
    flat_routes = routes.reshape(-1)
    pair_hot = (flat_routes[:, None] == expert_ids[None, :]).astype(jnp.int32)
    earlier = jnp.cumsum(pair_hot, axis=0, dtype=jnp.int32) - pair_hot
    slots = jnp.sum(earlier * pair_hot, axis=1, dtype=jnp.int32) * experts + flat_routes
    grid_shape = (capacity, expert_size, local_experts, width)

    def to_slots(pair_rows):
        placed = jnp.zeros((capacity * experts, width), jnp.bfloat16).at[slots].set(pair_rows)
        return placed.reshape(grid_shape)

    def from_slots(grid):
        return grid.reshape(capacity * experts, width)[slots].reshape(own_rows, TOPK, width)

    received, h_moe_all = to_experts(to_slots(jnp.repeat(h_moe, TOPK, axis=0)), h_moe)
    gate_act = jnp.einsum(
        "cnjd,jdf->cnjf", received, w_expert_gate, preferred_element_type=jnp.float32
    )
    up_act = jnp.einsum("cnjd,jdf->cnjf", received, w_expert_up, preferred_element_type=jnp.float32)
    hidden = (jax.nn.silu(gate_act) * up_act).astype(jnp.bfloat16)
    expert_part = jnp.einsum(
        "cnjf,jdf->cnjd", hidden, w_expert_down, preferred_element_type=jnp.float32
    ).astype(jnp.bfloat16)
    shared_gate_act = jnp.dot(h_moe_all, w_shared_gate, preferred_element_type=jnp.float32)
    shared_up_act = jnp.dot(h_moe_all, w_shared_up, preferred_element_type=jnp.float32)
    shared_hidden = (jax.nn.silu(shared_gate_act) * shared_up_act).astype(jnp.bfloat16)
    shared_part = jnp.einsum(
        "sf,df->sd", shared_hidden, w_shared_down, preferred_element_type=jnp.float32
    ).astype(jnp.bfloat16)
    expert_out, shared_out = from_experts(expert_part, shared_part)
    picked = from_slots(expert_out)
    output = (after_attn + jnp.sum(gates[:, :, None] * picked, axis=1) + shared_out).astype(
        jnp.bfloat16
    )
    grad_out = cotangent.astype(jnp.float32)
    grad_gates = jnp.sum(picked * grad_out[:, None, :], axis=-1)
    grad_select = gates * (grad_gates - jnp.sum(gates * grad_gates, axis=-1, keepdims=True))
    grad_logits = jnp.sum(grad_select[:, :, None] * route_hot, axis=1).astype(jnp.bfloat16)
    grad_router = jnp.einsum("td,te->de", h_moe, grad_logits, preferred_element_type=jnp.float32)
    pair_grads = (
        (gates[:, :, None] * grad_out[:, None, :])
        .astype(jnp.bfloat16)
        .reshape(own_rows * TOPK, width)
    )
    grad_received, cot_all = to_experts(to_slots(pair_grads), cotangent)
    grad_hidden = jnp.einsum(
        "cnjd,jdf->cnjf", grad_received, w_expert_down, preferred_element_type=jnp.float32
    )
    sigma = jax.nn.sigmoid(gate_act)
    grad_up = (grad_hidden * gate_act * sigma).astype(jnp.bfloat16)
    grad_gate = (grad_hidden * up_act * sigma * (1.0 + gate_act * (1.0 - sigma))).astype(
        jnp.bfloat16
    )
    grad_expert_down = jnp.einsum(
        "cnjd,cnjf->jdf", grad_received, hidden, preferred_element_type=jnp.float32
    )
    grad_expert_gate = jnp.einsum(
        "cnjd,cnjf->jdf", received, grad_gate, preferred_element_type=jnp.float32
    )
    grad_expert_up = jnp.einsum(
        "cnjd,cnjf->jdf", received, grad_up, preferred_element_type=jnp.float32
    )
    grad_rows_part = (
        jnp.einsum("cnjf,jdf->cnjd", grad_gate, w_expert_gate, preferred_element_type=jnp.float32)
        + jnp.einsum("cnjf,jdf->cnjd", grad_up, w_expert_up, preferred_element_type=jnp.float32)
    ).astype(jnp.bfloat16)
    shared_grad_hidden = jnp.einsum(
        "sd,df->sf", cot_all, w_shared_down, preferred_element_type=jnp.float32
    )
    shared_sigma = jax.nn.sigmoid(shared_gate_act)
    shared_grad_up = (shared_grad_hidden * shared_gate_act * shared_sigma).astype(jnp.bfloat16)
    shared_grad_gate = (
        shared_grad_hidden
        * shared_up_act
        * shared_sigma
        * (1.0 + shared_gate_act * (1.0 - shared_sigma))
    ).astype(jnp.bfloat16)
    grad_shared_down = jnp.einsum(
        "sd,sf->df", cot_all, shared_hidden, preferred_element_type=jnp.float32
    )
    grad_shared_gate = jnp.einsum(
        "sd,sf->df", h_moe_all, shared_grad_gate, preferred_element_type=jnp.float32
    )
    grad_shared_up = jnp.einsum(
        "sd,sf->df", h_moe_all, shared_grad_up, preferred_element_type=jnp.float32
    )
    shared_rows_part = (
        jnp.einsum("sf,df->sd", shared_grad_gate, w_shared_gate, preferred_element_type=jnp.float32)
        + jnp.einsum("sf,df->sd", shared_grad_up, w_shared_up, preferred_element_type=jnp.float32)
    ).astype(jnp.bfloat16)
    grad_rows, grad_shared_rows = from_experts(grad_rows_part, shared_rows_part)
    grad_moe = (
        jnp.sum(from_slots(grad_rows), axis=1)
        + grad_shared_rows
        + jnp.einsum("te,de->td", grad_logits, w_router, preferred_element_type=jnp.float32)
    )
    grad_mid, grad_norm_moe = norm_back(grad_moe, normed_two, scale_two, norm_moe)
    grad_mid = grad_mid + grad_out
    grad_attn = grad_mid.astype(jnp.bfloat16)
    grad_attn_all = lax.all_gather(grad_attn, TENSOR, axis=0, tiled=True)
    grad_output = jnp.einsum(
        "sd,sv->dv", grad_attn_all, attended_flat, preferred_element_type=jnp.float32
    )
    grad_attended = jnp.einsum(
        "sd,dv->sv", grad_attn_all, w_output, preferred_element_type=jnp.float32
    )
    grad_attended = grad_attended.astype(jnp.bfloat16).reshape(seq_rows, local_heads, VD)
    grad_query_full, grad_key_full, grad_value = attention_backward(
        query, key_full, value, grad_attended, log_totals, scale
    )
    grad_query_raw = jnp.concatenate(
        [grad_query_full[..., :NOPE], unrotate(grad_query_full[..., NOPE:], cos_all, sin_all)],
        axis=-1,
    )
    grad_query_raw = grad_query_raw.astype(jnp.bfloat16).reshape(
        seq_rows, local_heads * (NOPE + ROPE)
    )
    grad_query = jnp.einsum("sd,sq->dq", h_all, grad_query_raw, preferred_element_type=jnp.float32)
    grad_expanded = jnp.concatenate([grad_key_full[..., :NOPE], grad_value], axis=-1)
    grad_expanded = grad_expanded.astype(jnp.bfloat16).reshape(seq_rows, local_heads * (NOPE + VD))
    grad_expand = jnp.einsum(
        "sl,sk->lk", lat_all, grad_expanded, preferred_element_type=jnp.float32
    )
    grad_rope_part = jnp.sum(grad_key_full[..., NOPE:], axis=1)
    grad_h_part = jnp.einsum(
        "sq,dq->sd", grad_query_raw, w_query, preferred_element_type=jnp.float32
    )
    grad_lat_part = jnp.einsum(
        "sk,lk->sl", grad_expanded, w_expand, preferred_element_type=jnp.float32
    )
    grad_h_own, grad_lat_own, grad_rope_own = (
        lax.psum_scatter(
            grad_h_part.astype(jnp.bfloat16), TENSOR, scatter_dimension=0, tiled=True
        ).astype(jnp.float32),
        lax.psum_scatter(
            grad_lat_part.astype(jnp.bfloat16), TENSOR, scatter_dimension=0, tiled=True
        ).astype(jnp.float32),
        lax.psum_scatter(
            grad_rope_part.astype(jnp.bfloat16), TENSOR, scatter_dimension=0, tiled=True
        ).astype(jnp.float32),
    )
    grad_lat_raw, grad_norm_latent = norm_back(grad_lat_own, normed_lat, scale_lat, norm_latent)
    grad_compressed = jnp.concatenate(
        [grad_lat_raw, unrotate(grad_rope_own, cos_own, sin_own)], axis=-1
    ).astype(jnp.bfloat16)
    grad_latent = jnp.einsum(
        "td,tc->dc", h_own, grad_compressed, preferred_element_type=jnp.float32
    )
    grad_h = grad_h_own + jnp.einsum(
        "tc,dc->td", grad_compressed, w_latent, preferred_element_type=jnp.float32
    )
    grad_in, grad_norm_attn = norm_back(grad_h, normed_one, scale_one, norm_attn)
    grad_inputs = grad_mid + grad_in
    grad_query, grad_expand, grad_output, grad_shared_gate, grad_shared_up, grad_shared_down = (
        lax.psum_scatter(
            grad_query.astype(jnp.bfloat16), EXPERT, scatter_dimension=0, tiled=True
        ).astype(jnp.float32),
        lax.psum_scatter(
            grad_expand.astype(jnp.bfloat16), EXPERT, scatter_dimension=0, tiled=True
        ).astype(jnp.float32),
        lax.psum_scatter(
            grad_output.astype(jnp.bfloat16), EXPERT, scatter_dimension=0, tiled=True
        ).astype(jnp.float32),
        lax.psum_scatter(
            grad_shared_gate.astype(jnp.bfloat16), EXPERT, scatter_dimension=0, tiled=True
        ).astype(jnp.float32),
        lax.psum_scatter(
            grad_shared_up.astype(jnp.bfloat16), EXPERT, scatter_dimension=0, tiled=True
        ).astype(jnp.float32),
        lax.psum_scatter(
            grad_shared_down.astype(jnp.bfloat16), EXPERT, scatter_dimension=0, tiled=True
        ).astype(jnp.float32),
    )
    grad_latent, grad_router, grad_norm_attn, grad_norm_moe, grad_norm_latent = (
        lax.psum_scatter(grad_latent, (EXPERT, TENSOR), scatter_dimension=0, tiled=True),
        lax.psum_scatter(grad_router, (EXPERT, TENSOR), scatter_dimension=0, tiled=True),
        lax.psum_scatter(grad_norm_attn, (EXPERT, TENSOR), scatter_dimension=0, tiled=True),
        lax.psum_scatter(grad_norm_moe, (EXPERT, TENSOR), scatter_dimension=0, tiled=True),
        lax.psum_scatter(grad_norm_latent, (EXPERT, TENSOR), scatter_dimension=0, tiled=True),
    )
    return (
        output,
        grad_inputs,
        grad_norm_attn,
        grad_query,
        grad_latent,
        grad_norm_latent,
        grad_expand,
        grad_output,
        grad_norm_moe,
        grad_router,
        grad_shared_gate,
        grad_shared_up,
        grad_shared_down,
        grad_expert_gate,
        grad_expert_up,
        grad_expert_down,
    )


PLANES = 4


def send_core(values):
    return lax.ppermute(values, TENSOR, [(0, 1), (1, 0)])


def product(form, left, right):
    return jnp.einsum(form, left, right, preferred_element_type=jnp.float32)


EXTRA = 128
VMEM_LIMIT = 54 << 20
MESH = pl.DeviceIdType.MESH


def dot(left, right):
    return jnp.dot(left, right, preferred_element_type=jnp.float32)


def dot_nt(left, right):
    return lax.dot_general(
        left, right, (((1,), (1,)), ((), ())), preferred_element_type=jnp.float32
    )


def dot_tn(left, right):
    return lax.dot_general(
        left, right, (((0,), (0,)), ((), ())), preferred_element_type=jnp.float32
    )


class Chips:
    def __init__(self):
        index = lax.axis_index(EXPERT)
        self.z, self.y, self.x = index // 4, (index // 2) % 2, index % 2
        self.core = lax.axis_index(TENSOR)
        self.to_x = {EXPERT: self.at(self.z, self.y, 1 - self.x)}
        self.to_y = {EXPERT: self.at(self.z, 1 - self.y, self.x)}
        self.to_core = {TENSOR: 1 - self.core}

    def at(self, z, y, x):
        return (z * 2 + y) * 2 + x

    def to_z(self, distance):
        return {EXPERT: self.at((self.z + distance) % PLANES, self.y, self.x)}

    def places(self, step):
        plane = (self.z + PLANES - step) % PLANES
        x, y = self.x, self.y
        return [
            self.at(plane, row, column)
            for row, column in ((y, x), (y, 1 - x), (1 - y, x), (1 - y, 1 - x))
        ]


def greet(partners):
    barrier = pltpu.get_barrier_semaphore()
    for partner in partners:
        pl.semaphore_signal(barrier, inc=1, device_id=partner, device_id_type=MESH)
    pl.semaphore_wait(barrier, len(partners))


def add_rows(target, terms):
    @pl.loop(0, target.shape[0] // 16)
    def _(chunk):
        rows = pl.ds(pl.multiple_of(chunk * 16, 16), 16)
        total = terms[0][rows, :].astype(jnp.float32)
        for term in terms[1:]:
            total = total + term[rows, :].astype(jnp.float32)
        target[rows, :] = total.astype(target.dtype)


def sum_kernel(parts, exchanged, *refs):
    chips = Chips()
    refs = list(refs)
    arrays = 1 + max(part[0] for part in parts)
    kind_of = {part[0]: part[1] for part in parts}
    sources = [[refs.pop(0) for _ in range(2 if kind_of[a] == 2 else 1)] for a in range(arrays)]
    blocks = refs.pop(0) if exchanged else None
    results = [refs.pop(0) for _ in range(arrays)]
    arrived = refs.pop(0) if exchanged else None
    boxes = []
    for _, kind, _, _, _ in parts:
        mine = refs.pop(0)
        from_core = refs.pop(0) if kind else None
        boxes.append((mine, from_core) + tuple(refs.pop(0) for _ in range(4)))
    if exchanged:
        by_x, by_y, x_send, x_recv, z_send, z_recv = [refs.pop(0) for _ in range(6)]
    load_sem, send_sem, recv_sem = refs
    each = list(range(len(parts)))

    def copy_to(source, target, send, recv, to):
        return pltpu.make_async_remote_copy(
            src_ref=source,
            dst_ref=target,
            send_sem=send,
            recv_sem=recv,
            device_id=to,
            device_id_type=MESH,
        )

    def remote(part, step, index, source, target, to):
        sems = (send_sem.at[part, step, index], recv_sem.at[part, step, index])
        return copy_to(source, target, *sems, to)

    def loads(part, step):
        array, kind, start, stop, _ = parts[part]
        mine, source = boxes[part][0], sources[array]
        for k, place in enumerate(chips.places(step)):
            if kind == 2:
                block = source[0].at[step, k, :, start:stop]
            elif kind == 1:
                block = source[0].at[place, chips.core, :, start:stop]
            else:
                block = source[0].at[place, :, start:stop]
            yield pltpu.make_async_copy(block, mine.at[step, k], load_sem.at[part, step, k])

    def core_copies(part, step):
        array, kind, start, stop, _ = parts[part]
        if kind == 0:
            return
        for k, place in enumerate(chips.places(step)):
            if kind == 2:
                block = sources[array][1].at[step, k, :, start:stop]
            else:
                block = sources[array][0].at[place, 1 - chips.core, :, start:stop]
            target = boxes[part][1].at[step, k]
            yield remote(part, step, k, block, target, chips.to_core)

    def level(part, step):
        return 0 if parts[part][4] else step

    def corner_copies(part, step):
        mine, _, corners = boxes[part][:3]
        half = mine.shape[2] // 2
        here = corners.at[level(part, step)]
        yield remote(part, step, 4, mine.at[step, 3, :half], here.at[0], chips.to_y)
        yield remote(part, step, 5, mine.at[step, 3, half:], here.at[1], chips.to_x)

    def early_copies(part, step):
        mine, from_x, from_y = boxes[part][0], boxes[part][3], boxes[part][4]
        half = mine.shape[2] // 2
        x, y = from_x.at[level(part, step)], from_y.at[level(part, step)]
        yield remote(part, step, 6, mine.at[step, 1, half:], x.at[half:], chips.to_x)
        yield remote(part, step, 7, mine.at[step, 2, :half], y.at[:half], chips.to_y)

    def late_copies(part, step):
        mine, from_x, from_y = boxes[part][0], boxes[part][3], boxes[part][4]
        half = mine.shape[2] // 2
        x, y = from_x.at[level(part, step)], from_y.at[level(part, step)]
        yield remote(part, step, 9, mine.at[step, 1, :half], x.at[:half], chips.to_x)
        yield remote(part, step, 10, mine.at[step, 2, half:], y.at[half:], chips.to_y)

    def side_copies(part, step):
        return [*early_copies(part, step), *late_copies(part, step)]

    def z_copy(part, step):
        mine, from_z = boxes[part][0], boxes[part][5]
        source = mine.at[step] if parts[part][4] else mine.at[step, 0]
        return remote(part, step, 8, source, from_z.at[step - 1], chips.to_z(1))

    def x_copy():
        return copy_to(
            blocks.at[:, :, 1 - chips.x], by_x, x_send.at[0], x_recv.at[0], chips.to_x
        )

    def y_copies():
        own = blocks.at[:, 1 - chips.y, chips.x]
        passed = by_x.at[:, 1 - chips.y]
        return [
            copy_to(source, by_y.at[k], x_send.at[1 + k], x_recv.at[1 + k], chips.to_y)
            for k, source in enumerate((own, passed))
        ]

    def gathered(plane):
        return [
            blocks.at[plane, chips.y, chips.x],
            by_x.at[plane, chips.y],
            by_y.at[0, plane],
            by_y.at[1, plane],
        ]

    def z_sends(distance):
        plane = (chips.z + distance) % PLANES
        return [
            copy_to(
                source,
                arrived.at[place],
                z_send.at[distance, k],
                z_recv.at[distance, k],
                chips.to_z(distance),
            )
            for k, (source, place) in enumerate(zip(gathered(plane), chips.places(0)))
        ]

    def z_arrivals(distance):
        plane = (chips.z + distance) % PLANES
        return [
            copy_to(
                source,
                arrived.at[place],
                z_send.at[distance, k],
                z_recv.at[distance, k],
                chips.to_z(distance),
            )
            for k, (source, place) in enumerate(zip(gathered(plane), chips.places(distance)))
        ]

    def keeps():
        return [
            pltpu.make_async_copy(source, arrived.at[place], z_send.at[0, k])
            for k, (source, place) in enumerate(zip(gathered(chips.z), chips.places(0)))
        ]

    order = [*range(1, PLANES), 0]
    distances = range(1, PLANES) if exchanged else (1, PLANES - 1)
    greet([chips.to_x, chips.to_y, chips.to_core] + [chips.to_z(k) for k in distances])
    if exchanged:
        x_copy().start()

    def fetch(step):
        for part in each:
            for copy in core_copies(part, step):
                copy.start()
            for copy in loads(part, step):
                copy.start(priority=1)

    fetch(order[0])
    fetch(order[1])

    def chip_sum(step):
        ahead = order.index(step) + 2
        for part in each:
            mine, from_core = boxes[part][:2]
            for copy in loads(part, step):
                copy.wait()
            for copy in core_copies(part, step):
                copy.wait_recv()
            for k in (3, 1, 2, 0):
                if from_core is not None:
                    add_rows(mine.at[step, k], [mine.at[step, k], from_core.at[step, k]])
                if k == 3 and not parts[part][4]:
                    for copy in corner_copies(part, step):
                        copy.start()
            if not parts[part][4]:
                for copy in early_copies(part, step):
                    copy.start()
        if ahead < PLANES:
            fetch(order[ahead])

    def z_sum(step):
        for part in each:
            if parts[part][4]:
                part_z_sum(part, step)

    def part_z_sum(part, step):
        mine, from_z = boxes[part][0], boxes[part][5]
        if step != 1:
            before = (step - 1) % PLANES
            z_copy(part, before).wait_recv()
            for k in (3, 1, 2, 0):
                add_rows(mine.at[step, k], [mine.at[step, k], from_z.at[before - 1, k]])
        if step:
            z_copy(part, step).start()
        else:
            for copy in [*corner_copies(part, step), *early_copies(part, step)]:
                copy.start()

    def side_sum(step):
        for part in each:
            if parts[part][4] and step:
                continue
            mine, _, corners = boxes[part][:3]
            half = mine.shape[2] // 2
            for copy in corner_copies(part, step):
                copy.wait_recv()
            low_half, high_half = mine.at[step, 1, :half], mine.at[step, 2, half:]
            here = corners.at[level(part, step)]
            add_rows(low_half, [low_half, here.at[0]])
            add_rows(high_half, [high_half, here.at[1]])
            for copy in late_copies(part, step):
                copy.start()

    def plane_sum(step):
        for part in each:
            array, _, start, stop, along_z = parts[part]
            if along_z and step:
                continue
            mine, _, _, from_x, from_y, from_z = boxes[part]
            here = level(part, step)
            terms = [mine.at[step, 0], from_x.at[here], from_y.at[here]]
            for copy in side_copies(part, step):
                copy.wait_recv()
            if step != 1 and not along_z:
                before = (step - 1) % PLANES
                z_copy(part, before).wait_recv()
                terms.append(from_z.at[before - 1])
            if step == 0:
                add_rows(results[array].at[:, start:stop], terms)
            else:
                add_rows(mine.at[step, 0], terms)
                z_copy(part, step).start()

    stages = ((0, chip_sum), (1, side_sum), (0, z_sum), (2, plane_sum))
    for tick in range(PLANES + 2):
        for late, stage in stages:
            if 0 <= tick - late < PLANES:
                stage(order[tick - late])
        if exchanged and tick == 0:
            x_copy().wait_recv()
            for copy in y_copies():
                copy.start()
        if exchanged and tick == 1:
            for copy in y_copies():
                copy.wait_recv()
            for copy in keeps():
                copy.start()
            for distance in range(1, PLANES):
                for copy in z_sends(distance):
                    copy.start()
    if exchanged:
        for copy in [x_copy(), *y_copies()]:
            copy.wait_send()
        for copy in keeps():
            copy.wait()
        for distance in range(1, PLANES):
            for copy in z_arrivals(distance):
                copy.wait_recv()
            for copy in z_sends(distance):
                copy.wait_send()
    for part in each:
        along_z = parts[part][4]
        for step in range(PLANES):
            sent = [*core_copies(part, step)]
            if step == 0 or not along_z:
                sent += [*corner_copies(part, step), *side_copies(part, step)]
            if step:
                sent.append(z_copy(part, step))
            for copy in sent:
                copy.wait_send()


def sum_over_chips(collective_id, arrays, blocks=None):
    low = jnp.bfloat16
    parts, scratch, shapes = [], [], []
    for index, (kind, operands, z_columns) in enumerate(arrays):
        rows, columns = operands[0].shape[-2:]
        shapes.append((rows, columns))
        for start, stop in ((0, columns - z_columns), (columns - z_columns, columns)):
            if start == stop:
                continue
            along_z = start > 0
            parts.append((index, kind, start, stop, along_z))
            size = (rows, stop - start)
            levels = 1 if along_z else PLANES
            scratch += [pltpu.VMEM((PLANES, 4) + size, low)] * (2 if kind else 1)
            scratch += [
                pltpu.VMEM((levels, 2, rows // 2, stop - start), low),
                pltpu.VMEM((levels,) + size, low),
                pltpu.VMEM((levels,) + size, low),
                pltpu.VMEM((PLANES - 1,) + ((4,) if along_z else ()) + size, low),
            ]
    operands = [operand for _, group, _ in arrays for operand in group]
    out_shape = [jax.ShapeDtypeStruct(shape, jnp.float32) for shape in shapes]
    out_specs = [pl.BlockSpec(memory_space=pltpu.VMEM)] * len(shapes)
    if blocks is not None:
        operands.append(blocks)
        block = blocks.shape[3:]
        out_shape.append(jax.ShapeDtypeStruct((PLANES * 4,) + block, low))
        out_specs.append(pl.BlockSpec(memory_space=pl.ANY))
        scratch += [
            pltpu.VMEM((PLANES, 2) + block, low),
            pltpu.VMEM((2, PLANES) + block, low),
            pltpu.SemaphoreType.DMA((3,)),
            pltpu.SemaphoreType.DMA((3,)),
            pltpu.SemaphoreType.DMA((PLANES, 4)),
            pltpu.SemaphoreType.DMA((PLANES, 4)),
        ]
    size = sum(rows * columns for rows, columns in shapes)
    semaphores = (len(parts), PLANES, 11)
    return pl.pallas_call(
        functools.partial(sum_kernel, tuple(parts), blocks is not None),
        in_specs=[pl.BlockSpec(memory_space=pl.ANY)] * len(operands),
        out_specs=out_specs,
        out_shape=out_shape,
        scratch_shapes=scratch
        + [
            pltpu.SemaphoreType.DMA((len(parts), PLANES, 4)),
            pltpu.SemaphoreType.DMA(semaphores),
            pltpu.SemaphoreType.DMA(semaphores),
        ],
        compiler_params=pltpu.CompilerParams(
            collective_id=collective_id, has_side_effects=True, vmem_limit_bytes=VMEM_LIMIT
        ),
        cost_estimate=pl.CostEstimate(
            flops=size * 30, bytes_accessed=size * 64, transcendentals=0
        ),
    )(*operands)


def gated(gate_act, up_act, grad_hidden):
    sigma = jax.nn.sigmoid(gate_act)
    silu = gate_act * sigma
    hidden = silu * up_act
    grad_gate = grad_hidden * up_act * sigma * (1.0 + gate_act * (1.0 - sigma))
    grad_up = grad_hidden * silu
    return tuple(v.astype(jnp.bfloat16) for v in (hidden, grad_gate, grad_up))


def moe_kernel(own_rows_in, lanes, w_gate, w_up, w_down, sw_gate, sw_up, sw_down, *refs):
    land, out_mine, out_other, grad_mine, grad_other = refs[:5]
    rows_out, pairs_out, hidden_out, gate_out, up_out, shared_out = refs[5:11]
    rows_kept, grads_kept, out_kept, back_kept, extra_kept, s_hidden, s_grads, seats = refs[11:19]
    x_here, g_here, gate_here, up_here, down_here, s_in, s_down, sum_in, sum_down = refs[19:28]
    come, go, fetch, send_sem, recv_sem, z_send, z_recv = refs[28:]
    width, half = s_down.shape
    plane, step = pl.program_id(0), pl.program_id(1)
    experts, slots = out_kept.shape[:2]
    pairs, pair_rows_all, pair_slots = seats.shape
    own = slots // pairs
    low = jnp.bfloat16
    chips = Chips()

    def remote(step, index, source, target, to):
        return pltpu.make_async_remote_copy(
            src_ref=source,
            dst_ref=target,
            send_sem=send_sem.at[step, index],
            recv_sem=recv_sem.at[step, index],
            device_id=to,
            device_id_type=MESH,
        )

    def own_block(step):
        return own_rows_in if isinstance(step, int) and step == 0 else land.at[step, 0, 0]

    def side_copies(step):
        block = own_block(step)
        return [
            remote(step, 0, block, land.at[step, 0, 1], chips.to_x),
            remote(step, 1, block, land.at[step, 0, 2], chips.to_y),
        ]

    def corner_copies(step):
        return [
            remote(step, 2, land.at[step, 0, 1, 0], land.at[step, 0, 3, 0], chips.to_y),
            remote(step, 3, land.at[step, 0, 2, 1], land.at[step, 0, 3, 1], chips.to_x),
        ]

    def core_copy(step, k):
        if k < 3:
            source, target = land.at[step, 0, k] if k else own_block(step), land.at[step, 1, k]
        else:
            source, target = land.at[step, 0, 3, k - 3], land.at[step, 1, 3, k - 3]
        return remote(step, 4 + k, source, target, chips.to_core)

    def z_copy(k):
        return pltpu.make_async_remote_copy(
            src_ref=own_block(k - 1),
            dst_ref=land.at[k, 0, 0],
            send_sem=z_send.at[k],
            recv_sem=z_recv.at[k],
            device_id=chips.to_z(1),
            device_id_type=MESH,
        )

    def start_plane(step):
        for copy in side_copies(step) + [core_copy(step, 0)]:
            copy.start()

    def pass_corners(step):
        for copy in side_copies(step):
            copy.wait_recv()
        for copy in corner_copies(step) + [core_copy(step, 1), core_copy(step, 2)]:
            copy.start()

    def finish_plane(step):
        for copy in corner_copies(step):
            copy.wait_recv()
        for k in (3, 4):
            core_copy(step, k).start()
        for k in range(5):
            core_copy(step, k).wait_recv()

    def weight_copies(expert):
        return [
            pltpu.make_async_copy(source.at[expert], target.at[expert], fetch.at[expert, k])
            for k, (source, target) in enumerate(
                ((w_gate, gate_here), (w_up, up_here), (w_down, down_here))
            )
        ]

    shared_blocks = sw_gate.shape[1] // half
    chip = chips.at(chips.z, chips.y, chips.x)
    shared_here = chip < shared_blocks

    def shared_copies():
        columns = pl.ds(pl.multiple_of((chip % shared_blocks) * half, half), half)
        return [
            pltpu.make_async_copy(source.at[:, columns], target, fetch.at[experts, k])
            for k, (source, target) in enumerate(
                (
                    (sw_gate, s_in.at[:, :half]),
                    (sw_up, s_in.at[:, half:]),
                    (sw_down, s_down),
                )
            )
        ]

    @pl.when((plane == 0) & (step == 0))
    def _():
        greet(
            [chips.to_x, chips.to_y, chips.to_core, chips.to_z(1), chips.to_z(PLANES - 1)]
        )
        start_plane(0)
        z_copy(1).start()

        @pl.when(shared_here)
        def _():
            for copy in shared_copies():
                copy.start()

        for expert in range(experts):
            for copy in weight_copies(expert):
                copy.start()
        pass_corners(0)
        z_copy(1).wait_recv()
        z_copy(2).start()
        start_plane(1)

        @pl.when(shared_here)
        def _():
            for copy in shared_copies():
                copy.wait()

        @pl.when(~shared_here)
        def _():
            s_in[...] = jnp.zeros(s_in.shape, low)
            s_down[...] = jnp.zeros(s_down.shape, low)

        finish_plane(0)

    def pair_place(pair):
        return pair // (pairs // 2), slice((pair % (pairs // 2)) * 2, (pair % (pairs // 2)) * 2 + 2)

    def coming(pair):
        side, blocks = pair_place(pair)
        return [
            pltpu.make_async_copy(
                land.at[plane, side, blocks, which],
                here.at[2 * pair : 2 * pair + 2],
                come.at[which * pairs + pair],
            )
            for which, here in enumerate((x_here, g_here))
        ]

    def going(pair):
        side, blocks = pair_place(pair)
        return [
            pltpu.make_async_copy(
                here.at[2 * pair : 2 * pair + 2, :, :columns],
                targets[side].at[plane, blocks],
                go.at[which * pairs + pair],
            )
            for which, (targets, here, columns) in enumerate(
                (
                    ((out_mine, out_other), x_here, width),
                    ((grad_mine, grad_other), g_here, width + EXTRA),
                )
            )
        ]

    def pair_rows(here, pair, columns):
        return here[2 * pair : 2 * pair + 2, :, :columns].reshape(pair_rows_all, columns)

    def own_coming():
        for which, here in enumerate((x_here, g_here)):
            for block, source in enumerate((own_rows_in.at[which], land.at[0, 0, 1, which])):
                yield pltpu.make_async_copy(source, here.at[block], come.at[which * pairs])

    @pl.when((step == 0) & (plane == 0))
    def _():
        for copy in own_coming():
            copy.start()

    @pl.when((step == 0) & (plane > 0))
    def _():
        for copy in coming(0):
            copy.start()

    @pl.when(step == 0)
    def _():
        for pair in range(1, pairs):
            for copy in coming(pair):
                copy.start()
        tokens = lax.broadcasted_iota(jnp.int32, (pair_rows_all, pair_rows_all), 0)
        others = lax.broadcasted_iota(jnp.int32, (pair_rows_all, pair_rows_all), 1)
        own_rows = pair_rows_all // 2
        earlier = (others < tokens) & ((others >= own_rows) == (tokens >= own_rows))
        earlier = earlier.astype(jnp.float32).astype(low)
        lane = lax.broadcasted_iota(jnp.int32, (pair_rows_all, pair_slots), 1)
        block = lax.broadcasted_iota(jnp.int32, (pair_rows_all, pair_slots), 0) // own_rows
        capacity = own // 2
        at_block = lax.rem(lane // capacity, 2) == block
        at_slot = lax.rem(lane, capacity).astype(jnp.float32)
        for pair in range(pairs):
            for copy in coming(pair):
                copy.wait()
            grads = pair_rows(g_here, pair, width + EXTRA)
            routes = grads[:, width:].astype(jnp.float32)
            named = routes[:, :1] == lanes[:1]
            for k in range(1, TOPK):
                named = named | (routes[:, k : k + 1] == lanes[:1])
            named = named.astype(jnp.float32)
            rank = dot(earlier, named.astype(low))
            seat = jnp.where(at_block & (rank == at_slot), named, 0.0).astype(low)
            seats[pair] = seat
            rows = dot_tn(seat, pair_rows(x_here, pair, width + EXTRA))
            grads = dot_tn(seat, grads[:, :width])
            for expert in range(experts):
                here = slice(expert * own, (expert + 1) * own)
                there = slice(pair * own, (pair + 1) * own)
                low_rows = rows[here, :width].astype(jnp.bfloat16)
                low_grads = grads[here].astype(jnp.bfloat16)
                if expert == 0:
                    rows_out[0, there] = low_rows
                    pairs_out[0, there] = low_grads
                else:
                    rows_kept[expert - 1, there] = low_rows
                    grads_kept[expert - 1, there] = low_grads
                gate = jnp.sum(
                    rows[here, width:] * lanes[1 + expert : 2 + expert], axis=-1, keepdims=True
                )
                extra_kept[expert, there] = jnp.broadcast_to(gate, (own, EXTRA))
        for side in range(2):
            blocks = slice(side * pairs, (side + 1) * pairs)
            tokens = pairs * own_rows
            rows = x_here[blocks, :, :width].reshape(tokens, width)
            grads = g_here[blocks, :, :width].reshape(tokens, width)
            acts = dot(rows, s_in[...])
            hidden, grad_gate, grad_up = gated(
                acts[:, :half], acts[:, half:], dot(grads, s_down[...])
            )
            s_hidden[side * tokens : (side + 1) * tokens] = hidden
            both = jnp.concatenate([grad_gate, grad_up], axis=1)
            s_grads[side * tokens : (side + 1) * tokens] = both
            term_in, term_down = dot_tn(both, rows), dot_tn(hidden, grads)
            if side == 0:
                fresh = plane == 0
                sum_in[...] = jnp.where(fresh, 0.0, sum_in[...]) + term_in
                sum_down[...] = jnp.where(fresh, 0.0, sum_down[...]) + term_down
            else:
                sum_in[...] += term_in
                sum_down[...] += term_down

    @pl.when(step > 0)
    def _():
        rows_out[0] = rows_kept[step - 1]
        pairs_out[0] = grads_kept[step - 1]

    @pl.when(plane == 0)
    def _():
        for copy in weight_copies(step):
            copy.wait()

    rows = rows_out[0]
    grads = pairs_out[0].astype(jnp.float32)
    gates = extra_kept[step][:, :1]
    pair_grads = (grads * gates).astype(jnp.bfloat16)
    hidden, grad_gate, grad_up = gated(
        dot_nt(rows, gate_here[step]), dot_nt(rows, up_here[step]), dot_nt(pair_grads, down_here[step])
    )
    hidden_out[0] = hidden
    gate_out[0] = grad_gate
    up_out[0] = grad_up
    part = dot(hidden, down_here[step])
    out_kept[step] = (part * gates).astype(jnp.bfloat16)
    slot_grad = jnp.sum(part * grads, axis=-1, keepdims=True)
    pairs_out[0] = pair_grads
    high = slot_grad.astype(jnp.bfloat16).astype(jnp.float32)
    lane_row = 1 + experts + step * 2
    extra_kept[step] = high * lanes[pl.ds(lane_row, 1)] + (slot_grad - high) * lanes[
        pl.ds(lane_row + 1, 1)
    ]
    back_kept[step] = (dot(grad_gate, gate_here[step]) + dot(grad_up, up_here[step])).astype(
        jnp.bfloat16
    )

    @pl.when((step == 0) & (plane + 1 < PLANES))
    def _():
        pass_corners(plane + 1)

    @pl.when((step == 0) & (plane + 2 < PLANES))
    def _():
        for k in range(2, PLANES):

            @pl.when(plane == k - 2)
            def _(k=k):
                z_copy(k).wait_recv()
                if k + 1 < PLANES:
                    z_copy(k + 1).start()

        start_plane(plane + 2)

    @pl.when(step == experts - 1)
    def _():
        for pair in range(pairs):
            there = slice(pair * own, (pair + 1) * own)
            tokens = slice(pair * pair_rows_all, (pair + 1) * pair_rows_all)
            here = slice(2 * pair, 2 * pair + 2)
            back = seats[pair]
            total = dot(
                back, jnp.concatenate([out_kept[e, there] for e in range(experts)], 0)
            ) + dot_nt(s_hidden[tokens], s_down[...])
            x_here[here, :, :width] = total.astype(jnp.bfloat16).reshape(2, -1, width)
            total = dot(
                back, jnp.concatenate([back_kept[e, there] for e in range(experts)], 0)
            ) + dot_nt(s_grads[tokens], s_in[...])
            g_here[here, :, :width] = total.astype(jnp.bfloat16).reshape(
                2, -1, width
            )
            extra = jnp.concatenate([extra_kept[e, there] for e in range(experts)], 0)
            total = dot(back, extra.astype(jnp.bfloat16))
            g_here[here, :, width:] = total.astype(jnp.bfloat16).reshape(2, -1, EXTRA)
            for copy in going(pair):
                copy.start()
        for pair in range(pairs):
            for copy in going(pair):
                copy.wait()

    @pl.when((step == experts - 1) & (plane + 1 < PLANES))
    def _():
        finish_plane(plane + 1)

    @pl.when((step == experts - 1) & (plane == PLANES - 1))
    def _():
        block_rows = width // shared_out.shape[0]
        for to in range(shared_out.shape[0]):
            there = slice(to * block_rows, (to + 1) * block_rows)
            shared_out[to, : 2 * half] = sum_in[:, there].astype(low)
            shared_out[to, 2 * half :] = sum_down[:, there].astype(low)
        for k in range(1, PLANES):
            z_copy(k).wait_send()

        @pl.loop(0, PLANES)
        def _(sent):
            for copy in side_copies(sent) + corner_copies(sent):
                copy.wait_send()
            for k in range(5):
                core_copy(sent, k).wait_send()


def moe_layer(own_rows_in, lanes, weights):
    experts, units, width = weights[0].shape
    _, own_rows, wide = own_rows_in.shape
    blocks, pairs, pair_rows, pair_slots = 4, 4, 2 * own_rows, EXTRA
    slots = pairs * pair_slots // experts
    tokens = pairs * pair_rows
    half = EXTRA
    chips = lax.axis_size(EXPERT)
    low = jnp.bfloat16

    def whole(array):
        zeros = (0,) * len(array.shape)
        return pl.BlockSpec(array.shape, lambda s, j: zeros, pipeline_mode=pl.Buffered(1))

    anywhere = pl.BlockSpec(memory_space=pl.ANY)
    land = [jax.ShapeDtypeStruct((PLANES, 2, blocks, 2, own_rows, wide), low)]
    plain = [jax.ShapeDtypeStruct((PLANES, blocks, own_rows, width), low)] * 2
    extended = [jax.ShapeDtypeStruct((PLANES, blocks, own_rows, wide), low)] * 2
    keep = [
        jax.ShapeDtypeStruct((experts, PLANES * slots, columns), low)
        for columns in (width, width, units, units, units)
    ]
    shared = [jax.ShapeDtypeStruct((chips, 3 * half, width // chips), low)]
    operands = [own_rows_in, lanes] + list(weights)
    work = 2 * tokens * width * (8 * half + 2 * pair_slots) + 12 * experts * slots * width * units
    results = pl.pallas_call(
        moe_kernel,
        grid=(PLANES, experts),
        in_specs=[anywhere, whole(lanes)] + [anywhere] * len(weights),
        out_specs=[anywhere] * 5
        + [pl.BlockSpec((1, slots, v.shape[2]), lambda s, j: (j, s, 0)) for v in keep]
        + [whole(v) for v in shared],
        out_shape=land + plain + extended + keep + shared,
        scratch_shapes=[
            pltpu.VMEM((experts - 1, slots, width), low),
            pltpu.VMEM((experts - 1, slots, width), low),
            pltpu.VMEM((experts, slots, width), low),
            pltpu.VMEM((experts, slots, width), low),
            pltpu.VMEM((experts, slots, EXTRA), jnp.float32),
            pltpu.VMEM((tokens, half), low),
            pltpu.VMEM((tokens, 2 * half), low),
            pltpu.VMEM((pairs, pair_rows, pair_slots), low),
            pltpu.VMEM((2 * blocks, own_rows, wide), low),
            pltpu.VMEM((2 * blocks, own_rows, wide), low),
            pltpu.VMEM(weights[0].shape, low),
            pltpu.VMEM(weights[1].shape, low),
            pltpu.VMEM(weights[2].shape, low),
            pltpu.VMEM((width, 2 * half), low),
            pltpu.VMEM((width, half), low),
            pltpu.VMEM((2 * half, width), jnp.float32),
            pltpu.VMEM((half, width), jnp.float32),
            pltpu.SemaphoreType.DMA((2 * pairs,)),
            pltpu.SemaphoreType.DMA((2 * pairs,)),
            pltpu.SemaphoreType.DMA((experts + 1, 3)),
            pltpu.SemaphoreType.DMA((PLANES, 9)),
            pltpu.SemaphoreType.DMA((PLANES, 9)),
            pltpu.SemaphoreType.DMA((PLANES,)),
            pltpu.SemaphoreType.DMA((PLANES,)),
        ],
        compiler_params=pltpu.CompilerParams(
            collective_id=0, has_side_effects=True, vmem_limit_bytes=VMEM_LIMIT
        ),
        cost_estimate=pl.CostEstimate(
            flops=PLANES * work, bytes_accessed=120 << 20, transcendentals=0
        ),
    )(*operands)
    return results[1:3], results[3:5], results[5:]


def per_device_gathered(
    inputs,
    norm_attn,
    w_query,
    w_latent,
    norm_latent,
    w_expand,
    w_output,
    norm_moe,
    w_router,
    w_shared_gate,
    w_shared_up,
    w_shared_down,
    w_expert_gate,
    w_expert_up,
    w_expert_down,
    routes,
    cotangent,
):
    own_rows = inputs.shape[0]
    width = inputs.shape[1]
    tensor_size = lax.axis_size(TENSOR)
    expert_size = lax.axis_size(EXPERT)
    tensor_index = lax.axis_index(TENSOR)
    expert_index = lax.axis_index(EXPERT)
    seq_rows = own_rows * tensor_size
    local_heads = w_query.shape[1] // (NOPE + ROPE)
    experts = w_router.shape[1]
    local_experts = experts // expert_size
    capacity = own_rows * TOPK * 4 // (3 * experts)
    scale = 1.0 / math.sqrt(NOPE + ROPE)

    flat_in = inputs.astype(jnp.float32)
    scale_one = lax.rsqrt(jnp.mean(flat_in * flat_in, axis=-1, keepdims=True) + EPS)
    normed_one = flat_in * scale_one
    h_own = (normed_one * norm_attn).astype(jnp.bfloat16)
    compressed = jnp.dot(h_own, w_latent, preferred_element_type=jnp.float32)
    lat_raw = compressed[:, :LATENT]
    scale_lat = lax.rsqrt(jnp.mean(lat_raw * lat_raw, axis=-1, keepdims=True) + EPS)
    normed_lat = lat_raw * scale_lat
    lat_own = (normed_lat * norm_latent).astype(jnp.bfloat16)
    places = jnp.arange(own_rows)
    places_all = jnp.concatenate(
        [tensor_index * own_rows + places, (1 - tensor_index) * own_rows + places]
    )
    cos_own, sin_own = rope_tables(places_all[:own_rows], ROPE)
    rope_own = rotate(compressed[:, LATENT:], cos_own, sin_own).astype(jnp.bfloat16)

    def both(values):
        return jnp.concatenate([values, send_core(values)], axis=0)

    h_all = both(h_own)
    lat_rope = both(jnp.concatenate([lat_own, rope_own], axis=1))
    lat_all, rope_all = lat_rope[:, :LATENT], lat_rope[:, LATENT:]
    cos_all, sin_all = rope_tables(places_all, ROPE)
    cos_all = cos_all[:, None, :]
    sin_all = sin_all[:, None, :]
    query_raw = jnp.dot(h_all, w_query, preferred_element_type=jnp.float32).reshape(
        seq_rows, local_heads, NOPE + ROPE
    )
    query = jnp.concatenate(
        [query_raw[..., :NOPE], rotate(query_raw[..., NOPE:], cos_all, sin_all)], axis=-1
    ).astype(jnp.bfloat16)
    expanded = jnp.dot(lat_all, w_expand, preferred_element_type=jnp.float32).astype(jnp.bfloat16)
    expanded = expanded.reshape(seq_rows, local_heads, NOPE + VD)
    key_full = jnp.concatenate(
        [
            expanded[..., :NOPE],
            jnp.broadcast_to(rope_all[:, None, :], (seq_rows, local_heads, ROPE)),
        ],
        axis=-1,
    )
    value = expanded[..., NOPE:]
    allowed = (places_all[:, None] >= places_all[None, :])[None]
    scores = product("qhd,khd->hqk", query, key_full) * scale
    scores = jnp.where(allowed, scores, -1e30)
    weights = jnp.exp(scores - jnp.max(scores, axis=-1, keepdims=True))
    probs = weights / jnp.sum(weights, axis=-1, keepdims=True)
    attended = product("hqk,khd->qhd", probs.astype(jnp.bfloat16), value)
    attended_flat = attended.astype(jnp.bfloat16).reshape(seq_rows, local_heads * VD)
    attn_terms = product("sv,dv->sd", attended_flat, w_output)
    after_attn = (
        flat_in
        + attn_terms[:own_rows]
        + send_core(attn_terms[own_rows:].astype(jnp.bfloat16)).astype(jnp.float32)
    )
    scale_two = lax.rsqrt(jnp.mean(after_attn * after_attn, axis=-1, keepdims=True) + EPS)
    normed_two = after_attn * scale_two
    h_moe = (normed_two * norm_moe).astype(jnp.bfloat16)
    logits = jnp.dot(h_moe, w_router, preferred_element_type=jnp.float32)
    expert_ids = jnp.arange(experts, dtype=jnp.int32)
    chosen = jnp.any(routes[:, :, None] == expert_ids[None, None, :], axis=1)
    masked = jnp.where(chosen, logits, -1e30)
    raised = jnp.where(chosen, jnp.exp(masked - jnp.max(masked, axis=-1, keepdims=True)), 0.0)
    gates = raised / jnp.sum(raised, axis=-1, keepdims=True)
    high_gates = lax.reduce_precision(gates, 8, 7)
    beside = jnp.stack(
        [
            jnp.pad(
                jnp.concatenate([high_gates, gates - high_gates], axis=1),
                ((0, 0), (0, EXTRA - 2 * experts)),
            ),
            jnp.pad(routes.astype(jnp.float32), ((0, 0), (0, EXTRA - TOPK))),
        ]
    ).astype(jnp.bfloat16)
    own_rows_in = jnp.concatenate([jnp.stack([h_moe, cotangent]), beside], axis=2)

    own_ids = expert_index * local_experts + jnp.arange(local_experts, dtype=jnp.int32)
    lane_ids = jnp.arange(EXTRA, dtype=jnp.int32)[None, :]
    slot_experts = expert_index * local_experts + lane_ids // (2 * capacity)
    gate_lanes = (lane_ids == own_ids[:, None]) | (lane_ids == own_ids[:, None] + experts)
    back_lanes = (own_ids[:, None] * tensor_size + tensor_index) * 2 + jnp.arange(2)[None, :]
    lanes = jnp.concatenate(
        [slot_experts, gate_lanes, lane_ids == back_lanes.reshape(-1, 1)], axis=0
    ).astype(jnp.float32)
    lanes = jnp.pad(lanes, ((0, -lanes.shape[0] % 8), (0, 0)))

    all_weights = tuple(jnp.swapaxes(w, 1, 2) for w in (w_expert_gate, w_expert_up, w_expert_down))
    all_weights += (w_shared_gate, w_shared_up, w_shared_down)
    out_parts, grad_parts, kept = moe_layer(own_rows_in, lanes, all_weights)
    shared_grads = kept[5].reshape((PLANES, 2, 2) + kept[5].shape[1:])
    moe_back, moe_out, shared_grads = sum_over_chips(
        1, [(2, grad_parts, 512), (2, out_parts, 512)], shared_grads
    )
    output = (after_attn + moe_out).astype(jnp.bfloat16)

    grad_gates = jnp.sum(moe_back[:, width:].reshape(own_rows, experts, -1), axis=-1)
    grad_gates = jnp.where(chosen, grad_gates, 0.0)
    grad_select = gates * (grad_gates - jnp.sum(gates * grad_gates, axis=-1, keepdims=True))
    grad_logits = grad_select.astype(jnp.bfloat16)
    grad_router = product("td,te->de", h_moe, grad_logits)

    grad_out = cotangent.astype(jnp.float32)
    grad_moe = moe_back[:, :width] + product("te,de->td", grad_logits, w_router)
    grad_mid, grad_norm_moe = norm_back(grad_moe, normed_two, scale_two, norm_moe)
    grad_mid = grad_mid + grad_out
    grad_attn_all = both(grad_mid.astype(jnp.bfloat16))
    grad_output = product("sd,sv->dv", grad_attn_all, attended_flat)
    grad_attended = product("sd,dv->sv", grad_attn_all, w_output)
    grad_attended = grad_attended.astype(jnp.bfloat16).reshape(seq_rows, local_heads, VD)
    grad_probs = product("qhv,khv->hqk", grad_attended, value)
    centre = jnp.sum(probs * grad_probs, axis=-1, keepdims=True)
    grad_scores = (probs * (grad_probs - centre)).astype(jnp.bfloat16)
    grad_query_full = product("hqk,khd->qhd", grad_scores, key_full) * scale
    grad_key_full = product("hqk,qhd->khd", grad_scores, query) * scale
    grad_value = product("hqk,qhv->khv", probs.astype(jnp.bfloat16), grad_attended)
    grad_query_raw = jnp.concatenate(
        [grad_query_full[..., :NOPE], unrotate(grad_query_full[..., NOPE:], cos_all, sin_all)],
        axis=-1,
    )
    grad_query_raw = grad_query_raw.astype(jnp.bfloat16).reshape(
        seq_rows, local_heads * (NOPE + ROPE)
    )
    grad_query = product("sd,sq->dq", h_all, grad_query_raw)
    grad_expanded = jnp.concatenate([grad_key_full[..., :NOPE], grad_value], axis=-1)
    grad_expanded = grad_expanded.astype(jnp.bfloat16).reshape(seq_rows, local_heads * (NOPE + VD))
    grad_expand = product("sl,sk->lk", lat_all, grad_expanded)
    grad_rope_part = jnp.sum(grad_key_full[..., NOPE:], axis=1)
    grad_h_part = product("sq,dq->sd", grad_query_raw, w_query)
    grad_lat_part = product("sk,lk->sl", grad_expanded, w_expand)
    own_side = jnp.concatenate([grad_lat_part, grad_rope_part], axis=1)
    own_side = own_side[:own_rows] + send_core(own_side[own_rows:].astype(jnp.bfloat16)).astype(
        jnp.float32
    )
    grad_h_own = grad_h_part[:own_rows] + send_core(
        grad_h_part[own_rows:].astype(jnp.bfloat16)
    ).astype(jnp.float32)
    grad_lat_raw, grad_norm_latent = norm_back(
        own_side[:, :LATENT], normed_lat, scale_lat, norm_latent
    )
    grad_compressed = jnp.concatenate(
        [grad_lat_raw, unrotate(own_side[:, LATENT:], cos_own, sin_own)], axis=-1
    ).astype(jnp.bfloat16)
    grad_latent = product("td,tc->dc", h_own, grad_compressed)
    grad_h = grad_h_own + product("tc,dc->td", grad_compressed, w_latent)
    grad_in, grad_norm_attn = norm_back(grad_h, normed_one, scale_one, norm_attn)
    grad_inputs = grad_mid + grad_in

    share = width // expert_size
    low_rows = expert_size * share
    own_part = share // tensor_size

    def in_two(values):
        high = lax.reduce_precision(values, 8, 7)
        return jnp.stack([high, values - high], axis=-1)

    gains = in_two(grad_norm_latent).reshape(expert_size * tensor_size, -1, 2)
    gain_rows = gains.shape[1]
    gains = jnp.pad(gains, ((0, 0), (0, own_part - gain_rows), (0, 0))).reshape(low_rows, 2)
    small = jnp.concatenate(
        [grad_router, in_two(grad_norm_attn), in_two(grad_norm_moe), gains], axis=1
    )
    small = jnp.pad(small, ((0, 0), (0, EXTRA - small.shape[1])))
    small, grad_latent = [
        v.astype(jnp.bfloat16).reshape(expert_size, tensor_size, own_part, -1)
        for v in (small, grad_latent)
    ]
    grad_output = grad_output.astype(jnp.bfloat16).reshape(expert_size, share, -1)
    grad_query = grad_query.astype(jnp.bfloat16).reshape(expert_size, share, -1)
    grad_expand = grad_expand.astype(jnp.bfloat16).reshape(expert_size, -1, w_expand.shape[1])
    grad_output, grad_query, grad_expand, grad_latent, small = sum_over_chips(
        2,
        [
            (0, [grad_output], 256),
            (0, [grad_query], 384),
            (0, [grad_expand], 512),
            (1, [grad_latent], 0),
            (1, [small], 0),
        ],
    )
    grad_router = small[:, :experts]
    grad_norm_attn = small[:, experts] + small[:, experts + 1]
    grad_norm_moe = small[:, experts + 2] + small[:, experts + 3]
    grad_norm_latent = (small[:, experts + 4] + small[:, experts + 5])[:gain_rows]

    rows, pair_grads, hidden, grad_gate, grad_up = kept[:5]
    grad_expert_down = product("jsd,jsf->jdf", pair_grads, hidden)
    grad_expert_gate = product("jsd,jsf->jdf", rows, grad_gate)
    grad_expert_up = product("jsd,jsf->jdf", rows, grad_up)
    columns = w_shared_gate.shape[1]
    shared_grads = shared_grads[: columns // EXTRA].reshape(-1, 3, EXTRA, share)
    shared_grads = (
        jnp.transpose(shared_grads, (1, 3, 0, 2)).reshape(3, share, columns).astype(jnp.float32)
    )
    return (
        output,
        grad_inputs,
        grad_norm_attn,
        grad_query,
        grad_latent,
        grad_norm_latent,
        grad_expand,
        grad_output,
        grad_norm_moe,
        grad_router,
        shared_grads[0],
        shared_grads[1],
        shared_grads[2],
        grad_expert_gate,
        grad_expert_up,
        grad_expert_down,
    )


def per_device_for(mesh):
    if mesh.shape[EXPERT] == PLANES * 4 and mesh.shape[TENSOR] == 2:
        return per_device_gathered
    return per_device_exchanged


def solution(mesh):
    return jax.shard_map(
        per_device_for(mesh),
        mesh=mesh,
        in_specs=(
            P((EXPERT, TENSOR), None),
            P(),
            P(None, TENSOR),
            P(),
            P(),
            P(None, TENSOR),
            P(None, TENSOR),
            P(),
            P(),
            P(None, TENSOR),
            P(None, TENSOR),
            P(None, TENSOR),
            P(EXPERT, None, TENSOR),
            P(EXPERT, None, TENSOR),
            P(EXPERT, None, TENSOR),
            P((EXPERT, TENSOR), None),
            P((EXPERT, TENSOR), None),
        ),
        out_specs=(
            P((EXPERT, TENSOR), None),
            P((EXPERT, TENSOR), None),
            P((EXPERT, TENSOR)),
            P(EXPERT, TENSOR),
            P((EXPERT, TENSOR), None),
            P((EXPERT, TENSOR)),
            P(EXPERT, TENSOR),
            P(EXPERT, TENSOR),
            P((EXPERT, TENSOR)),
            P((EXPERT, TENSOR), None),
            P(EXPERT, TENSOR),
            P(EXPERT, TENSOR),
            P(EXPERT, TENSOR),
            P(EXPERT, None, TENSOR),
            P(EXPERT, None, TENSOR),
            P(EXPERT, None, TENSOR),
        ),
        check_vma=False,
    )
```

```python
import functools
import math

import jax
import jax.numpy as jnp
from jax import lax
from jax.experimental import pallas as pl
from jax.experimental.pallas import tpu as pltpu
from jax.sharding import PartitionSpec as P

EXPERT = "expert"
TENSOR = "tensor"
NOPE = 128
ROPE = 64
VD = 128
LATENT = 512
TOPK = 6


EPS = 1e-06


def rope_tables(positions, width):
    half = width // 2
    freq = 10000.0 ** (-(jnp.arange(half, dtype=jnp.float32) * 2.0) / width)
    angle = positions.astype(jnp.float32)[:, None] * freq[None, :]
    return (jnp.cos(angle), jnp.sin(angle))


def rotate(values, cosine, sine):
    half = values.shape[-1] // 2
    first = values[..., :half]
    second = values[..., half:]
    return jnp.concatenate(
        [first * cosine - second * sine, first * sine + second * cosine], axis=-1
    )


def unrotate(grads, cosine, sine):
    half = grads.shape[-1] // 2
    first = grads[..., :half]
    second = grads[..., half:]
    return jnp.concatenate(
        [first * cosine + second * sine, second * cosine - first * sine], axis=-1
    )


def norm_back(grad_out, normed, scale, gain):
    scaled = grad_out * gain
    grad_in = scale * (scaled - normed * jnp.mean(scaled * normed, axis=-1, keepdims=True))
    return (grad_in, jnp.sum(grad_out * normed, axis=0))


def masked_scores(rows_query, key_full, first_row, scale):
    block = rows_query.shape[0]
    scores = (
        jnp.einsum("qhd,khd->hqk", rows_query, key_full, preferred_element_type=jnp.float32) * scale
    )
    allowed = (first_row + jnp.arange(block))[:, None] >= jnp.arange(key_full.shape[0])[None, :]
    return jnp.where(allowed[None], scores, -1e30)


def attention_forward(query, key_full, value, scale):
    seq_rows = query.shape[0]
    block = min(seq_rows, 512)

    def one_block(index):
        first_row = index * block
        scores = masked_scores(query, key_full, first_row, scale)
        peak = jnp.max(scores, axis=-1, keepdims=True)
        weights = jnp.exp(scores - peak)
        total = jnp.sum(weights, axis=-1, keepdims=True)
        probs = (weights / total).astype(jnp.bfloat16)
        result = jnp.einsum("hqk,khd->qhd", probs, value, preferred_element_type=jnp.float32)
        return (result.astype(jnp.bfloat16), (peak + jnp.log(total))[..., 0])

    results, log_totals = lax.map(one_block, jnp.arange(seq_rows // block))
    return (results.reshape(seq_rows, query.shape[1], value.shape[2]), log_totals)


def attention_backward(query, key_full, value, grad_attended, log_totals, scale):
    seq_rows = query.shape[0]
    block = min(seq_rows, 512)

    def one_block(carry, index):
        grad_key, grad_value = carry
        first_row = index * block
        scores = masked_scores(query, key_full, first_row, scale)
        probs = jnp.exp(scores - log_totals[index][..., None])
        grad_probs = jnp.einsum(
            "qhv,khv->hqk", grad_attended, value, preferred_element_type=jnp.float32
        )
        centre = jnp.sum(probs * grad_probs, axis=-1, keepdims=True)
        grad_scores = (probs * (grad_probs - centre)).astype(jnp.bfloat16)
        grad_rows = (
            jnp.einsum("hqk,khd->qhd", grad_scores, key_full, preferred_element_type=jnp.float32)
            * scale
        )
        grad_key = (
            grad_key
            + jnp.einsum("hqk,qhd->khd", grad_scores, query, preferred_element_type=jnp.float32)
            * scale
        )
        grad_value = grad_value + jnp.einsum(
            "hqk,qhv->khv",
            probs.astype(jnp.bfloat16),
            grad_attended,
            preferred_element_type=jnp.float32,
        )
        return ((grad_key, grad_value), grad_rows)

    start_key = jnp.zeros(key_full.shape, jnp.float32)
    start_value = jnp.zeros(value.shape, jnp.float32)
    (grad_key, grad_value), grad_query = lax.scan(
        one_block, (start_key, start_value), jnp.arange(seq_rows // block)
    )
    return (grad_query.reshape(query.shape), grad_key, grad_value)


def to_experts(grid, rows):
    gathered, rows_all = (
        lax.all_gather(grid, TENSOR, axis=0, tiled=True),
        lax.all_gather(rows, TENSOR, axis=0, tiled=True),
    )
    received = lax.all_to_all(gathered, EXPERT, split_axis=1, concat_axis=1, tiled=True)
    return (received, rows_all)


def from_experts(expert_part, shared_part):
    returned = lax.all_to_all(expert_part, EXPERT, split_axis=1, concat_axis=1, tiled=True)
    summed, shared_sum = (
        lax.psum_scatter(returned, TENSOR, scatter_dimension=0, tiled=True).astype(jnp.float32),
        lax.psum_scatter(shared_part, TENSOR, scatter_dimension=0, tiled=True).astype(
            jnp.float32
        ),
    )
    return (summed, shared_sum)


def per_device_exchanged(
    inputs,
    norm_attn,
    w_query,
    w_latent,
    norm_latent,
    w_expand,
    w_output,
    norm_moe,
    w_router,
    w_shared_gate,
    w_shared_up,
    w_shared_down,
    w_expert_gate,
    w_expert_up,
    w_expert_down,
    routes,
    cotangent,
):
    own_rows = inputs.shape[0]
    width = inputs.shape[1]
    tensor_size = lax.axis_size(TENSOR)
    expert_size = lax.axis_size(EXPERT)
    tensor_index = lax.axis_index(TENSOR)
    seq_rows = own_rows * tensor_size
    local_heads = w_query.shape[1] // (NOPE + ROPE)
    experts = w_router.shape[1]
    local_experts = experts // expert_size
    capacity = own_rows * TOPK * 4 // (3 * experts)
    scale = 1.0 / math.sqrt(NOPE + ROPE)
    flat_in = inputs.astype(jnp.float32)
    scale_one = lax.rsqrt(jnp.mean(flat_in * flat_in, axis=-1, keepdims=True) + EPS)
    normed_one = flat_in * scale_one
    h_own = (normed_one * norm_attn).astype(jnp.bfloat16)
    compressed = jnp.dot(h_own, w_latent, preferred_element_type=jnp.float32)
    lat_raw = compressed[:, :LATENT]
    scale_lat = lax.rsqrt(jnp.mean(lat_raw * lat_raw, axis=-1, keepdims=True) + EPS)
    normed_lat = lat_raw * scale_lat
    lat_own = (normed_lat * norm_latent).astype(jnp.bfloat16)
    cos_own, sin_own = rope_tables(tensor_index * own_rows + jnp.arange(own_rows), ROPE)
    rope_own = rotate(compressed[:, LATENT:], cos_own, sin_own).astype(jnp.bfloat16)
    h_all, lat_all, rope_all = (
        lax.all_gather(h_own, TENSOR, axis=0, tiled=True),
        lax.all_gather(lat_own, TENSOR, axis=0, tiled=True),
        lax.all_gather(rope_own, TENSOR, axis=0, tiled=True),
    )
    cos_all, sin_all = rope_tables(jnp.arange(seq_rows), ROPE)
    cos_all = cos_all[:, None, :]
    sin_all = sin_all[:, None, :]
    query_raw = jnp.dot(h_all, w_query, preferred_element_type=jnp.float32).reshape(
        seq_rows, local_heads, NOPE + ROPE
    )
    query = jnp.concatenate(
        [query_raw[..., :NOPE], rotate(query_raw[..., NOPE:], cos_all, sin_all)], axis=-1
    ).astype(jnp.bfloat16)
    expanded = jnp.dot(lat_all, w_expand, preferred_element_type=jnp.float32).astype(jnp.bfloat16)
    expanded = expanded.reshape(seq_rows, local_heads, NOPE + VD)
    key_full = jnp.concatenate(
        [
            expanded[..., :NOPE],
            jnp.broadcast_to(rope_all[:, None, :], (seq_rows, local_heads, ROPE)),
        ],
        axis=-1,
    )
    value = expanded[..., NOPE:]
    attended, log_totals = attention_forward(query, key_full, value, scale)
    attended_flat = attended.reshape(seq_rows, local_heads * VD)
    attn_terms = jnp.einsum(
        "sv,dv->sd", attended_flat, w_output, preferred_element_type=jnp.float32
    )
    after_attn = flat_in + lax.psum_scatter(
        attn_terms.astype(jnp.bfloat16), TENSOR, scatter_dimension=0, tiled=True
    ).astype(jnp.float32)
    scale_two = lax.rsqrt(jnp.mean(after_attn * after_attn, axis=-1, keepdims=True) + EPS)
    normed_two = after_attn * scale_two
    h_moe = (normed_two * norm_moe).astype(jnp.bfloat16)
    logits = jnp.dot(h_moe, w_router, preferred_element_type=jnp.float32)
    expert_ids = jnp.arange(experts, dtype=jnp.int32)
    route_hot = (routes[:, :, None] == expert_ids[None, None, :]).astype(jnp.float32)
    gates = jax.nn.softmax(jnp.sum(route_hot * logits[:, None, :], axis=-1), axis=-1)
    flat_routes = routes.reshape(-1)
    pair_hot = (flat_routes[:, None] == expert_ids[None, :]).astype(jnp.int32)
    earlier = jnp.cumsum(pair_hot, axis=0, dtype=jnp.int32) - pair_hot
    slots = jnp.sum(earlier * pair_hot, axis=1, dtype=jnp.int32) * experts + flat_routes
    grid_shape = (capacity, expert_size, local_experts, width)

    def to_slots(pair_rows):
        placed = jnp.zeros((capacity * experts, width), jnp.bfloat16).at[slots].set(pair_rows)
        return placed.reshape(grid_shape)

    def from_slots(grid):
        return grid.reshape(capacity * experts, width)[slots].reshape(own_rows, TOPK, width)

    received, h_moe_all = to_experts(to_slots(jnp.repeat(h_moe, TOPK, axis=0)), h_moe)
    gate_act = jnp.einsum(
        "cnjd,jdf->cnjf", received, w_expert_gate, preferred_element_type=jnp.float32
    )
    up_act = jnp.einsum("cnjd,jdf->cnjf", received, w_expert_up, preferred_element_type=jnp.float32)
    hidden = (jax.nn.silu(gate_act) * up_act).astype(jnp.bfloat16)
    expert_part = jnp.einsum(
        "cnjf,jdf->cnjd", hidden, w_expert_down, preferred_element_type=jnp.float32
    ).astype(jnp.bfloat16)
    shared_gate_act = jnp.dot(h_moe_all, w_shared_gate, preferred_element_type=jnp.float32)
    shared_up_act = jnp.dot(h_moe_all, w_shared_up, preferred_element_type=jnp.float32)
    shared_hidden = (jax.nn.silu(shared_gate_act) * shared_up_act).astype(jnp.bfloat16)
    shared_part = jnp.einsum(
        "sf,df->sd", shared_hidden, w_shared_down, preferred_element_type=jnp.float32
    ).astype(jnp.bfloat16)
    expert_out, shared_out = from_experts(expert_part, shared_part)
    picked = from_slots(expert_out)
    output = (after_attn + jnp.sum(gates[:, :, None] * picked, axis=1) + shared_out).astype(
        jnp.bfloat16
    )
    grad_out = cotangent.astype(jnp.float32)
    grad_gates = jnp.sum(picked * grad_out[:, None, :], axis=-1)
    grad_select = gates * (grad_gates - jnp.sum(gates * grad_gates, axis=-1, keepdims=True))
    grad_logits = jnp.sum(grad_select[:, :, None] * route_hot, axis=1).astype(jnp.bfloat16)
    grad_router = jnp.einsum("td,te->de", h_moe, grad_logits, preferred_element_type=jnp.float32)
    pair_grads = (
        (gates[:, :, None] * grad_out[:, None, :])
        .astype(jnp.bfloat16)
        .reshape(own_rows * TOPK, width)
    )
    grad_received, cot_all = to_experts(to_slots(pair_grads), cotangent)
    grad_hidden = jnp.einsum(
        "cnjd,jdf->cnjf", grad_received, w_expert_down, preferred_element_type=jnp.float32
    )
    sigma = jax.nn.sigmoid(gate_act)
    grad_up = (grad_hidden * gate_act * sigma).astype(jnp.bfloat16)
    grad_gate = (grad_hidden * up_act * sigma * (1.0 + gate_act * (1.0 - sigma))).astype(
        jnp.bfloat16
    )
    grad_expert_down = jnp.einsum(
        "cnjd,cnjf->jdf", grad_received, hidden, preferred_element_type=jnp.float32
    )
    grad_expert_gate = jnp.einsum(
        "cnjd,cnjf->jdf", received, grad_gate, preferred_element_type=jnp.float32
    )
    grad_expert_up = jnp.einsum(
        "cnjd,cnjf->jdf", received, grad_up, preferred_element_type=jnp.float32
    )
    grad_rows_part = (
        jnp.einsum("cnjf,jdf->cnjd", grad_gate, w_expert_gate, preferred_element_type=jnp.float32)
        + jnp.einsum("cnjf,jdf->cnjd", grad_up, w_expert_up, preferred_element_type=jnp.float32)
    ).astype(jnp.bfloat16)
    shared_grad_hidden = jnp.einsum(
        "sd,df->sf", cot_all, w_shared_down, preferred_element_type=jnp.float32
    )
    shared_sigma = jax.nn.sigmoid(shared_gate_act)
    shared_grad_up = (shared_grad_hidden * shared_gate_act * shared_sigma).astype(jnp.bfloat16)
    shared_grad_gate = (
        shared_grad_hidden
        * shared_up_act
        * shared_sigma
        * (1.0 + shared_gate_act * (1.0 - shared_sigma))
    ).astype(jnp.bfloat16)
    grad_shared_down = jnp.einsum(
        "sd,sf->df", cot_all, shared_hidden, preferred_element_type=jnp.float32
    )
    grad_shared_gate = jnp.einsum(
        "sd,sf->df", h_moe_all, shared_grad_gate, preferred_element_type=jnp.float32
    )
    grad_shared_up = jnp.einsum(
        "sd,sf->df", h_moe_all, shared_grad_up, preferred_element_type=jnp.float32
    )
    shared_rows_part = (
        jnp.einsum("sf,df->sd", shared_grad_gate, w_shared_gate, preferred_element_type=jnp.float32)
        + jnp.einsum("sf,df->sd", shared_grad_up, w_shared_up, preferred_element_type=jnp.float32)
    ).astype(jnp.bfloat16)
    grad_rows, grad_shared_rows = from_experts(grad_rows_part, shared_rows_part)
    grad_moe = (
        jnp.sum(from_slots(grad_rows), axis=1)
        + grad_shared_rows
        + jnp.einsum("te,de->td", grad_logits, w_router, preferred_element_type=jnp.float32)
    )
    grad_mid, grad_norm_moe = norm_back(grad_moe, normed_two, scale_two, norm_moe)
    grad_mid = grad_mid + grad_out
    grad_attn = grad_mid.astype(jnp.bfloat16)
    grad_attn_all = lax.all_gather(grad_attn, TENSOR, axis=0, tiled=True)
    grad_output = jnp.einsum(
        "sd,sv->dv", grad_attn_all, attended_flat, preferred_element_type=jnp.float32
    )
    grad_attended = jnp.einsum(
        "sd,dv->sv", grad_attn_all, w_output, preferred_element_type=jnp.float32
    )
    grad_attended = grad_attended.astype(jnp.bfloat16).reshape(seq_rows, local_heads, VD)
    grad_query_full, grad_key_full, grad_value = attention_backward(
        query, key_full, value, grad_attended, log_totals, scale
    )
    grad_query_raw = jnp.concatenate(
        [grad_query_full[..., :NOPE], unrotate(grad_query_full[..., NOPE:], cos_all, sin_all)],
        axis=-1,
    )
    grad_query_raw = grad_query_raw.astype(jnp.bfloat16).reshape(
        seq_rows, local_heads * (NOPE + ROPE)
    )
    grad_query = jnp.einsum("sd,sq->dq", h_all, grad_query_raw, preferred_element_type=jnp.float32)
    grad_expanded = jnp.concatenate([grad_key_full[..., :NOPE], grad_value], axis=-1)
    grad_expanded = grad_expanded.astype(jnp.bfloat16).reshape(seq_rows, local_heads * (NOPE + VD))
    grad_expand = jnp.einsum(
        "sl,sk->lk", lat_all, grad_expanded, preferred_element_type=jnp.float32
    )
    grad_rope_part = jnp.sum(grad_key_full[..., NOPE:], axis=1)
    grad_h_part = jnp.einsum(
        "sq,dq->sd", grad_query_raw, w_query, preferred_element_type=jnp.float32
    )
    grad_lat_part = jnp.einsum(
        "sk,lk->sl", grad_expanded, w_expand, preferred_element_type=jnp.float32
    )
    grad_h_own, grad_lat_own, grad_rope_own = (
        lax.psum_scatter(
            grad_h_part.astype(jnp.bfloat16), TENSOR, scatter_dimension=0, tiled=True
        ).astype(jnp.float32),
        lax.psum_scatter(
            grad_lat_part.astype(jnp.bfloat16), TENSOR, scatter_dimension=0, tiled=True
        ).astype(jnp.float32),
        lax.psum_scatter(
            grad_rope_part.astype(jnp.bfloat16), TENSOR, scatter_dimension=0, tiled=True
        ).astype(jnp.float32),
    )
    grad_lat_raw, grad_norm_latent = norm_back(grad_lat_own, normed_lat, scale_lat, norm_latent)
    grad_compressed = jnp.concatenate(
        [grad_lat_raw, unrotate(grad_rope_own, cos_own, sin_own)], axis=-1
    ).astype(jnp.bfloat16)
    grad_latent = jnp.einsum(
        "td,tc->dc", h_own, grad_compressed, preferred_element_type=jnp.float32
    )
    grad_h = grad_h_own + jnp.einsum(
        "tc,dc->td", grad_compressed, w_latent, preferred_element_type=jnp.float32
    )
    grad_in, grad_norm_attn = norm_back(grad_h, normed_one, scale_one, norm_attn)
    grad_inputs = grad_mid + grad_in
    grad_query, grad_expand, grad_output, grad_shared_gate, grad_shared_up, grad_shared_down = (
        lax.psum_scatter(
            grad_query.astype(jnp.bfloat16), EXPERT, scatter_dimension=0, tiled=True
        ).astype(jnp.float32),
        lax.psum_scatter(
            grad_expand.astype(jnp.bfloat16), EXPERT, scatter_dimension=0, tiled=True
        ).astype(jnp.float32),
        lax.psum_scatter(
            grad_output.astype(jnp.bfloat16), EXPERT, scatter_dimension=0, tiled=True
        ).astype(jnp.float32),
        lax.psum_scatter(
            grad_shared_gate.astype(jnp.bfloat16), EXPERT, scatter_dimension=0, tiled=True
        ).astype(jnp.float32),
        lax.psum_scatter(
            grad_shared_up.astype(jnp.bfloat16), EXPERT, scatter_dimension=0, tiled=True
        ).astype(jnp.float32),
        lax.psum_scatter(
            grad_shared_down.astype(jnp.bfloat16), EXPERT, scatter_dimension=0, tiled=True
        ).astype(jnp.float32),
    )
    grad_latent, grad_router, grad_norm_attn, grad_norm_moe, grad_norm_latent = (
        lax.psum_scatter(grad_latent, (EXPERT, TENSOR), scatter_dimension=0, tiled=True),
        lax.psum_scatter(grad_router, (EXPERT, TENSOR), scatter_dimension=0, tiled=True),
        lax.psum_scatter(grad_norm_attn, (EXPERT, TENSOR), scatter_dimension=0, tiled=True),
        lax.psum_scatter(grad_norm_moe, (EXPERT, TENSOR), scatter_dimension=0, tiled=True),
        lax.psum_scatter(grad_norm_latent, (EXPERT, TENSOR), scatter_dimension=0, tiled=True),
    )
    return (
        output,
        grad_inputs,
        grad_norm_attn,
        grad_query,
        grad_latent,
        grad_norm_latent,
        grad_expand,
        grad_output,
        grad_norm_moe,
        grad_router,
        grad_shared_gate,
        grad_shared_up,
        grad_shared_down,
        grad_expert_gate,
        grad_expert_up,
        grad_expert_down,
    )


PLANES = 4


def send_core(values):
    return lax.ppermute(values, TENSOR, [(0, 1), (1, 0)])


def chip_pairs(move):
    chips = [(z, y, x) for z in range(PLANES) for y in range(2) for x in range(2)]
    moved = [move(*chip) for chip in chips]
    return [tuple((z * 2 + y) * 2 + x for z, y, x in pair) for pair in zip(chips, moved)]


def send_x(values):
    return lax.ppermute(values, EXPERT, chip_pairs(lambda z, y, x: (z, y, 1 - x)))


def send_y(values):
    return lax.ppermute(values, EXPERT, chip_pairs(lambda z, y, x: (z, 1 - y, x)))


def product(form, left, right):
    return jnp.einsum(form, left, right, preferred_element_type=jnp.float32)


EXTRA = 128
VMEM_LIMIT = 54 << 20
MESH = pl.DeviceIdType.MESH


def dot(left, right):
    return jnp.dot(left, right, preferred_element_type=jnp.float32)


def dot_nt(left, right):
    return lax.dot_general(
        left, right, (((1,), (1,)), ((), ())), preferred_element_type=jnp.float32
    )


def dot_tn(left, right):
    return lax.dot_general(
        left, right, (((0,), (0,)), ((), ())), preferred_element_type=jnp.float32
    )


class Chips:
    def __init__(self):
        index = lax.axis_index(EXPERT)
        self.z, self.y, self.x = index // 4, (index // 2) % 2, index % 2
        self.core = lax.axis_index(TENSOR)
        self.to_x = {EXPERT: self.at(self.z, self.y, 1 - self.x)}
        self.to_y = {EXPERT: self.at(self.z, 1 - self.y, self.x)}
        self.to_core = {TENSOR: 1 - self.core}

    def at(self, z, y, x):
        return (z * 2 + y) * 2 + x

    def to_z(self, distance):
        return {EXPERT: self.at((self.z + distance) % PLANES, self.y, self.x)}

    def places(self, step):
        plane = (self.z + PLANES - step) % PLANES
        x, y = self.x, self.y
        return [
            self.at(plane, row, column)
            for row, column in ((y, x), (y, 1 - x), (1 - y, x), (1 - y, 1 - x))
        ]


def greet(partners):
    barrier = pltpu.get_barrier_semaphore()
    for partner in partners:
        pl.semaphore_signal(barrier, inc=1, device_id=partner, device_id_type=MESH)
    pl.semaphore_wait(barrier, len(partners))


def add_rows(target, terms):
    @pl.loop(0, target.shape[0] // 16)
    def _(chunk):
        rows = pl.ds(pl.multiple_of(chunk * 16, 16), 16)
        total = terms[0][rows, :].astype(jnp.float32)
        for term in terms[1:]:
            total = total + term[rows, :].astype(jnp.float32)
        target[rows, :] = total.astype(target.dtype)


def sum_kernel(parts, exchanged, *refs):
    chips = Chips()
    refs = list(refs)
    arrays = 1 + max(part[0] for part in parts)
    kind_of = {part[0]: part[1] for part in parts}
    sources = [[refs.pop(0) for _ in range(2 if kind_of[a] == 2 else 1)] for a in range(arrays)]
    blocks = refs.pop(0) if exchanged else None
    results = [refs.pop(0) for _ in range(arrays)]
    arrived = refs.pop(0) if exchanged else None
    boxes = []
    for _, kind, _, _, _ in parts:
        mine = refs.pop(0)
        from_core = refs.pop(0) if kind else None
        boxes.append((mine, from_core) + tuple(refs.pop(0) for _ in range(4)))
    if exchanged:
        by_x, by_y, x_send, x_recv, z_send, z_recv = [refs.pop(0) for _ in range(6)]
    load_sem, send_sem, recv_sem = refs
    each = list(range(len(parts)))

    def copy_to(source, target, send, recv, to):
        return pltpu.make_async_remote_copy(
            src_ref=source,
            dst_ref=target,
            send_sem=send,
            recv_sem=recv,
            device_id=to,
            device_id_type=MESH,
        )

    def remote(part, step, index, source, target, to):
        sems = (send_sem.at[part, step, index], recv_sem.at[part, step, index])
        return copy_to(source, target, *sems, to)

    def loads(part, step):
        array, kind, start, stop, _ = parts[part]
        mine, source = boxes[part][0], sources[array]
        for k, place in enumerate(chips.places(step)):
            if kind == 2:
                block = source[0].at[step, k, :, start:stop]
            elif kind == 1:
                block = source[0].at[place, chips.core, :, start:stop]
            else:
                block = source[0].at[place, :, start:stop]
            yield pltpu.make_async_copy(block, mine.at[step, k], load_sem.at[part, step, k])

    def core_copies(part, step):
        array, kind, start, stop, _ = parts[part]
        if kind == 0:
            return
        for k, place in enumerate(chips.places(step)):
            if kind == 2:
                block = sources[array][1].at[step, k, :, start:stop]
            else:
                block = sources[array][0].at[place, 1 - chips.core, :, start:stop]
            target = boxes[part][1].at[step, k]
            yield remote(part, step, k, block, target, chips.to_core)

    def level(part, step):
        return 0 if parts[part][4] else step

    def corner_copies(part, step):
        mine, _, corners = boxes[part][:3]
        half = mine.shape[2] // 2
        here = corners.at[level(part, step)]
        yield remote(part, step, 4, mine.at[step, 3, :half], here.at[0], chips.to_y)
        yield remote(part, step, 5, mine.at[step, 3, half:], here.at[1], chips.to_x)

    def early_copies(part, step):
        mine, from_x, from_y = boxes[part][0], boxes[part][3], boxes[part][4]
        half = mine.shape[2] // 2
        x, y = from_x.at[level(part, step)], from_y.at[level(part, step)]
        yield remote(part, step, 6, mine.at[step, 1, half:], x.at[half:], chips.to_x)
        yield remote(part, step, 7, mine.at[step, 2, :half], y.at[:half], chips.to_y)

    def late_copies(part, step):
        mine, from_x, from_y = boxes[part][0], boxes[part][3], boxes[part][4]
        half = mine.shape[2] // 2
        x, y = from_x.at[level(part, step)], from_y.at[level(part, step)]
        yield remote(part, step, 9, mine.at[step, 1, :half], x.at[:half], chips.to_x)
        yield remote(part, step, 10, mine.at[step, 2, half:], y.at[half:], chips.to_y)

    def side_copies(part, step):
        return [*early_copies(part, step), *late_copies(part, step)]

    def z_copy(part, step):
        mine, from_z = boxes[part][0], boxes[part][5]
        source = mine.at[step] if parts[part][4] else mine.at[step, 0]
        return remote(part, step, 8, source, from_z.at[step - 1], chips.to_z(1))

    def x_copy():
        return copy_to(
            blocks.at[:, :, 1 - chips.x], by_x, x_send.at[0], x_recv.at[0], chips.to_x
        )

    def y_copies():
        own = blocks.at[:, 1 - chips.y, chips.x]
        passed = by_x.at[:, 1 - chips.y]
        return [
            copy_to(source, by_y.at[k], x_send.at[1 + k], x_recv.at[1 + k], chips.to_y)
            for k, source in enumerate((own, passed))
        ]

    def gathered(plane):
        return [
            blocks.at[plane, chips.y, chips.x],
            by_x.at[plane, chips.y],
            by_y.at[0, plane],
            by_y.at[1, plane],
        ]

    def z_sends(distance):
        plane = (chips.z + distance) % PLANES
        return [
            copy_to(
                source,
                arrived.at[place],
                z_send.at[distance, k],
                z_recv.at[distance, k],
                chips.to_z(distance),
            )
            for k, (source, place) in enumerate(zip(gathered(plane), chips.places(0)))
        ]

    def z_arrivals(distance):
        plane = (chips.z + distance) % PLANES
        return [
            copy_to(
                source,
                arrived.at[place],
                z_send.at[distance, k],
                z_recv.at[distance, k],
                chips.to_z(distance),
            )
            for k, (source, place) in enumerate(zip(gathered(plane), chips.places(distance)))
        ]

    def keeps():
        return [
            pltpu.make_async_copy(source, arrived.at[place], z_send.at[0, k])
            for k, (source, place) in enumerate(zip(gathered(chips.z), chips.places(0)))
        ]

    order = [*range(1, PLANES), 0]
    distances = range(1, PLANES) if exchanged else (1, PLANES - 1)
    greet([chips.to_x, chips.to_y, chips.to_core] + [chips.to_z(k) for k in distances])
    if exchanged:
        x_copy().start()

    def fetch(step):
        for part in each:
            for copy in core_copies(part, step):
                copy.start()
            for copy in loads(part, step):
                copy.start(priority=1)

    fetch(order[0])
    fetch(order[1])

    def chip_sum(step):
        ahead = order.index(step) + 2
        for part in each:
            mine, from_core = boxes[part][:2]
            for copy in loads(part, step):
                copy.wait()
            for copy in core_copies(part, step):
                copy.wait_recv()
            for k in (3, 1, 2, 0):
                if from_core is not None:
                    add_rows(mine.at[step, k], [mine.at[step, k], from_core.at[step, k]])
                if k == 3 and not parts[part][4]:
                    for copy in corner_copies(part, step):
                        copy.start()
            if not parts[part][4]:
                for copy in early_copies(part, step):
                    copy.start()
        if ahead < PLANES:
            fetch(order[ahead])

    def z_sum(step):
        for part in each:
            if parts[part][4]:
                part_z_sum(part, step)

    def part_z_sum(part, step):
        mine, from_z = boxes[part][0], boxes[part][5]
        if step != 1:
            before = (step - 1) % PLANES
            z_copy(part, before).wait_recv()
            for k in (3, 1, 2, 0):
                add_rows(mine.at[step, k], [mine.at[step, k], from_z.at[before - 1, k]])
        if step:
            z_copy(part, step).start()
        else:
            for copy in [*corner_copies(part, step), *early_copies(part, step)]:
                copy.start()

    def side_sum(step):
        for part in each:
            if parts[part][4] and step:
                continue
            mine, _, corners = boxes[part][:3]
            half = mine.shape[2] // 2
            for copy in corner_copies(part, step):
                copy.wait_recv()
            low_half, high_half = mine.at[step, 1, :half], mine.at[step, 2, half:]
            here = corners.at[level(part, step)]
            add_rows(low_half, [low_half, here.at[0]])
            add_rows(high_half, [high_half, here.at[1]])
            for copy in late_copies(part, step):
                copy.start()

    def plane_sum(step):
        for part in each:
            array, _, start, stop, along_z = parts[part]
            if along_z and step:
                continue
            mine, _, _, from_x, from_y, from_z = boxes[part]
            here = level(part, step)
            terms = [mine.at[step, 0], from_x.at[here], from_y.at[here]]
            for copy in side_copies(part, step):
                copy.wait_recv()
            if step != 1 and not along_z:
                before = (step - 1) % PLANES
                z_copy(part, before).wait_recv()
                terms.append(from_z.at[before - 1])
            if step == 0:
                add_rows(results[array].at[:, start:stop], terms)
            else:
                add_rows(mine.at[step, 0], terms)
                z_copy(part, step).start()

    stages = ((0, chip_sum), (1, side_sum), (0, z_sum), (2, plane_sum))
    for tick in range(PLANES + 2):
        for late, stage in stages:
            if 0 <= tick - late < PLANES:
                stage(order[tick - late])
        if exchanged and tick == 0:
            x_copy().wait_recv()
            for copy in y_copies():
                copy.start()
        if exchanged and tick == 1:
            for copy in y_copies():
                copy.wait_recv()
            for copy in keeps():
                copy.start()
            for distance in range(1, PLANES):
                for copy in z_sends(distance):
                    copy.start()
    if exchanged:
        for copy in [x_copy(), *y_copies()]:
            copy.wait_send()
        for copy in keeps():
            copy.wait()
        for distance in range(1, PLANES):
            for copy in z_arrivals(distance):
                copy.wait_recv()
            for copy in z_sends(distance):
                copy.wait_send()
    for part in each:
        along_z = parts[part][4]
        for step in range(PLANES):
            sent = [*core_copies(part, step)]
            if step == 0 or not along_z:
                sent += [*corner_copies(part, step), *side_copies(part, step)]
            if step:
                sent.append(z_copy(part, step))
            for copy in sent:
                copy.wait_send()


def sum_over_chips(collective_id, arrays, blocks=None):
    low = jnp.bfloat16
    parts, scratch, shapes = [], [], []
    for index, (kind, operands, z_columns) in enumerate(arrays):
        rows, columns = operands[0].shape[-2:]
        shapes.append((rows, columns))
        for start, stop in ((0, columns - z_columns), (columns - z_columns, columns)):
            if start == stop:
                continue
            along_z = start > 0
            parts.append((index, kind, start, stop, along_z))
            size = (rows, stop - start)
            levels = 1 if along_z else PLANES
            scratch += [pltpu.VMEM((PLANES, 4) + size, low)] * (2 if kind else 1)
            scratch += [
                pltpu.VMEM((levels, 2, rows // 2, stop - start), low),
                pltpu.VMEM((levels,) + size, low),
                pltpu.VMEM((levels,) + size, low),
                pltpu.VMEM((PLANES - 1,) + ((4,) if along_z else ()) + size, low),
            ]
    operands = [operand for _, group, _ in arrays for operand in group]
    out_shape = [jax.ShapeDtypeStruct(shape, jnp.float32) for shape in shapes]
    out_specs = [pl.BlockSpec(memory_space=pltpu.VMEM)] * len(shapes)
    if blocks is not None:
        operands.append(blocks)
        block = blocks.shape[3:]
        out_shape.append(jax.ShapeDtypeStruct((PLANES * 4,) + block, low))
        out_specs.append(pl.BlockSpec(memory_space=pl.ANY))
        scratch += [
            pltpu.VMEM((PLANES, 2) + block, low),
            pltpu.VMEM((2, PLANES) + block, low),
            pltpu.SemaphoreType.DMA((3,)),
            pltpu.SemaphoreType.DMA((3,)),
            pltpu.SemaphoreType.DMA((PLANES, 4)),
            pltpu.SemaphoreType.DMA((PLANES, 4)),
        ]
    size = sum(rows * columns for rows, columns in shapes)
    semaphores = (len(parts), PLANES, 11)
    return pl.pallas_call(
        functools.partial(sum_kernel, tuple(parts), blocks is not None),
        in_specs=[pl.BlockSpec(memory_space=pl.ANY)] * len(operands),
        out_specs=out_specs,
        out_shape=out_shape,
        scratch_shapes=scratch
        + [
            pltpu.SemaphoreType.DMA((len(parts), PLANES, 4)),
            pltpu.SemaphoreType.DMA(semaphores),
            pltpu.SemaphoreType.DMA(semaphores),
        ],
        compiler_params=pltpu.CompilerParams(
            collective_id=collective_id, has_side_effects=True, vmem_limit_bytes=VMEM_LIMIT
        ),
        cost_estimate=pl.CostEstimate(
            flops=size * 30, bytes_accessed=size * 64, transcendentals=0
        ),
    )(*operands)


def gated(gate_act, up_act, grad_hidden):
    sigma = jax.nn.sigmoid(gate_act)
    silu = gate_act * sigma
    hidden = silu * up_act
    grad_gate = grad_hidden * up_act * sigma * (1.0 + gate_act * (1.0 - sigma))
    grad_up = grad_hidden * silu
    return tuple(v.astype(jnp.bfloat16) for v in (hidden, grad_gate, grad_up))


def moe_kernel(own_rows_in, lanes, w_gate, w_up, w_down, sw_gate, sw_up, sw_down, *refs):
    near, refs = refs[:3], refs[3:]
    land, out_mine, out_other, grad_mine, grad_other = refs[:5]
    rows_out, pairs_out, hidden_out, gate_out, up_out, shared_out = refs[5:11]
    rows_kept, grads_kept, out_kept, back_kept, extra_kept, s_hidden, s_grads, seats = refs[11:19]
    x_here, g_here, gate_here, up_here, down_here, s_in, s_down, sum_in, sum_down = refs[19:28]
    come, go, fetch, send_sem, recv_sem, z_send, z_recv = refs[28:]
    width, half = s_down.shape
    plane, step = pl.program_id(0), pl.program_id(1)
    experts, slots = out_kept.shape[:2]
    pairs, pair_rows_all, pair_slots = seats.shape
    own = slots // pairs
    low = jnp.bfloat16
    chips = Chips()

    def remote(step, index, source, target, to):
        return pltpu.make_async_remote_copy(
            src_ref=source,
            dst_ref=target,
            send_sem=send_sem.at[step, index],
            recv_sem=recv_sem.at[step, index],
            device_id=to,
            device_id_type=MESH,
        )

    def own_block(step):
        return own_rows_in if isinstance(step, int) and step == 0 else land.at[step, 0, 0]

    def side_copies(step):
        block = own_block(step)
        return [
            remote(step, 0, block, land.at[step, 0, 1], chips.to_x),
            remote(step, 1, block, land.at[step, 0, 2], chips.to_y),
        ]

    def corner_copies(step):
        return [
            remote(step, 2, land.at[step, 0, 1, 0], land.at[step, 0, 3, 0], chips.to_y),
            remote(step, 3, land.at[step, 0, 2, 1], land.at[step, 0, 3, 1], chips.to_x),
        ]

    def core_copy(step, k):
        if k < 3:
            source, target = land.at[step, 0, k] if k else own_block(step), land.at[step, 1, k]
        else:
            source, target = land.at[step, 0, 3, k - 3], land.at[step, 1, 3, k - 3]
        return remote(step, 4 + k, source, target, chips.to_core)

    def z_copy(k):
        return pltpu.make_async_remote_copy(
            src_ref=own_block(k - 1),
            dst_ref=land.at[k, 0, 0],
            send_sem=z_send.at[k],
            recv_sem=z_recv.at[k],
            device_id=chips.to_z(1),
            device_id_type=MESH,
        )

    def near_sides():
        own = own_rows_in.at[0]
        return [
            remote(0, 0, own, land.at[0, 0, 1, 0], chips.to_x),
            remote(0, 1, own, land.at[0, 0, 2, 0], chips.to_y),
        ]

    def near_corners():
        half = land.shape[4] // 2
        ends = (slice(0, half), slice(half, 2 * half))
        return [
            remote(0, 2 + k, land.at[0, 0, 1 + k, 0, rows], land.at[0, 0, 3, 0, rows], to)
            for k, (rows, to) in enumerate(zip(ends, (chips.to_y, chips.to_x)))
        ]

    def near_core(place):
        source = land.at[0, 0, place, 0]
        return remote(0, 4 + place, source, land.at[0, 1, place, 0], chips.to_core)

    def near_cores_at_once():
        own = remote(0, 4, own_rows_in, land.at[0, 1, 0], chips.to_core)
        return [own] + [
            remote(0, 8 + k, near[k], land.at[0, 1, 1 + k, 1], chips.to_core) for k in range(3)
        ]

    def start_plane(step):
        for copy in side_copies(step) + [core_copy(step, 0)]:
            copy.start()

    def pass_corners(step):
        for copy in side_copies(step):
            copy.wait_recv()
        for copy in corner_copies(step) + [core_copy(step, 1), core_copy(step, 2)]:
            copy.start()

    def finish_plane(step):
        for copy in corner_copies(step):
            copy.wait_recv()
        for k in (3, 4):
            core_copy(step, k).start()
        for k in range(5):
            core_copy(step, k).wait_recv()

    def weight_copies(expert):
        return [
            pltpu.make_async_copy(source.at[expert], target.at[expert], fetch.at[expert, k])
            for k, (source, target) in enumerate(
                ((w_gate, gate_here), (w_up, up_here), (w_down, down_here))
            )
        ]

    shared_blocks = sw_gate.shape[1] // half
    chip = chips.at(chips.z, chips.y, chips.x)
    shared_here = chip < shared_blocks

    def shared_copies():
        columns = pl.ds(pl.multiple_of((chip % shared_blocks) * half, half), half)
        return [
            pltpu.make_async_copy(source.at[:, columns], target, fetch.at[experts, k])
            for k, (source, target) in enumerate(
                (
                    (sw_gate, s_in.at[:, :half]),
                    (sw_up, s_in.at[:, half:]),
                    (sw_down, s_down),
                )
            )
        ]

    @pl.when((plane == 0) & (step == 0))
    def _():
        greet(
            [chips.to_x, chips.to_y, chips.to_core, chips.to_z(1), chips.to_z(PLANES - 1)]
        )
        for copy in near_sides() + near_cores_at_once():
            copy.start()
        z_copy(1).start()

        @pl.when(shared_here)
        def _():
            for copy in shared_copies():
                copy.start()

        for expert in range(experts):
            for copy in weight_copies(expert):
                copy.start()
        for copy in near_sides():
            copy.wait_recv()
        for copy in near_corners() + [near_core(1), near_core(2)]:
            copy.start()
        z_copy(1).wait_recv()
        z_copy(2).start()
        start_plane(1)

        @pl.when(shared_here)
        def _():
            for copy in shared_copies():
                copy.wait()

        @pl.when(~shared_here)
        def _():
            s_in[...] = jnp.zeros(s_in.shape, low)
            s_down[...] = jnp.zeros(s_down.shape, low)

        for copy in near_corners():
            copy.wait_recv()
        near_core(3).start()
        for copy in near_cores_at_once() + [near_core(place) for place in (1, 2, 3)]:
            copy.wait_recv()

    def pair_place(pair):
        return pair // (pairs // 2), slice((pair % (pairs // 2)) * 2, (pair % (pairs // 2)) * 2 + 2)

    def coming(pair):
        side, blocks = pair_place(pair)
        return [
            pltpu.make_async_copy(
                land.at[plane, side, blocks, which],
                here.at[2 * pair : 2 * pair + 2],
                come.at[which * pairs + pair],
            )
            for which, here in enumerate((x_here, g_here))
        ]

    def going(pair):
        side, blocks = pair_place(pair)
        return [
            pltpu.make_async_copy(
                here.at[2 * pair : 2 * pair + 2, :, :columns],
                targets[side].at[plane, blocks],
                go.at[which * pairs + pair],
            )
            for which, (targets, here, columns) in enumerate(
                (
                    ((out_mine, out_other), x_here, width),
                    ((grad_mine, grad_other), g_here, width + EXTRA),
                )
            )
        ]

    def pair_rows(here, pair, columns):
        return here[2 * pair : 2 * pair + 2, :, :columns].reshape(pair_rows_all, columns)

    def own_coming():
        rows = [own_rows_in.at[0]] + [land.at[0, 0, place, 0] for place in (1, 2, 3)]
        grads = [own_rows_in.at[1], *near]
        for which, (here, sources) in enumerate(((x_here, rows), (g_here, grads))):
            for block, source in enumerate(sources):
                yield pltpu.make_async_copy(
                    source, here.at[block], come.at[which * pairs + block // 2]
                )

    @pl.when((step == 0) & (plane == 0))
    def _():
        for copy in own_coming():
            copy.start()

    @pl.when((step == 0) & (plane > 0))
    def _():
        for pair in range(pairs // 2):
            for copy in coming(pair):
                copy.start()

    @pl.when(step == 0)
    def _():
        for pair in range(pairs // 2, pairs):
            for copy in coming(pair):
                copy.start()
        tokens = lax.broadcasted_iota(jnp.int32, (pair_rows_all, pair_rows_all), 0)
        others = lax.broadcasted_iota(jnp.int32, (pair_rows_all, pair_rows_all), 1)
        own_rows = pair_rows_all // 2
        earlier = (others < tokens) & ((others >= own_rows) == (tokens >= own_rows))
        earlier = earlier.astype(jnp.float32).astype(low)
        lane = lax.broadcasted_iota(jnp.int32, (pair_rows_all, pair_slots), 1)
        block = lax.broadcasted_iota(jnp.int32, (pair_rows_all, pair_slots), 0) // own_rows
        capacity = own // 2
        at_block = lax.rem(lane // capacity, 2) == block
        at_slot = lax.rem(lane, capacity).astype(jnp.float32)
        for pair in range(pairs):
            for copy in coming(pair):
                copy.wait()
            grads = pair_rows(g_here, pair, width + EXTRA)
            routes = grads[:, width:].astype(jnp.float32)
            named = routes[:, :1] == lanes[:1]
            for k in range(1, TOPK):
                named = named | (routes[:, k : k + 1] == lanes[:1])
            named = named.astype(jnp.float32)
            rank = dot(earlier, named.astype(low))
            seat = jnp.where(at_block & (rank == at_slot), named, 0.0).astype(low)
            seats[pair] = seat
            rows = dot_tn(seat, pair_rows(x_here, pair, width + EXTRA))
            grads = dot_tn(seat, grads[:, :width])
            for expert in range(experts):
                here = slice(expert * own, (expert + 1) * own)
                there = slice(pair * own, (pair + 1) * own)
                low_rows = rows[here, :width].astype(jnp.bfloat16)
                low_grads = grads[here].astype(jnp.bfloat16)
                if expert == 0:
                    rows_out[0, there] = low_rows
                    pairs_out[0, there] = low_grads
                else:
                    rows_kept[expert - 1, there] = low_rows
                    grads_kept[expert - 1, there] = low_grads
                gate = jnp.sum(
                    rows[here, width:] * lanes[1 + expert : 2 + expert], axis=-1, keepdims=True
                )
                extra_kept[expert, there] = jnp.broadcast_to(gate, (own, EXTRA))
        for side in range(2):
            blocks = slice(side * pairs, (side + 1) * pairs)
            tokens = pairs * own_rows
            rows = x_here[blocks, :, :width].reshape(tokens, width)
            grads = g_here[blocks, :, :width].reshape(tokens, width)
            acts = dot(rows, s_in[...])
            hidden, grad_gate, grad_up = gated(
                acts[:, :half], acts[:, half:], dot(grads, s_down[...])
            )
            s_hidden[side * tokens : (side + 1) * tokens] = hidden
            both = jnp.concatenate([grad_gate, grad_up], axis=1)
            s_grads[side * tokens : (side + 1) * tokens] = both
            term_in, term_down = dot_tn(both, rows), dot_tn(hidden, grads)
            if side == 0:
                fresh = plane == 0
                sum_in[...] = jnp.where(fresh, 0.0, sum_in[...]) + term_in
                sum_down[...] = jnp.where(fresh, 0.0, sum_down[...]) + term_down
            else:
                sum_in[...] += term_in
                sum_down[...] += term_down

    @pl.when(step > 0)
    def _():
        rows_out[0] = rows_kept[step - 1]
        pairs_out[0] = grads_kept[step - 1]

    @pl.when(plane == 0)
    def _():
        for copy in weight_copies(step):
            copy.wait()

    rows = rows_out[0]
    grads = pairs_out[0].astype(jnp.float32)
    gates = extra_kept[step][:, :1]
    pair_grads = (grads * gates).astype(jnp.bfloat16)
    hidden, grad_gate, grad_up = gated(
        dot_nt(rows, gate_here[step]), dot_nt(rows, up_here[step]), dot_nt(pair_grads, down_here[step])
    )
    hidden_out[0] = hidden
    gate_out[0] = grad_gate
    up_out[0] = grad_up
    part = dot(hidden, down_here[step])
    out_kept[step] = (part * gates).astype(jnp.bfloat16)
    slot_grad = jnp.sum(part * grads, axis=-1, keepdims=True)
    pairs_out[0] = pair_grads
    high = slot_grad.astype(jnp.bfloat16).astype(jnp.float32)
    lane_row = 1 + experts + step * 2
    extra_kept[step] = high * lanes[pl.ds(lane_row, 1)] + (slot_grad - high) * lanes[
        pl.ds(lane_row + 1, 1)
    ]
    back_kept[step] = (dot(grad_gate, gate_here[step]) + dot(grad_up, up_here[step])).astype(
        jnp.bfloat16
    )

    @pl.when((step == 0) & (plane + 1 < PLANES))
    def _():
        pass_corners(plane + 1)

    @pl.when((step == 0) & (plane + 2 < PLANES))
    def _():
        for k in range(2, PLANES):

            @pl.when(plane == k - 2)
            def _(k=k):
                z_copy(k).wait_recv()
                if k + 1 < PLANES:
                    z_copy(k + 1).start()

        start_plane(plane + 2)

    @pl.when(step == experts - 1)
    def _():
        for pair in range(pairs):
            there = slice(pair * own, (pair + 1) * own)
            tokens = slice(pair * pair_rows_all, (pair + 1) * pair_rows_all)
            here = slice(2 * pair, 2 * pair + 2)
            back = seats[pair]
            total = dot(
                back, jnp.concatenate([out_kept[e, there] for e in range(experts)], 0)
            ) + dot_nt(s_hidden[tokens], s_down[...])
            x_here[here, :, :width] = total.astype(jnp.bfloat16).reshape(2, -1, width)
            total = dot(
                back, jnp.concatenate([back_kept[e, there] for e in range(experts)], 0)
            ) + dot_nt(s_grads[tokens], s_in[...])
            g_here[here, :, :width] = total.astype(jnp.bfloat16).reshape(
                2, -1, width
            )
            extra = jnp.concatenate([extra_kept[e, there] for e in range(experts)], 0)
            total = dot(back, extra.astype(jnp.bfloat16))
            g_here[here, :, width:] = total.astype(jnp.bfloat16).reshape(2, -1, EXTRA)
            for copy in going(pair):
                copy.start()
        for pair in range(pairs):
            for copy in going(pair):
                copy.wait()

    @pl.when((step == experts - 1) & (plane + 1 < PLANES))
    def _():
        finish_plane(plane + 1)

    @pl.when((step == experts - 1) & (plane == PLANES - 1))
    def _():
        block_rows = width // shared_out.shape[0]
        for to in range(shared_out.shape[0]):
            there = slice(to * block_rows, (to + 1) * block_rows)
            shared_out[to, : 2 * half] = sum_in[:, there].astype(low)
            shared_out[to, 2 * half :] = sum_down[:, there].astype(low)
        for k in range(1, PLANES):
            z_copy(k).wait_send()

        near_cores = near_cores_at_once() + [near_core(place) for place in (1, 2, 3)]
        for copy in near_sides() + near_corners() + near_cores:
            copy.wait_send()

        @pl.loop(1, PLANES)
        def _(sent):
            for copy in side_copies(sent) + corner_copies(sent):
                copy.wait_send()
            for k in range(5):
                core_copy(sent, k).wait_send()


def moe_layer(own_rows_in, near, lanes, weights):
    experts, units, width = weights[0].shape
    _, own_rows, wide = own_rows_in.shape
    blocks, pairs, pair_rows, pair_slots = 4, 4, 2 * own_rows, EXTRA
    slots = pairs * pair_slots // experts
    tokens = pairs * pair_rows
    half = EXTRA
    chips = lax.axis_size(EXPERT)
    low = jnp.bfloat16

    def whole(array):
        zeros = (0,) * len(array.shape)
        return pl.BlockSpec(array.shape, lambda s, j: zeros, pipeline_mode=pl.Buffered(1))

    anywhere = pl.BlockSpec(memory_space=pl.ANY)
    land = [jax.ShapeDtypeStruct((PLANES, 2, blocks, 2, own_rows, wide), low)]
    plain = [jax.ShapeDtypeStruct((PLANES, blocks, own_rows, width), low)] * 2
    extended = [jax.ShapeDtypeStruct((PLANES, blocks, own_rows, wide), low)] * 2
    keep = [
        jax.ShapeDtypeStruct((experts, PLANES * slots, columns), low)
        for columns in (width, width, units, units, units)
    ]
    shared = [jax.ShapeDtypeStruct((chips, 3 * half, width // chips), low)]
    operands = [own_rows_in, lanes] + list(weights) + near
    work = 2 * tokens * width * (8 * half + 2 * pair_slots) + 12 * experts * slots * width * units
    results = pl.pallas_call(
        moe_kernel,
        grid=(PLANES, experts),
        in_specs=[anywhere, whole(lanes)] + [anywhere] * (len(weights) + len(near)),
        out_specs=[anywhere] * 5
        + [pl.BlockSpec((1, slots, v.shape[2]), lambda s, j: (j, s, 0)) for v in keep]
        + [whole(v) for v in shared],
        out_shape=land + plain + extended + keep + shared,
        scratch_shapes=[
            pltpu.VMEM((experts - 1, slots, width), low),
            pltpu.VMEM((experts - 1, slots, width), low),
            pltpu.VMEM((experts, slots, width), low),
            pltpu.VMEM((experts, slots, width), low),
            pltpu.VMEM((experts, slots, EXTRA), jnp.float32),
            pltpu.VMEM((tokens, half), low),
            pltpu.VMEM((tokens, 2 * half), low),
            pltpu.VMEM((pairs, pair_rows, pair_slots), low),
            pltpu.VMEM((2 * blocks, own_rows, wide), low),
            pltpu.VMEM((2 * blocks, own_rows, wide), low),
            pltpu.VMEM(weights[0].shape, low),
            pltpu.VMEM(weights[1].shape, low),
            pltpu.VMEM(weights[2].shape, low),
            pltpu.VMEM((width, 2 * half), low),
            pltpu.VMEM((width, half), low),
            pltpu.VMEM((2 * half, width), jnp.float32),
            pltpu.VMEM((half, width), jnp.float32),
            pltpu.SemaphoreType.DMA((2 * pairs,)),
            pltpu.SemaphoreType.DMA((2 * pairs,)),
            pltpu.SemaphoreType.DMA((experts + 1, 3)),
            pltpu.SemaphoreType.DMA((PLANES, 11)),
            pltpu.SemaphoreType.DMA((PLANES, 11)),
            pltpu.SemaphoreType.DMA((PLANES,)),
            pltpu.SemaphoreType.DMA((PLANES,)),
        ],
        compiler_params=pltpu.CompilerParams(
            collective_id=0, has_side_effects=True, vmem_limit_bytes=VMEM_LIMIT
        ),
        cost_estimate=pl.CostEstimate(
            flops=PLANES * work, bytes_accessed=120 << 20, transcendentals=0
        ),
    )(*operands)
    return results[1:3], results[3:5], results[5:]


def expert_grads_kernel(rows, pair_grads, grad_gate, grad_up, hidden, for_gate, for_up, for_down):
    for_gate[0] = dot_tn(grad_gate[0], rows[0])
    for_up[0] = dot_tn(grad_up[0], rows[0])
    for_down[0] = dot_tn(hidden[0], pair_grads[0])


def expert_grads(rows, pair_grads, grad_gate, grad_up, hidden):
    experts, slots, width = rows.shape
    units = hidden.shape[2]
    columns = width // 2
    of_columns = pl.BlockSpec((1, slots, columns), lambda j, c: (j, 0, c))
    of_units = pl.BlockSpec((1, slots, units), lambda j, c: (j, 0, 0))
    grads = pl.pallas_call(
        expert_grads_kernel,
        grid=(experts, width // columns),
        in_specs=[of_columns] * 2 + [of_units] * 3,
        out_specs=[pl.BlockSpec((1, units, columns), lambda j, c: (j, 0, c))] * 3,
        out_shape=[jax.ShapeDtypeStruct((experts, units, width), jnp.float32)] * 3,
        compiler_params=pltpu.CompilerParams(vmem_limit_bytes=VMEM_LIMIT),
        cost_estimate=pl.CostEstimate(
            flops=6 * experts * slots * width * units,
            bytes_accessed=60 << 20,
            transcendentals=0,
        ),
    )(rows, pair_grads, grad_gate, grad_up, hidden)
    return [jnp.swapaxes(grad, 1, 2) for grad in grads]


def per_device_gathered(
    inputs,
    norm_attn,
    w_query,
    w_latent,
    norm_latent,
    w_expand,
    w_output,
    norm_moe,
    w_router,
    w_shared_gate,
    w_shared_up,
    w_shared_down,
    w_expert_gate,
    w_expert_up,
    w_expert_down,
    routes,
    cotangent,
):
    own_rows = inputs.shape[0]
    width = inputs.shape[1]
    tensor_size = lax.axis_size(TENSOR)
    expert_size = lax.axis_size(EXPERT)
    tensor_index = lax.axis_index(TENSOR)
    expert_index = lax.axis_index(EXPERT)
    seq_rows = own_rows * tensor_size
    local_heads = w_query.shape[1] // (NOPE + ROPE)
    experts = w_router.shape[1]
    local_experts = experts // expert_size
    capacity = own_rows * TOPK * 4 // (3 * experts)
    scale = 1.0 / math.sqrt(NOPE + ROPE)

    beside = jnp.pad(routes.astype(jnp.bfloat16), ((0, 0), (0, EXTRA - TOPK)))
    block = jnp.concatenate([cotangent, beside], axis=1)
    from_x, from_y = send_x(block), send_y(block)

    flat_in = inputs.astype(jnp.float32)
    scale_one = lax.rsqrt(jnp.mean(flat_in * flat_in, axis=-1, keepdims=True) + EPS)
    normed_one = flat_in * scale_one
    h_own = (normed_one * norm_attn).astype(jnp.bfloat16)
    compressed = jnp.dot(h_own, w_latent, preferred_element_type=jnp.float32)
    lat_raw = compressed[:, :LATENT]
    scale_lat = lax.rsqrt(jnp.mean(lat_raw * lat_raw, axis=-1, keepdims=True) + EPS)
    normed_lat = lat_raw * scale_lat
    lat_own = (normed_lat * norm_latent).astype(jnp.bfloat16)
    places = jnp.arange(own_rows)
    places_all = jnp.concatenate(
        [tensor_index * own_rows + places, (1 - tensor_index) * own_rows + places]
    )
    cos_own, sin_own = rope_tables(places_all[:own_rows], ROPE)
    rope_own = rotate(compressed[:, LATENT:], cos_own, sin_own).astype(jnp.bfloat16)

    def both(values):
        return jnp.concatenate([values, send_core(values)], axis=0)

    h_all = both(h_own)
    h_all, from_x, from_y = lax.optimization_barrier((h_all, from_x, from_y))
    near = [from_x, from_y, send_y(from_x)]
    lat_rope = both(jnp.concatenate([lat_own, rope_own], axis=1))
    lat_all, rope_all = lat_rope[:, :LATENT], lat_rope[:, LATENT:]
    cos_all, sin_all = rope_tables(places_all, ROPE)
    cos_all = cos_all[:, None, :]
    sin_all = sin_all[:, None, :]
    query_raw = jnp.dot(h_all, w_query, preferred_element_type=jnp.float32).reshape(
        seq_rows, local_heads, NOPE + ROPE
    )
    query = jnp.concatenate(
        [query_raw[..., :NOPE], rotate(query_raw[..., NOPE:], cos_all, sin_all)], axis=-1
    ).astype(jnp.bfloat16)
    expanded = jnp.dot(lat_all, w_expand, preferred_element_type=jnp.float32).astype(jnp.bfloat16)
    expanded = expanded.reshape(seq_rows, local_heads, NOPE + VD)
    key_full = jnp.concatenate(
        [
            expanded[..., :NOPE],
            jnp.broadcast_to(rope_all[:, None, :], (seq_rows, local_heads, ROPE)),
        ],
        axis=-1,
    )
    value = expanded[..., NOPE:]
    allowed = (places_all[:, None] >= places_all[None, :])[None]
    scores = product("qhd,khd->hqk", query, key_full) * scale
    scores = jnp.where(allowed, scores, -1e30)
    weights = jnp.exp(scores - jnp.max(scores, axis=-1, keepdims=True))
    probs = weights / jnp.sum(weights, axis=-1, keepdims=True)
    attended = product("hqk,khd->qhd", probs.astype(jnp.bfloat16), value)
    attended_flat = attended.astype(jnp.bfloat16).reshape(seq_rows, local_heads * VD)
    attn_terms = product("sv,dv->sd", attended_flat, w_output)
    after_attn = (
        flat_in
        + attn_terms[:own_rows]
        + send_core(attn_terms[own_rows:].astype(jnp.bfloat16)).astype(jnp.float32)
    )
    scale_two = lax.rsqrt(jnp.mean(after_attn * after_attn, axis=-1, keepdims=True) + EPS)
    normed_two = after_attn * scale_two
    h_moe = (normed_two * norm_moe).astype(jnp.bfloat16)
    logits = jnp.dot(h_moe, w_router, preferred_element_type=jnp.float32)
    expert_ids = jnp.arange(experts, dtype=jnp.int32)
    chosen = jnp.any(routes[:, :, None] == expert_ids[None, None, :], axis=1)
    masked = jnp.where(chosen, logits, -1e30)
    raised = jnp.where(chosen, jnp.exp(masked - jnp.max(masked, axis=-1, keepdims=True)), 0.0)
    gates = raised / jnp.sum(raised, axis=-1, keepdims=True)
    high_gates = lax.reduce_precision(gates, 8, 7)
    beside = [high_gates.astype(jnp.bfloat16), (gates - high_gates).astype(jnp.bfloat16)]
    beside.append(jnp.zeros((own_rows, EXTRA - 2 * experts), jnp.bfloat16))
    own_rows_in = jnp.stack([jnp.concatenate([h_moe, *beside], axis=1), block])

    own_ids = expert_index * local_experts + jnp.arange(local_experts, dtype=jnp.int32)
    lane_ids = jnp.arange(EXTRA, dtype=jnp.int32)[None, :]
    slot_experts = expert_index * local_experts + lane_ids // (2 * capacity)
    gate_lanes = (lane_ids == own_ids[:, None]) | (lane_ids == own_ids[:, None] + experts)
    back_lanes = (own_ids[:, None] * tensor_size + tensor_index) * 2 + jnp.arange(2)[None, :]
    lanes = jnp.concatenate(
        [slot_experts, gate_lanes, lane_ids == back_lanes.reshape(-1, 1)], axis=0
    ).astype(jnp.float32)
    lanes = jnp.pad(lanes, ((0, -lanes.shape[0] % 8), (0, 0)))

    all_weights = tuple(jnp.swapaxes(w, 1, 2) for w in (w_expert_gate, w_expert_up, w_expert_down))
    all_weights += (w_shared_gate, w_shared_up, w_shared_down)
    out_parts, grad_parts, kept = moe_layer(own_rows_in, near, lanes, all_weights)
    shared_grads = kept[5].reshape((PLANES, 2, 2) + kept[5].shape[1:])
    moe_back, moe_out, shared_grads = sum_over_chips(
        1, [(2, grad_parts, 512), (2, out_parts, 512)], shared_grads
    )
    output = (after_attn + moe_out).astype(jnp.bfloat16)

    grad_gates = jnp.sum(moe_back[:, width:].reshape(own_rows, experts, -1), axis=-1)
    grad_gates = jnp.where(chosen, grad_gates, 0.0)
    grad_select = gates * (grad_gates - jnp.sum(gates * grad_gates, axis=-1, keepdims=True))
    grad_logits = grad_select.astype(jnp.bfloat16)
    grad_router = product("td,te->de", h_moe, grad_logits)

    grad_out = cotangent.astype(jnp.float32)
    grad_moe = moe_back[:, :width] + product("te,de->td", grad_logits, w_router)
    grad_mid, grad_norm_moe = norm_back(grad_moe, normed_two, scale_two, norm_moe)
    grad_mid = grad_mid + grad_out
    grad_attn_all = both(grad_mid.astype(jnp.bfloat16))
    grad_output = product("sd,sv->dv", grad_attn_all, attended_flat)
    grad_attended = product("sd,dv->sv", grad_attn_all, w_output)
    grad_attended = grad_attended.astype(jnp.bfloat16).reshape(seq_rows, local_heads, VD)
    grad_probs = product("qhv,khv->hqk", grad_attended, value)
    centre = jnp.sum(probs * grad_probs, axis=-1, keepdims=True)
    grad_scores = (probs * (grad_probs - centre)).astype(jnp.bfloat16)
    grad_query_full = product("hqk,khd->qhd", grad_scores, key_full) * scale
    grad_key_full = product("hqk,qhd->khd", grad_scores, query) * scale
    grad_value = product("hqk,qhv->khv", probs.astype(jnp.bfloat16), grad_attended)
    grad_query_raw = jnp.concatenate(
        [grad_query_full[..., :NOPE], unrotate(grad_query_full[..., NOPE:], cos_all, sin_all)],
        axis=-1,
    )
    grad_query_raw = grad_query_raw.astype(jnp.bfloat16).reshape(
        seq_rows, local_heads * (NOPE + ROPE)
    )
    grad_query = product("sd,sq->dq", h_all, grad_query_raw)
    grad_expanded = jnp.concatenate([grad_key_full[..., :NOPE], grad_value], axis=-1)
    grad_expanded = grad_expanded.astype(jnp.bfloat16).reshape(seq_rows, local_heads * (NOPE + VD))
    grad_expand = product("sl,sk->lk", lat_all, grad_expanded)
    grad_rope_part = jnp.sum(grad_key_full[..., NOPE:], axis=1)
    grad_h_part = product("sq,dq->sd", grad_query_raw, w_query)
    grad_lat_part = product("sk,lk->sl", grad_expanded, w_expand)
    own_side = jnp.concatenate([grad_lat_part, grad_rope_part], axis=1)
    own_side = own_side[:own_rows] + send_core(own_side[own_rows:].astype(jnp.bfloat16)).astype(
        jnp.float32
    )
    grad_h_own = grad_h_part[:own_rows] + send_core(
        grad_h_part[own_rows:].astype(jnp.bfloat16)
    ).astype(jnp.float32)
    grad_lat_raw, grad_norm_latent = norm_back(
        own_side[:, :LATENT], normed_lat, scale_lat, norm_latent
    )
    grad_compressed = jnp.concatenate(
        [grad_lat_raw, unrotate(own_side[:, LATENT:], cos_own, sin_own)], axis=-1
    ).astype(jnp.bfloat16)
    grad_latent = product("td,tc->dc", h_own, grad_compressed)
    grad_h = grad_h_own + product("tc,dc->td", grad_compressed, w_latent)
    grad_in, grad_norm_attn = norm_back(grad_h, normed_one, scale_one, norm_attn)
    grad_inputs = grad_mid + grad_in

    share = width // expert_size
    low_rows = expert_size * share
    own_part = share // tensor_size

    def in_two(values):
        high = lax.reduce_precision(values, 8, 7)
        return jnp.stack([high, values - high], axis=-1)

    gains = in_two(grad_norm_latent).reshape(expert_size * tensor_size, -1, 2)
    gain_rows = gains.shape[1]
    gains = jnp.pad(gains, ((0, 0), (0, own_part - gain_rows), (0, 0))).reshape(low_rows, 2)
    small = jnp.concatenate(
        [grad_router, in_two(grad_norm_attn), in_two(grad_norm_moe), gains], axis=1
    )
    small = jnp.pad(small, ((0, 0), (0, EXTRA - small.shape[1])))
    small, grad_latent = [
        v.astype(jnp.bfloat16).reshape(expert_size, tensor_size, own_part, -1)
        for v in (small, grad_latent)
    ]
    grad_output = grad_output.astype(jnp.bfloat16).reshape(expert_size, share, -1)
    grad_query = grad_query.astype(jnp.bfloat16).reshape(expert_size, share, -1)
    grad_expand = grad_expand.astype(jnp.bfloat16).reshape(expert_size, -1, w_expand.shape[1])
    grad_output, grad_query, grad_expand, grad_latent, small = sum_over_chips(
        2,
        [
            (0, [grad_output], 256),
            (0, [grad_query], 384),
            (0, [grad_expand], 512),
            (1, [grad_latent], 0),
            (1, [small], 0),
        ],
    )
    grad_router = small[:, :experts]
    grad_norm_attn = small[:, experts] + small[:, experts + 1]
    grad_norm_moe = small[:, experts + 2] + small[:, experts + 3]
    grad_norm_latent = (small[:, experts + 4] + small[:, experts + 5])[:gain_rows]

    rows, pair_grads, hidden, grad_gate, grad_up = kept[:5]
    grad_expert_gate, grad_expert_up, grad_expert_down = expert_grads(
        rows, pair_grads, grad_gate, grad_up, hidden
    )
    columns = w_shared_gate.shape[1]
    shared_grads = shared_grads[: columns // EXTRA].reshape(-1, 3, EXTRA, share)
    shared_grads = (
        jnp.transpose(shared_grads, (1, 3, 0, 2)).reshape(3, share, columns).astype(jnp.float32)
    )
    return (
        output,
        grad_inputs,
        grad_norm_attn,
        grad_query,
        grad_latent,
        grad_norm_latent,
        grad_expand,
        grad_output,
        grad_norm_moe,
        grad_router,
        shared_grads[0],
        shared_grads[1],
        shared_grads[2],
        grad_expert_gate,
        grad_expert_up,
        grad_expert_down,
    )


def per_device_for(mesh):
    if mesh.shape[EXPERT] == PLANES * 4 and mesh.shape[TENSOR] == 2:
        return per_device_gathered
    return per_device_exchanged


def solution(mesh):
    return jax.shard_map(
        per_device_for(mesh),
        mesh=mesh,
        in_specs=(
            P((EXPERT, TENSOR), None),
            P(),
            P(None, TENSOR),
            P(),
            P(),
            P(None, TENSOR),
            P(None, TENSOR),
            P(),
            P(),
            P(None, TENSOR),
            P(None, TENSOR),
            P(None, TENSOR),
            P(EXPERT, None, TENSOR),
            P(EXPERT, None, TENSOR),
            P(EXPERT, None, TENSOR),
            P((EXPERT, TENSOR), None),
            P((EXPERT, TENSOR), None),
        ),
        out_specs=(
            P((EXPERT, TENSOR), None),
            P((EXPERT, TENSOR), None),
            P((EXPERT, TENSOR)),
            P(EXPERT, TENSOR),
            P((EXPERT, TENSOR), None),
            P((EXPERT, TENSOR)),
            P(EXPERT, TENSOR),
            P(EXPERT, TENSOR),
            P((EXPERT, TENSOR)),
            P((EXPERT, TENSOR), None),
            P(EXPERT, TENSOR),
            P(EXPERT, TENSOR),
            P(EXPERT, TENSOR),
            P(EXPERT, None, TENSOR),
            P(EXPERT, None, TENSOR),
            P(EXPERT, None, TENSOR),
        ),
        check_vma=False,
    )
```

```python
import functools
import math

import jax
import jax.numpy as jnp
from jax import lax
from jax.experimental import pallas as pl
from jax.experimental.pallas import tpu as pltpu
from jax.sharding import PartitionSpec as P

EXPERT = "expert"
TENSOR = "tensor"
NOPE = 128
ROPE = 64
VD = 128
LATENT = 512
TOPK = 6


EPS = 1e-06


def rope_tables(positions, width):
    half = width // 2
    freq = 10000.0 ** (-(jnp.arange(half, dtype=jnp.float32) * 2.0) / width)
    angle = positions.astype(jnp.float32)[:, None] * freq[None, :]
    return (jnp.cos(angle), jnp.sin(angle))


def rotate(values, cosine, sine):
    half = values.shape[-1] // 2
    first = values[..., :half]
    second = values[..., half:]
    return jnp.concatenate(
        [first * cosine - second * sine, first * sine + second * cosine], axis=-1
    )


def unrotate(grads, cosine, sine):
    half = grads.shape[-1] // 2
    first = grads[..., :half]
    second = grads[..., half:]
    return jnp.concatenate(
        [first * cosine + second * sine, second * cosine - first * sine], axis=-1
    )


def norm_back(grad_out, normed, scale, gain):
    scaled = grad_out * gain
    grad_in = scale * (scaled - normed * jnp.mean(scaled * normed, axis=-1, keepdims=True))
    return (grad_in, jnp.sum(grad_out * normed, axis=0))


def masked_scores(rows_query, key_full, first_row, scale):
    block = rows_query.shape[0]
    scores = (
        jnp.einsum("qhd,khd->hqk", rows_query, key_full, preferred_element_type=jnp.float32) * scale
    )
    allowed = (first_row + jnp.arange(block))[:, None] >= jnp.arange(key_full.shape[0])[None, :]
    return jnp.where(allowed[None], scores, -1e30)


def attention_forward(query, key_full, value, scale):
    seq_rows = query.shape[0]
    block = min(seq_rows, 512)

    def one_block(index):
        first_row = index * block
        scores = masked_scores(query, key_full, first_row, scale)
        peak = jnp.max(scores, axis=-1, keepdims=True)
        weights = jnp.exp(scores - peak)
        total = jnp.sum(weights, axis=-1, keepdims=True)
        probs = (weights / total).astype(jnp.bfloat16)
        result = jnp.einsum("hqk,khd->qhd", probs, value, preferred_element_type=jnp.float32)
        return (result.astype(jnp.bfloat16), (peak + jnp.log(total))[..., 0])

    results, log_totals = lax.map(one_block, jnp.arange(seq_rows // block))
    return (results.reshape(seq_rows, query.shape[1], value.shape[2]), log_totals)


def attention_backward(query, key_full, value, grad_attended, log_totals, scale):
    seq_rows = query.shape[0]
    block = min(seq_rows, 512)

    def one_block(carry, index):
        grad_key, grad_value = carry
        first_row = index * block
        scores = masked_scores(query, key_full, first_row, scale)
        probs = jnp.exp(scores - log_totals[index][..., None])
        grad_probs = jnp.einsum(
            "qhv,khv->hqk", grad_attended, value, preferred_element_type=jnp.float32
        )
        centre = jnp.sum(probs * grad_probs, axis=-1, keepdims=True)
        grad_scores = (probs * (grad_probs - centre)).astype(jnp.bfloat16)
        grad_rows = (
            jnp.einsum("hqk,khd->qhd", grad_scores, key_full, preferred_element_type=jnp.float32)
            * scale
        )
        grad_key = (
            grad_key
            + jnp.einsum("hqk,qhd->khd", grad_scores, query, preferred_element_type=jnp.float32)
            * scale
        )
        grad_value = grad_value + jnp.einsum(
            "hqk,qhv->khv",
            probs.astype(jnp.bfloat16),
            grad_attended,
            preferred_element_type=jnp.float32,
        )
        return ((grad_key, grad_value), grad_rows)

    start_key = jnp.zeros(key_full.shape, jnp.float32)
    start_value = jnp.zeros(value.shape, jnp.float32)
    (grad_key, grad_value), grad_query = lax.scan(
        one_block, (start_key, start_value), jnp.arange(seq_rows // block)
    )
    return (grad_query.reshape(query.shape), grad_key, grad_value)


def to_experts(grid, rows):
    gathered, rows_all = (
        lax.all_gather(grid, TENSOR, axis=0, tiled=True),
        lax.all_gather(rows, TENSOR, axis=0, tiled=True),
    )
    received = lax.all_to_all(gathered, EXPERT, split_axis=1, concat_axis=1, tiled=True)
    return (received, rows_all)


def from_experts(expert_part, shared_part):
    returned = lax.all_to_all(expert_part, EXPERT, split_axis=1, concat_axis=1, tiled=True)
    summed, shared_sum = (
        lax.psum_scatter(returned, TENSOR, scatter_dimension=0, tiled=True).astype(jnp.float32),
        lax.psum_scatter(shared_part, TENSOR, scatter_dimension=0, tiled=True).astype(
            jnp.float32
        ),
    )
    return (summed, shared_sum)


def per_device_exchanged(
    inputs,
    norm_attn,
    w_query,
    w_latent,
    norm_latent,
    w_expand,
    w_output,
    norm_moe,
    w_router,
    w_shared_gate,
    w_shared_up,
    w_shared_down,
    w_expert_gate,
    w_expert_up,
    w_expert_down,
    routes,
    cotangent,
):
    own_rows = inputs.shape[0]
    width = inputs.shape[1]
    tensor_size = lax.axis_size(TENSOR)
    expert_size = lax.axis_size(EXPERT)
    tensor_index = lax.axis_index(TENSOR)
    seq_rows = own_rows * tensor_size
    local_heads = w_query.shape[1] // (NOPE + ROPE)
    experts = w_router.shape[1]
    local_experts = experts // expert_size
    capacity = own_rows * TOPK * 4 // (3 * experts)
    scale = 1.0 / math.sqrt(NOPE + ROPE)
    flat_in = inputs.astype(jnp.float32)
    scale_one = lax.rsqrt(jnp.mean(flat_in * flat_in, axis=-1, keepdims=True) + EPS)
    normed_one = flat_in * scale_one
    h_own = (normed_one * norm_attn).astype(jnp.bfloat16)
    compressed = jnp.dot(h_own, w_latent, preferred_element_type=jnp.float32)
    lat_raw = compressed[:, :LATENT]
    scale_lat = lax.rsqrt(jnp.mean(lat_raw * lat_raw, axis=-1, keepdims=True) + EPS)
    normed_lat = lat_raw * scale_lat
    lat_own = (normed_lat * norm_latent).astype(jnp.bfloat16)
    cos_own, sin_own = rope_tables(tensor_index * own_rows + jnp.arange(own_rows), ROPE)
    rope_own = rotate(compressed[:, LATENT:], cos_own, sin_own).astype(jnp.bfloat16)
    h_all, lat_all, rope_all = (
        lax.all_gather(h_own, TENSOR, axis=0, tiled=True),
        lax.all_gather(lat_own, TENSOR, axis=0, tiled=True),
        lax.all_gather(rope_own, TENSOR, axis=0, tiled=True),
    )
    cos_all, sin_all = rope_tables(jnp.arange(seq_rows), ROPE)
    cos_all = cos_all[:, None, :]
    sin_all = sin_all[:, None, :]
    query_raw = jnp.dot(h_all, w_query, preferred_element_type=jnp.float32).reshape(
        seq_rows, local_heads, NOPE + ROPE
    )
    query = jnp.concatenate(
        [query_raw[..., :NOPE], rotate(query_raw[..., NOPE:], cos_all, sin_all)], axis=-1
    ).astype(jnp.bfloat16)
    expanded = jnp.dot(lat_all, w_expand, preferred_element_type=jnp.float32).astype(jnp.bfloat16)
    expanded = expanded.reshape(seq_rows, local_heads, NOPE + VD)
    key_full = jnp.concatenate(
        [
            expanded[..., :NOPE],
            jnp.broadcast_to(rope_all[:, None, :], (seq_rows, local_heads, ROPE)),
        ],
        axis=-1,
    )
    value = expanded[..., NOPE:]
    attended, log_totals = attention_forward(query, key_full, value, scale)
    attended_flat = attended.reshape(seq_rows, local_heads * VD)
    attn_terms = jnp.einsum(
        "sv,dv->sd", attended_flat, w_output, preferred_element_type=jnp.float32
    )
    after_attn = flat_in + lax.psum_scatter(
        attn_terms.astype(jnp.bfloat16), TENSOR, scatter_dimension=0, tiled=True
    ).astype(jnp.float32)
    scale_two = lax.rsqrt(jnp.mean(after_attn * after_attn, axis=-1, keepdims=True) + EPS)
    normed_two = after_attn * scale_two
    h_moe = (normed_two * norm_moe).astype(jnp.bfloat16)
    logits = jnp.dot(h_moe, w_router, preferred_element_type=jnp.float32)
    expert_ids = jnp.arange(experts, dtype=jnp.int32)
    route_hot = (routes[:, :, None] == expert_ids[None, None, :]).astype(jnp.float32)
    gates = jax.nn.softmax(jnp.sum(route_hot * logits[:, None, :], axis=-1), axis=-1)
    flat_routes = routes.reshape(-1)
    pair_hot = (flat_routes[:, None] == expert_ids[None, :]).astype(jnp.int32)
    earlier = jnp.cumsum(pair_hot, axis=0, dtype=jnp.int32) - pair_hot
    slots = jnp.sum(earlier * pair_hot, axis=1, dtype=jnp.int32) * experts + flat_routes
    grid_shape = (capacity, expert_size, local_experts, width)

    def to_slots(pair_rows):
        placed = jnp.zeros((capacity * experts, width), jnp.bfloat16).at[slots].set(pair_rows)
        return placed.reshape(grid_shape)

    def from_slots(grid):
        return grid.reshape(capacity * experts, width)[slots].reshape(own_rows, TOPK, width)

    received, h_moe_all = to_experts(to_slots(jnp.repeat(h_moe, TOPK, axis=0)), h_moe)
    gate_act = jnp.einsum(
        "cnjd,jdf->cnjf", received, w_expert_gate, preferred_element_type=jnp.float32
    )
    up_act = jnp.einsum("cnjd,jdf->cnjf", received, w_expert_up, preferred_element_type=jnp.float32)
    hidden = (jax.nn.silu(gate_act) * up_act).astype(jnp.bfloat16)
    expert_part = jnp.einsum(
        "cnjf,jdf->cnjd", hidden, w_expert_down, preferred_element_type=jnp.float32
    ).astype(jnp.bfloat16)
    shared_gate_act = jnp.dot(h_moe_all, w_shared_gate, preferred_element_type=jnp.float32)
    shared_up_act = jnp.dot(h_moe_all, w_shared_up, preferred_element_type=jnp.float32)
    shared_hidden = (jax.nn.silu(shared_gate_act) * shared_up_act).astype(jnp.bfloat16)
    shared_part = jnp.einsum(
        "sf,df->sd", shared_hidden, w_shared_down, preferred_element_type=jnp.float32
    ).astype(jnp.bfloat16)
    expert_out, shared_out = from_experts(expert_part, shared_part)
    picked = from_slots(expert_out)
    output = (after_attn + jnp.sum(gates[:, :, None] * picked, axis=1) + shared_out).astype(
        jnp.bfloat16
    )
    grad_out = cotangent.astype(jnp.float32)
    grad_gates = jnp.sum(picked * grad_out[:, None, :], axis=-1)
    grad_select = gates * (grad_gates - jnp.sum(gates * grad_gates, axis=-1, keepdims=True))
    grad_logits = jnp.sum(grad_select[:, :, None] * route_hot, axis=1).astype(jnp.bfloat16)
    grad_router = jnp.einsum("td,te->de", h_moe, grad_logits, preferred_element_type=jnp.float32)
    pair_grads = (
        (gates[:, :, None] * grad_out[:, None, :])
        .astype(jnp.bfloat16)
        .reshape(own_rows * TOPK, width)
    )
    grad_received, cot_all = to_experts(to_slots(pair_grads), cotangent)
    grad_hidden = jnp.einsum(
        "cnjd,jdf->cnjf", grad_received, w_expert_down, preferred_element_type=jnp.float32
    )
    sigma = jax.nn.sigmoid(gate_act)
    grad_up = (grad_hidden * gate_act * sigma).astype(jnp.bfloat16)
    grad_gate = (grad_hidden * up_act * sigma * (1.0 + gate_act * (1.0 - sigma))).astype(
        jnp.bfloat16
    )
    grad_expert_down = jnp.einsum(
        "cnjd,cnjf->jdf", grad_received, hidden, preferred_element_type=jnp.float32
    )
    grad_expert_gate = jnp.einsum(
        "cnjd,cnjf->jdf", received, grad_gate, preferred_element_type=jnp.float32
    )
    grad_expert_up = jnp.einsum(
        "cnjd,cnjf->jdf", received, grad_up, preferred_element_type=jnp.float32
    )
    grad_rows_part = (
        jnp.einsum("cnjf,jdf->cnjd", grad_gate, w_expert_gate, preferred_element_type=jnp.float32)
        + jnp.einsum("cnjf,jdf->cnjd", grad_up, w_expert_up, preferred_element_type=jnp.float32)
    ).astype(jnp.bfloat16)
    shared_grad_hidden = jnp.einsum(
        "sd,df->sf", cot_all, w_shared_down, preferred_element_type=jnp.float32
    )
    shared_sigma = jax.nn.sigmoid(shared_gate_act)
    shared_grad_up = (shared_grad_hidden * shared_gate_act * shared_sigma).astype(jnp.bfloat16)
    shared_grad_gate = (
        shared_grad_hidden
        * shared_up_act
        * shared_sigma
        * (1.0 + shared_gate_act * (1.0 - shared_sigma))
    ).astype(jnp.bfloat16)
    grad_shared_down = jnp.einsum(
        "sd,sf->df", cot_all, shared_hidden, preferred_element_type=jnp.float32
    )
    grad_shared_gate = jnp.einsum(
        "sd,sf->df", h_moe_all, shared_grad_gate, preferred_element_type=jnp.float32
    )
    grad_shared_up = jnp.einsum(
        "sd,sf->df", h_moe_all, shared_grad_up, preferred_element_type=jnp.float32
    )
    shared_rows_part = (
        jnp.einsum("sf,df->sd", shared_grad_gate, w_shared_gate, preferred_element_type=jnp.float32)
        + jnp.einsum("sf,df->sd", shared_grad_up, w_shared_up, preferred_element_type=jnp.float32)
    ).astype(jnp.bfloat16)
    grad_rows, grad_shared_rows = from_experts(grad_rows_part, shared_rows_part)
    grad_moe = (
        jnp.sum(from_slots(grad_rows), axis=1)
        + grad_shared_rows
        + jnp.einsum("te,de->td", grad_logits, w_router, preferred_element_type=jnp.float32)
    )
    grad_mid, grad_norm_moe = norm_back(grad_moe, normed_two, scale_two, norm_moe)
    grad_mid = grad_mid + grad_out
    grad_attn = grad_mid.astype(jnp.bfloat16)
    grad_attn_all = lax.all_gather(grad_attn, TENSOR, axis=0, tiled=True)
    grad_output = jnp.einsum(
        "sd,sv->dv", grad_attn_all, attended_flat, preferred_element_type=jnp.float32
    )
    grad_attended = jnp.einsum(
        "sd,dv->sv", grad_attn_all, w_output, preferred_element_type=jnp.float32
    )
    grad_attended = grad_attended.astype(jnp.bfloat16).reshape(seq_rows, local_heads, VD)
    grad_query_full, grad_key_full, grad_value = attention_backward(
        query, key_full, value, grad_attended, log_totals, scale
    )
    grad_query_raw = jnp.concatenate(
        [grad_query_full[..., :NOPE], unrotate(grad_query_full[..., NOPE:], cos_all, sin_all)],
        axis=-1,
    )
    grad_query_raw = grad_query_raw.astype(jnp.bfloat16).reshape(
        seq_rows, local_heads * (NOPE + ROPE)
    )
    grad_query = jnp.einsum("sd,sq->dq", h_all, grad_query_raw, preferred_element_type=jnp.float32)
    grad_expanded = jnp.concatenate([grad_key_full[..., :NOPE], grad_value], axis=-1)
    grad_expanded = grad_expanded.astype(jnp.bfloat16).reshape(seq_rows, local_heads * (NOPE + VD))
    grad_expand = jnp.einsum(
        "sl,sk->lk", lat_all, grad_expanded, preferred_element_type=jnp.float32
    )
    grad_rope_part = jnp.sum(grad_key_full[..., NOPE:], axis=1)
    grad_h_part = jnp.einsum(
        "sq,dq->sd", grad_query_raw, w_query, preferred_element_type=jnp.float32
    )
    grad_lat_part = jnp.einsum(
        "sk,lk->sl", grad_expanded, w_expand, preferred_element_type=jnp.float32
    )
    grad_h_own, grad_lat_own, grad_rope_own = (
        lax.psum_scatter(
            grad_h_part.astype(jnp.bfloat16), TENSOR, scatter_dimension=0, tiled=True
        ).astype(jnp.float32),
        lax.psum_scatter(
            grad_lat_part.astype(jnp.bfloat16), TENSOR, scatter_dimension=0, tiled=True
        ).astype(jnp.float32),
        lax.psum_scatter(
            grad_rope_part.astype(jnp.bfloat16), TENSOR, scatter_dimension=0, tiled=True
        ).astype(jnp.float32),
    )
    grad_lat_raw, grad_norm_latent = norm_back(grad_lat_own, normed_lat, scale_lat, norm_latent)
    grad_compressed = jnp.concatenate(
        [grad_lat_raw, unrotate(grad_rope_own, cos_own, sin_own)], axis=-1
    ).astype(jnp.bfloat16)
    grad_latent = jnp.einsum(
        "td,tc->dc", h_own, grad_compressed, preferred_element_type=jnp.float32
    )
    grad_h = grad_h_own + jnp.einsum(
        "tc,dc->td", grad_compressed, w_latent, preferred_element_type=jnp.float32
    )
    grad_in, grad_norm_attn = norm_back(grad_h, normed_one, scale_one, norm_attn)
    grad_inputs = grad_mid + grad_in
    grad_query, grad_expand, grad_output, grad_shared_gate, grad_shared_up, grad_shared_down = (
        lax.psum_scatter(
            grad_query.astype(jnp.bfloat16), EXPERT, scatter_dimension=0, tiled=True
        ).astype(jnp.float32),
        lax.psum_scatter(
            grad_expand.astype(jnp.bfloat16), EXPERT, scatter_dimension=0, tiled=True
        ).astype(jnp.float32),
        lax.psum_scatter(
            grad_output.astype(jnp.bfloat16), EXPERT, scatter_dimension=0, tiled=True
        ).astype(jnp.float32),
        lax.psum_scatter(
            grad_shared_gate.astype(jnp.bfloat16), EXPERT, scatter_dimension=0, tiled=True
        ).astype(jnp.float32),
        lax.psum_scatter(
            grad_shared_up.astype(jnp.bfloat16), EXPERT, scatter_dimension=0, tiled=True
        ).astype(jnp.float32),
        lax.psum_scatter(
            grad_shared_down.astype(jnp.bfloat16), EXPERT, scatter_dimension=0, tiled=True
        ).astype(jnp.float32),
    )
    grad_latent, grad_router, grad_norm_attn, grad_norm_moe, grad_norm_latent = (
        lax.psum_scatter(grad_latent, (EXPERT, TENSOR), scatter_dimension=0, tiled=True),
        lax.psum_scatter(grad_router, (EXPERT, TENSOR), scatter_dimension=0, tiled=True),
        lax.psum_scatter(grad_norm_attn, (EXPERT, TENSOR), scatter_dimension=0, tiled=True),
        lax.psum_scatter(grad_norm_moe, (EXPERT, TENSOR), scatter_dimension=0, tiled=True),
        lax.psum_scatter(grad_norm_latent, (EXPERT, TENSOR), scatter_dimension=0, tiled=True),
    )
    return (
        output,
        grad_inputs,
        grad_norm_attn,
        grad_query,
        grad_latent,
        grad_norm_latent,
        grad_expand,
        grad_output,
        grad_norm_moe,
        grad_router,
        grad_shared_gate,
        grad_shared_up,
        grad_shared_down,
        grad_expert_gate,
        grad_expert_up,
        grad_expert_down,
    )


PLANES = 4


def send_core(values):
    return lax.ppermute(values, TENSOR, [(0, 1), (1, 0)])


def chip_pairs(move):
    chips = [(z, y, x) for z in range(PLANES) for y in range(2) for x in range(2)]
    moved = [move(*chip) for chip in chips]
    return [tuple((z * 2 + y) * 2 + x for z, y, x in pair) for pair in zip(chips, moved)]


def send_x(values):
    return lax.ppermute(values, EXPERT, chip_pairs(lambda z, y, x: (z, y, 1 - x)))


def send_y(values):
    return lax.ppermute(values, EXPERT, chip_pairs(lambda z, y, x: (z, 1 - y, x)))


def product(form, left, right):
    return jnp.einsum(form, left, right, preferred_element_type=jnp.float32)


EXTRA = 128
VMEM_LIMIT = 54 << 20
MESH = pl.DeviceIdType.MESH


def dot(left, right):
    return jnp.dot(left, right, preferred_element_type=jnp.float32)


def dot_nt(left, right):
    return lax.dot_general(
        left, right, (((1,), (1,)), ((), ())), preferred_element_type=jnp.float32
    )


def dot_tn(left, right):
    return lax.dot_general(
        left, right, (((0,), (0,)), ((), ())), preferred_element_type=jnp.float32
    )


class Chips:
    def __init__(self):
        index = lax.axis_index(EXPERT)
        self.z, self.y, self.x = index // 4, (index // 2) % 2, index % 2
        self.core = lax.axis_index(TENSOR)
        self.to_x = {EXPERT: self.at(self.z, self.y, 1 - self.x)}
        self.to_y = {EXPERT: self.at(self.z, 1 - self.y, self.x)}
        self.to_core = {TENSOR: 1 - self.core}

    def at(self, z, y, x):
        return (z * 2 + y) * 2 + x

    def to_z(self, distance):
        return {EXPERT: self.at((self.z + distance) % PLANES, self.y, self.x)}

    def places(self, step):
        plane = (self.z + PLANES - step) % PLANES
        x, y = self.x, self.y
        return [
            self.at(plane, row, column)
            for row, column in ((y, x), (y, 1 - x), (1 - y, x), (1 - y, 1 - x))
        ]


def greet(partners):
    barrier = pltpu.get_barrier_semaphore()
    for partner in partners:
        pl.semaphore_signal(barrier, inc=1, device_id=partner, device_id_type=MESH)
    pl.semaphore_wait(barrier, len(partners))


def add_rows(target, terms):
    @pl.loop(0, target.shape[0] // 16)
    def _(chunk):
        rows = pl.ds(pl.multiple_of(chunk * 16, 16), 16)
        total = terms[0][rows, :].astype(jnp.float32)
        for term in terms[1:]:
            total = total + term[rows, :].astype(jnp.float32)
        target[rows, :] = total.astype(target.dtype)


def sum_kernel(parts, exchanged, *refs):
    chips = Chips()
    refs = list(refs)
    arrays = 1 + max(part[0] for part in parts)
    kind_of = {part[0]: part[1] for part in parts}
    sources = [[refs.pop(0) for _ in range(2 if kind_of[a] == 2 else 1)] for a in range(arrays)]
    blocks = refs.pop(0) if exchanged else None
    results = [refs.pop(0) for _ in range(arrays)]
    arrived = refs.pop(0) if exchanged else None
    boxes = []
    for _, kind, _, _, _ in parts:
        mine = refs.pop(0)
        from_core = refs.pop(0) if kind else None
        boxes.append((mine, from_core) + tuple(refs.pop(0) for _ in range(4)))
    if exchanged:
        by_x, by_y, x_send, x_recv, z_send, z_recv = [refs.pop(0) for _ in range(6)]
    load_sem, send_sem, recv_sem = refs
    each = list(range(len(parts)))

    def copy_to(source, target, send, recv, to):
        return pltpu.make_async_remote_copy(
            src_ref=source,
            dst_ref=target,
            send_sem=send,
            recv_sem=recv,
            device_id=to,
            device_id_type=MESH,
        )

    def remote(part, step, index, source, target, to):
        sems = (send_sem.at[part, step, index], recv_sem.at[part, step, index])
        return copy_to(source, target, *sems, to)

    def loads(part, step):
        array, kind, start, stop, _ = parts[part]
        mine, source = boxes[part][0], sources[array]
        for k, place in enumerate(chips.places(step)):
            if kind == 2:
                block = source[0].at[step, k, :, start:stop]
            elif kind == 1:
                block = source[0].at[place, chips.core, :, start:stop]
            else:
                block = source[0].at[place, :, start:stop]
            yield pltpu.make_async_copy(block, mine.at[step, k], load_sem.at[part, step, k])

    def core_copies(part, step):
        array, kind, start, stop, _ = parts[part]
        if kind == 0:
            return
        for k, place in enumerate(chips.places(step)):
            if kind == 2:
                block = sources[array][1].at[step, k, :, start:stop]
            else:
                block = sources[array][0].at[place, 1 - chips.core, :, start:stop]
            target = boxes[part][1].at[step, k]
            yield remote(part, step, k, block, target, chips.to_core)

    def level(part, step):
        return 0 if parts[part][4] else step

    def corner_copies(part, step):
        mine, _, corners = boxes[part][:3]
        half = mine.shape[2] // 2
        here = corners.at[level(part, step)]
        yield remote(part, step, 4, mine.at[step, 3, :half], here.at[0], chips.to_y)
        yield remote(part, step, 5, mine.at[step, 3, half:], here.at[1], chips.to_x)

    def early_copies(part, step):
        mine, from_x, from_y = boxes[part][0], boxes[part][3], boxes[part][4]
        half = mine.shape[2] // 2
        x, y = from_x.at[level(part, step)], from_y.at[level(part, step)]
        yield remote(part, step, 6, mine.at[step, 1, half:], x.at[half:], chips.to_x)
        yield remote(part, step, 7, mine.at[step, 2, :half], y.at[:half], chips.to_y)

    def late_copies(part, step):
        mine, from_x, from_y = boxes[part][0], boxes[part][3], boxes[part][4]
        half = mine.shape[2] // 2
        x, y = from_x.at[level(part, step)], from_y.at[level(part, step)]
        yield remote(part, step, 9, mine.at[step, 1, :half], x.at[:half], chips.to_x)
        yield remote(part, step, 10, mine.at[step, 2, half:], y.at[half:], chips.to_y)

    def side_copies(part, step):
        return [*early_copies(part, step), *late_copies(part, step)]

    def z_copy(part, step):
        mine, from_z = boxes[part][0], boxes[part][5]
        source = mine.at[step] if parts[part][4] else mine.at[step, 0]
        return remote(part, step, 8, source, from_z.at[step - 1], chips.to_z(1))

    def x_copy():
        return copy_to(
            blocks.at[:, :, 1 - chips.x], by_x, x_send.at[0], x_recv.at[0], chips.to_x
        )

    def y_copies():
        own = blocks.at[:, 1 - chips.y, chips.x]
        passed = by_x.at[:, 1 - chips.y]
        return [
            copy_to(source, by_y.at[k], x_send.at[1 + k], x_recv.at[1 + k], chips.to_y)
            for k, source in enumerate((own, passed))
        ]

    def gathered(plane):
        return [
            blocks.at[plane, chips.y, chips.x],
            by_x.at[plane, chips.y],
            by_y.at[0, plane],
            by_y.at[1, plane],
        ]

    def z_sends(distance):
        plane = (chips.z + distance) % PLANES
        return [
            copy_to(
                source,
                arrived.at[place],
                z_send.at[distance, k],
                z_recv.at[distance, k],
                chips.to_z(distance),
            )
            for k, (source, place) in enumerate(zip(gathered(plane), chips.places(0)))
        ]

    def z_arrivals(distance):
        plane = (chips.z + distance) % PLANES
        return [
            copy_to(
                source,
                arrived.at[place],
                z_send.at[distance, k],
                z_recv.at[distance, k],
                chips.to_z(distance),
            )
            for k, (source, place) in enumerate(zip(gathered(plane), chips.places(distance)))
        ]

    def keeps():
        return [
            pltpu.make_async_copy(source, arrived.at[place], z_send.at[0, k])
            for k, (source, place) in enumerate(zip(gathered(chips.z), chips.places(0)))
        ]

    order = [*range(1, PLANES), 0]
    distances = range(1, PLANES) if exchanged else (1, PLANES - 1)
    greet([chips.to_x, chips.to_y, chips.to_core] + [chips.to_z(k) for k in distances])
    if exchanged:
        x_copy().start()

    def fetch(step):
        for part in each:
            for copy in core_copies(part, step):
                copy.start()
            for copy in loads(part, step):
                copy.start(priority=1)

    fetch(order[0])
    fetch(order[1])

    def chip_sum(step):
        ahead = order.index(step) + 2
        for part in each:
            mine, from_core = boxes[part][:2]
            for copy in loads(part, step):
                copy.wait()
            for copy in core_copies(part, step):
                copy.wait_recv()
            for k in (3, 1, 2, 0):
                if from_core is not None:
                    add_rows(mine.at[step, k], [mine.at[step, k], from_core.at[step, k]])
                if k == 3 and not parts[part][4]:
                    for copy in corner_copies(part, step):
                        copy.start()
            if not parts[part][4]:
                for copy in early_copies(part, step):
                    copy.start()
        if ahead < PLANES:
            fetch(order[ahead])

    def z_sum(step):
        for part in each:
            if parts[part][4]:
                part_z_sum(part, step)

    def part_z_sum(part, step):
        mine, from_z = boxes[part][0], boxes[part][5]
        if step != 1:
            before = (step - 1) % PLANES
            z_copy(part, before).wait_recv()
            for k in (3, 1, 2, 0):
                add_rows(mine.at[step, k], [mine.at[step, k], from_z.at[before - 1, k]])
        if step:
            z_copy(part, step).start()
        else:
            for copy in [*corner_copies(part, step), *early_copies(part, step)]:
                copy.start()

    def side_sum(step):
        for part in each:
            if parts[part][4] and step:
                continue
            mine, _, corners = boxes[part][:3]
            half = mine.shape[2] // 2
            for copy in corner_copies(part, step):
                copy.wait_recv()
            low_half, high_half = mine.at[step, 1, :half], mine.at[step, 2, half:]
            here = corners.at[level(part, step)]
            add_rows(low_half, [low_half, here.at[0]])
            add_rows(high_half, [high_half, here.at[1]])
            for copy in late_copies(part, step):
                copy.start()

    def plane_sum(step):
        for part in each:
            array, _, start, stop, along_z = parts[part]
            if along_z and step:
                continue
            mine, _, _, from_x, from_y, from_z = boxes[part]
            here = level(part, step)
            terms = [mine.at[step, 0], from_x.at[here], from_y.at[here]]
            for copy in side_copies(part, step):
                copy.wait_recv()
            if step != 1 and not along_z:
                before = (step - 1) % PLANES
                z_copy(part, before).wait_recv()
                terms.append(from_z.at[before - 1])
            if step == 0:
                add_rows(results[array].at[:, start:stop], terms)
            else:
                add_rows(mine.at[step, 0], terms)
                z_copy(part, step).start()

    stages = ((0, chip_sum), (1, side_sum), (0, z_sum), (2, plane_sum))
    for tick in range(PLANES + 2):
        for late, stage in stages:
            if 0 <= tick - late < PLANES:
                stage(order[tick - late])
        if exchanged and tick == 0:
            x_copy().wait_recv()
            for copy in y_copies():
                copy.start()
        if exchanged and tick == 1:
            for copy in y_copies():
                copy.wait_recv()
            for copy in keeps():
                copy.start()
            for distance in range(1, PLANES):
                for copy in z_sends(distance):
                    copy.start()
    if exchanged:
        for copy in [x_copy(), *y_copies()]:
            copy.wait_send()
        for copy in keeps():
            copy.wait()
        for distance in range(1, PLANES):
            for copy in z_arrivals(distance):
                copy.wait_recv()
            for copy in z_sends(distance):
                copy.wait_send()
    for part in each:
        along_z = parts[part][4]
        for step in range(PLANES):
            sent = [*core_copies(part, step)]
            if step == 0 or not along_z:
                sent += [*corner_copies(part, step), *side_copies(part, step)]
            if step:
                sent.append(z_copy(part, step))
            for copy in sent:
                copy.wait_send()


def sum_over_chips(collective_id, arrays, blocks=None):
    low = jnp.bfloat16
    parts, scratch, shapes = [], [], []
    for index, (kind, operands, z_columns) in enumerate(arrays):
        rows, columns = operands[0].shape[-2:]
        shapes.append((rows, columns))
        for start, stop in ((0, columns - z_columns), (columns - z_columns, columns)):
            if start == stop:
                continue
            along_z = start > 0
            parts.append((index, kind, start, stop, along_z))
            size = (rows, stop - start)
            levels = 1 if along_z else PLANES
            scratch += [pltpu.VMEM((PLANES, 4) + size, low)] * (2 if kind else 1)
            scratch += [
                pltpu.VMEM((levels, 2, rows // 2, stop - start), low),
                pltpu.VMEM((levels,) + size, low),
                pltpu.VMEM((levels,) + size, low),
                pltpu.VMEM((PLANES - 1,) + ((4,) if along_z else ()) + size, low),
            ]
    operands = [operand for _, group, _ in arrays for operand in group]
    out_shape = [jax.ShapeDtypeStruct(shape, jnp.float32) for shape in shapes]
    out_specs = [pl.BlockSpec(memory_space=pltpu.VMEM)] * len(shapes)
    if blocks is not None:
        operands.append(blocks)
        block = blocks.shape[3:]
        out_shape.append(jax.ShapeDtypeStruct((PLANES * 4,) + block, low))
        out_specs.append(pl.BlockSpec(memory_space=pl.ANY))
        scratch += [
            pltpu.VMEM((PLANES, 2) + block, low),
            pltpu.VMEM((2, PLANES) + block, low),
            pltpu.SemaphoreType.DMA((3,)),
            pltpu.SemaphoreType.DMA((3,)),
            pltpu.SemaphoreType.DMA((PLANES, 4)),
            pltpu.SemaphoreType.DMA((PLANES, 4)),
        ]
    size = sum(rows * columns for rows, columns in shapes)
    semaphores = (len(parts), PLANES, 11)
    return pl.pallas_call(
        functools.partial(sum_kernel, tuple(parts), blocks is not None),
        in_specs=[pl.BlockSpec(memory_space=pl.ANY)] * len(operands),
        out_specs=out_specs,
        out_shape=out_shape,
        scratch_shapes=scratch
        + [
            pltpu.SemaphoreType.DMA((len(parts), PLANES, 4)),
            pltpu.SemaphoreType.DMA(semaphores),
            pltpu.SemaphoreType.DMA(semaphores),
        ],
        compiler_params=pltpu.CompilerParams(
            collective_id=collective_id, has_side_effects=True, vmem_limit_bytes=VMEM_LIMIT
        ),
        cost_estimate=pl.CostEstimate(
            flops=size * 30, bytes_accessed=size * 64, transcendentals=0
        ),
    )(*operands)


def gated(gate_act, up_act, grad_hidden):
    sigma = jax.nn.sigmoid(gate_act)
    silu = gate_act * sigma
    hidden = silu * up_act
    grad_gate = grad_hidden * up_act * sigma * (1.0 + gate_act * (1.0 - sigma))
    grad_up = grad_hidden * silu
    return tuple(v.astype(jnp.bfloat16) for v in (hidden, grad_gate, grad_up))


def moe_kernel(own_rows_in, lanes, w_gate, w_up, w_down, sw_gate, sw_up, sw_down, *refs):
    near, refs = refs[:3], refs[3:]
    land, out_mine, out_other, grad_mine, grad_other = refs[:5]
    rows_out, pairs_out, hidden_out, gate_out, up_out, shared_out = refs[5:11]
    rows_kept, grads_kept, out_kept, back_kept, extra_kept, s_hidden, s_grads, seats = refs[11:19]
    x_here, g_here, gate_here, up_here, down_here, s_in, s_down, sum_in, sum_down = refs[19:28]
    come, go, fetch, send_sem, recv_sem, z_send, z_recv = refs[28:]
    width, half = s_down.shape
    plane, step = pl.program_id(0), pl.program_id(1)
    experts, slots = out_kept.shape[:2]
    pairs, pair_rows_all, pair_slots = seats.shape
    own = slots // pairs
    low = jnp.bfloat16
    chips = Chips()

    def remote(step, index, source, target, to):
        return pltpu.make_async_remote_copy(
            src_ref=source,
            dst_ref=target,
            send_sem=send_sem.at[step, index],
            recv_sem=recv_sem.at[step, index],
            device_id=to,
            device_id_type=MESH,
        )

    def own_block(step):
        return own_rows_in if isinstance(step, int) and step == 0 else land.at[step, 0, 0]

    def side_copies(step):
        block = own_block(step)
        return [
            remote(step, 0, block, land.at[step, 0, 1], chips.to_x),
            remote(step, 1, block, land.at[step, 0, 2], chips.to_y),
        ]

    def corner_copies(step):
        return [
            remote(step, 2, land.at[step, 0, 1, 0], land.at[step, 0, 3, 0], chips.to_y),
            remote(step, 3, land.at[step, 0, 2, 1], land.at[step, 0, 3, 1], chips.to_x),
        ]

    def core_copy(step, k):
        if k < 3:
            source, target = land.at[step, 0, k] if k else own_block(step), land.at[step, 1, k]
        else:
            source, target = land.at[step, 0, 3, k - 3], land.at[step, 1, 3, k - 3]
        return remote(step, 4 + k, source, target, chips.to_core)

    def z_copy(k):
        return pltpu.make_async_remote_copy(
            src_ref=own_block(k - 1),
            dst_ref=land.at[k, 0, 0],
            send_sem=z_send.at[k],
            recv_sem=z_recv.at[k],
            device_id=chips.to_z(1),
            device_id_type=MESH,
        )

    def near_sides():
        own = own_rows_in.at[0]
        return [
            remote(0, 0, own, land.at[0, 0, 1, 0], chips.to_x),
            remote(0, 1, own, land.at[0, 0, 2, 0], chips.to_y),
        ]

    def near_corners():
        half = land.shape[4] // 2
        ends = (slice(0, half), slice(half, 2 * half))
        return [
            remote(0, 2 + k, land.at[0, 0, 1 + k, 0, rows], land.at[0, 0, 3, 0, rows], to)
            for k, (rows, to) in enumerate(zip(ends, (chips.to_y, chips.to_x)))
        ]

    def near_core(place):
        source = land.at[0, 0, place, 0]
        return remote(0, 4 + place, source, land.at[0, 1, place, 0], chips.to_core)

    def near_cores_at_once():
        own = remote(0, 4, own_rows_in, land.at[0, 1, 0], chips.to_core)
        return [own] + [
            remote(0, 8 + k, near[k], land.at[0, 1, 1 + k, 1], chips.to_core) for k in range(3)
        ]

    def start_plane(step):
        for copy in side_copies(step) + [core_copy(step, 0)]:
            copy.start()

    def pass_corners(step):
        for copy in side_copies(step):
            copy.wait_recv()
        for copy in corner_copies(step) + [core_copy(step, 1), core_copy(step, 2)]:
            copy.start()

    def finish_plane(step):
        for copy in corner_copies(step):
            copy.wait_recv()
        for k in (3, 4):
            core_copy(step, k).start()
        for k in range(5):
            core_copy(step, k).wait_recv()

    def weight_copies(expert):
        return [
            pltpu.make_async_copy(source.at[expert], target.at[expert], fetch.at[expert, k])
            for k, (source, target) in enumerate(
                ((w_gate, gate_here), (w_up, up_here), (w_down, down_here))
            )
        ]

    shared_blocks = sw_gate.shape[1] // half
    chip = chips.at(chips.z, chips.y, chips.x)
    shared_here = chip < shared_blocks

    def shared_copies():
        columns = pl.ds(pl.multiple_of((chip % shared_blocks) * half, half), half)
        return [
            pltpu.make_async_copy(source.at[:, columns], target, fetch.at[experts, k])
            for k, (source, target) in enumerate(
                (
                    (sw_gate, s_in.at[:, :half]),
                    (sw_up, s_in.at[:, half:]),
                    (sw_down, s_down),
                )
            )
        ]

    @pl.when((plane == 0) & (step == 0))
    def _():
        greet(
            [chips.to_x, chips.to_y, chips.to_core, chips.to_z(1), chips.to_z(PLANES - 1)]
        )
        for copy in near_sides() + near_cores_at_once():
            copy.start()
        z_copy(1).start()

        @pl.when(shared_here)
        def _():
            for copy in shared_copies():
                copy.start()

        for expert in range(experts):
            for copy in weight_copies(expert):
                copy.start()
        for copy in near_sides():
            copy.wait_recv()
        for copy in near_corners() + [near_core(1), near_core(2)]:
            copy.start()
        z_copy(1).wait_recv()
        z_copy(2).start()
        start_plane(1)

        @pl.when(shared_here)
        def _():
            for copy in shared_copies():
                copy.wait()

        @pl.when(~shared_here)
        def _():
            s_in[...] = jnp.zeros(s_in.shape, low)
            s_down[...] = jnp.zeros(s_down.shape, low)

        for copy in near_corners():
            copy.wait_recv()
        near_core(3).start()
        for copy in near_cores_at_once() + [near_core(place) for place in (1, 2, 3)]:
            copy.wait_recv()

    def pair_place(pair):
        return pair // (pairs // 2), slice((pair % (pairs // 2)) * 2, (pair % (pairs // 2)) * 2 + 2)

    def coming(pair):
        side, blocks = pair_place(pair)
        return [
            pltpu.make_async_copy(
                land.at[plane, side, blocks, which],
                here.at[2 * pair : 2 * pair + 2],
                come.at[which * pairs + pair],
            )
            for which, here in enumerate((x_here, g_here))
        ]

    def going(pair):
        side, blocks = pair_place(pair)
        return [
            pltpu.make_async_copy(
                here.at[2 * pair : 2 * pair + 2, :, :columns],
                targets[side].at[plane, blocks],
                go.at[which * pairs + pair],
            )
            for which, (targets, here, columns) in enumerate(
                (
                    ((out_mine, out_other), x_here, width),
                    ((grad_mine, grad_other), g_here, width + EXTRA),
                )
            )
        ]

    def pair_rows(here, pair, columns):
        return here[2 * pair : 2 * pair + 2, :, :columns].reshape(pair_rows_all, columns)

    def own_coming():
        rows = [own_rows_in.at[0]] + [land.at[0, 0, place, 0] for place in (1, 2, 3)]
        grads = [own_rows_in.at[1], *near]
        for which, (here, sources) in enumerate(((x_here, rows), (g_here, grads))):
            for block, source in enumerate(sources):
                yield pltpu.make_async_copy(
                    source, here.at[block], come.at[which * pairs + block // 2]
                )

    @pl.when((step == 0) & (plane == 0))
    def _():
        for copy in own_coming():
            copy.start()

    @pl.when((step == 0) & (plane > 0))
    def _():
        for pair in range(pairs // 2):
            for copy in coming(pair):
                copy.start()

    @pl.when(step == 0)
    def _():
        for pair in range(pairs // 2, pairs):
            for copy in coming(pair):
                copy.start()
        tokens = lax.broadcasted_iota(jnp.int32, (pair_rows_all, pair_rows_all), 0)
        others = lax.broadcasted_iota(jnp.int32, (pair_rows_all, pair_rows_all), 1)
        own_rows = pair_rows_all // 2
        earlier = (others < tokens) & ((others >= own_rows) == (tokens >= own_rows))
        earlier = earlier.astype(jnp.float32).astype(low)
        lane = lax.broadcasted_iota(jnp.int32, (pair_rows_all, pair_slots), 1)
        block = lax.broadcasted_iota(jnp.int32, (pair_rows_all, pair_slots), 0) // own_rows
        capacity = own // 2
        at_block = lax.rem(lane // capacity, 2) == block
        at_slot = lax.rem(lane, capacity).astype(jnp.float32)
        for pair in range(pairs):
            for copy in coming(pair):
                copy.wait()
            grads = pair_rows(g_here, pair, width + EXTRA)
            routes = grads[:, width:].astype(jnp.float32)
            named = routes[:, :1] == lanes[:1]
            for k in range(1, TOPK):
                named = named | (routes[:, k : k + 1] == lanes[:1])
            named = named.astype(jnp.float32)
            rank = dot(earlier, named.astype(low))
            seat = jnp.where(at_block & (rank == at_slot), named, 0.0).astype(low)
            seats[pair] = seat
            rows = dot_tn(seat, pair_rows(x_here, pair, width + EXTRA))
            grads = dot_tn(seat, grads[:, :width])
            for expert in range(experts):
                here = slice(expert * own, (expert + 1) * own)
                there = slice(pair * own, (pair + 1) * own)
                low_rows = rows[here, :width].astype(jnp.bfloat16)
                low_grads = grads[here].astype(jnp.bfloat16)
                if expert == 0:
                    rows_out[0, there] = low_rows
                    pairs_out[0, there] = low_grads
                else:
                    rows_kept[expert - 1, there] = low_rows
                    grads_kept[expert - 1, there] = low_grads
                gate = jnp.sum(
                    rows[here, width:] * lanes[1 + expert : 2 + expert], axis=-1, keepdims=True
                )
                extra_kept[expert, there] = jnp.broadcast_to(gate, (own, EXTRA))
        for side in range(2):
            blocks = slice(side * pairs, (side + 1) * pairs)
            tokens = pairs * own_rows
            rows = x_here[blocks, :, :width].reshape(tokens, width)
            grads = g_here[blocks, :, :width].reshape(tokens, width)
            acts = dot(rows, s_in[...])
            hidden, grad_gate, grad_up = gated(
                acts[:, :half], acts[:, half:], dot(grads, s_down[...])
            )
            s_hidden[side * tokens : (side + 1) * tokens] = hidden
            both = jnp.concatenate([grad_gate, grad_up], axis=1)
            s_grads[side * tokens : (side + 1) * tokens] = both
            term_in, term_down = dot_tn(both, rows), dot_tn(hidden, grads)
            if side == 0:
                fresh = plane == 0
                sum_in[...] = jnp.where(fresh, 0.0, sum_in[...]) + term_in
                sum_down[...] = jnp.where(fresh, 0.0, sum_down[...]) + term_down
            else:
                sum_in[...] += term_in
                sum_down[...] += term_down

    @pl.when(step > 0)
    def _():
        rows_out[0] = rows_kept[step - 1]
        pairs_out[0] = grads_kept[step - 1]

    @pl.when(plane == 0)
    def _():
        for copy in weight_copies(step):
            copy.wait()

    rows = rows_out[0]
    grads = pairs_out[0].astype(jnp.float32)
    gates = extra_kept[step][:, :1]
    pair_grads = (grads * gates).astype(jnp.bfloat16)
    hidden, grad_gate, grad_up = gated(
        dot_nt(rows, gate_here[step]), dot_nt(rows, up_here[step]), dot_nt(pair_grads, down_here[step])
    )
    hidden_out[0] = hidden
    gate_out[0] = grad_gate
    up_out[0] = grad_up
    part = dot(hidden, down_here[step])
    out_kept[step] = (part * gates).astype(jnp.bfloat16)
    slot_grad = jnp.sum(part * grads, axis=-1, keepdims=True)
    pairs_out[0] = pair_grads
    high = slot_grad.astype(jnp.bfloat16).astype(jnp.float32)
    lane_row = 1 + experts + step * 2
    extra_kept[step] = high * lanes[pl.ds(lane_row, 1)] + (slot_grad - high) * lanes[
        pl.ds(lane_row + 1, 1)
    ]
    back_kept[step] = (dot(grad_gate, gate_here[step]) + dot(grad_up, up_here[step])).astype(
        jnp.bfloat16
    )

    @pl.when((step == 0) & (plane + 1 < PLANES))
    def _():
        pass_corners(plane + 1)

    @pl.when((step == 0) & (plane + 2 < PLANES))
    def _():
        for k in range(2, PLANES):

            @pl.when(plane == k - 2)
            def _(k=k):
                z_copy(k).wait_recv()
                if k + 1 < PLANES:
                    z_copy(k + 1).start()

        start_plane(plane + 2)

    @pl.when(step == experts - 1)
    def _():
        for pair in range(pairs):
            there = slice(pair * own, (pair + 1) * own)
            tokens = slice(pair * pair_rows_all, (pair + 1) * pair_rows_all)
            here = slice(2 * pair, 2 * pair + 2)
            back = seats[pair]
            total = dot(
                back, jnp.concatenate([out_kept[e, there] for e in range(experts)], 0)
            ) + dot_nt(s_hidden[tokens], s_down[...])
            x_here[here, :, :width] = total.astype(jnp.bfloat16).reshape(2, -1, width)
            total = dot(
                back, jnp.concatenate([back_kept[e, there] for e in range(experts)], 0)
            ) + dot_nt(s_grads[tokens], s_in[...])
            g_here[here, :, :width] = total.astype(jnp.bfloat16).reshape(
                2, -1, width
            )
            extra = jnp.concatenate([extra_kept[e, there] for e in range(experts)], 0)
            total = dot(back, extra.astype(jnp.bfloat16))
            g_here[here, :, width:] = total.astype(jnp.bfloat16).reshape(2, -1, EXTRA)
            for copy in going(pair):
                copy.start()
        for pair in range(pairs):
            for copy in going(pair):
                copy.wait()

    @pl.when((step == experts - 1) & (plane + 1 < PLANES))
    def _():
        finish_plane(plane + 1)

    @pl.when((step == experts - 1) & (plane == PLANES - 1))
    def _():
        block_rows = width // shared_out.shape[0]
        for to in range(shared_out.shape[0]):
            there = slice(to * block_rows, (to + 1) * block_rows)
            shared_out[to, : 2 * half] = sum_in[:, there].astype(low)
            shared_out[to, 2 * half :] = sum_down[:, there].astype(low)
        for k in range(1, PLANES):
            z_copy(k).wait_send()

        near_cores = near_cores_at_once() + [near_core(place) for place in (1, 2, 3)]
        for copy in near_sides() + near_corners() + near_cores:
            copy.wait_send()

        @pl.loop(1, PLANES)
        def _(sent):
            for copy in side_copies(sent) + corner_copies(sent):
                copy.wait_send()
            for k in range(5):
                core_copy(sent, k).wait_send()


def moe_layer(own_rows_in, near, lanes, weights):
    experts, units, width = weights[0].shape
    _, own_rows, wide = own_rows_in.shape
    blocks, pairs, pair_rows, pair_slots = 4, 4, 2 * own_rows, EXTRA
    slots = pairs * pair_slots // experts
    tokens = pairs * pair_rows
    half = EXTRA
    chips = lax.axis_size(EXPERT)
    low = jnp.bfloat16

    def whole(array):
        zeros = (0,) * len(array.shape)
        return pl.BlockSpec(array.shape, lambda s, j: zeros, pipeline_mode=pl.Buffered(1))

    anywhere = pl.BlockSpec(memory_space=pl.ANY)
    land = [jax.ShapeDtypeStruct((PLANES, 2, blocks, 2, own_rows, wide), low)]
    plain = [jax.ShapeDtypeStruct((PLANES, blocks, own_rows, width), low)] * 2
    extended = [jax.ShapeDtypeStruct((PLANES, blocks, own_rows, wide), low)] * 2
    keep = [
        jax.ShapeDtypeStruct((experts, PLANES * slots, columns), low)
        for columns in (width, width, units, units, units)
    ]
    shared = [jax.ShapeDtypeStruct((chips, 3 * half, width // chips), low)]
    operands = [own_rows_in, lanes] + list(weights) + near
    work = 2 * tokens * width * (8 * half + 2 * pair_slots) + 12 * experts * slots * width * units
    results = pl.pallas_call(
        moe_kernel,
        grid=(PLANES, experts),
        in_specs=[anywhere, whole(lanes)] + [anywhere] * (len(weights) + len(near)),
        out_specs=[anywhere] * 5
        + [pl.BlockSpec((1, slots, v.shape[2]), lambda s, j: (j, s, 0)) for v in keep]
        + [whole(v) for v in shared],
        out_shape=land + plain + extended + keep + shared,
        scratch_shapes=[
            pltpu.VMEM((experts - 1, slots, width), low),
            pltpu.VMEM((experts - 1, slots, width), low),
            pltpu.VMEM((experts, slots, width), low),
            pltpu.VMEM((experts, slots, width), low),
            pltpu.VMEM((experts, slots, EXTRA), jnp.float32),
            pltpu.VMEM((tokens, half), low),
            pltpu.VMEM((tokens, 2 * half), low),
            pltpu.VMEM((pairs, pair_rows, pair_slots), low),
            pltpu.VMEM((2 * blocks, own_rows, wide), low),
            pltpu.VMEM((2 * blocks, own_rows, wide), low),
            pltpu.VMEM(weights[0].shape, low),
            pltpu.VMEM(weights[1].shape, low),
            pltpu.VMEM(weights[2].shape, low),
            pltpu.VMEM((width, 2 * half), low),
            pltpu.VMEM((width, half), low),
            pltpu.VMEM((2 * half, width), jnp.float32),
            pltpu.VMEM((half, width), jnp.float32),
            pltpu.SemaphoreType.DMA((2 * pairs,)),
            pltpu.SemaphoreType.DMA((2 * pairs,)),
            pltpu.SemaphoreType.DMA((experts + 1, 3)),
            pltpu.SemaphoreType.DMA((PLANES, 11)),
            pltpu.SemaphoreType.DMA((PLANES, 11)),
            pltpu.SemaphoreType.DMA((PLANES,)),
            pltpu.SemaphoreType.DMA((PLANES,)),
        ],
        compiler_params=pltpu.CompilerParams(
            collective_id=0, has_side_effects=True, vmem_limit_bytes=VMEM_LIMIT
        ),
        cost_estimate=pl.CostEstimate(
            flops=PLANES * work, bytes_accessed=120 << 20, transcendentals=0
        ),
    )(*operands)
    return results[1:3], results[3:5], results[5:]


def expert_grads_kernel(rows, pair_grads, grad_gate, grad_up, hidden, for_gate, for_up, for_down):
    for_gate[0] = dot_tn(grad_gate[0], rows[0])
    for_up[0] = dot_tn(grad_up[0], rows[0])
    for_down[0] = dot_tn(hidden[0], pair_grads[0])


def expert_grads(rows, pair_grads, grad_gate, grad_up, hidden):
    experts, slots, width = rows.shape
    units = hidden.shape[2]
    columns = width // 2
    of_columns = pl.BlockSpec((1, slots, columns), lambda j, c: (j, 0, c))
    of_units = pl.BlockSpec((1, slots, units), lambda j, c: (j, 0, 0))
    grads = pl.pallas_call(
        expert_grads_kernel,
        grid=(experts, width // columns),
        in_specs=[of_columns] * 2 + [of_units] * 3,
        out_specs=[pl.BlockSpec((1, units, columns), lambda j, c: (j, 0, c))] * 3,
        out_shape=[jax.ShapeDtypeStruct((experts, units, width), jnp.float32)] * 3,
        compiler_params=pltpu.CompilerParams(vmem_limit_bytes=VMEM_LIMIT),
        cost_estimate=pl.CostEstimate(
            flops=6 * experts * slots * width * units,
            bytes_accessed=60 << 20,
            transcendentals=0,
        ),
    )(rows, pair_grads, grad_gate, grad_up, hidden)
    return [jnp.swapaxes(grad, 1, 2) for grad in grads]


def per_device_gathered(
    inputs,
    norm_attn,
    w_query,
    w_latent,
    norm_latent,
    w_expand,
    w_output,
    norm_moe,
    w_router,
    w_shared_gate,
    w_shared_up,
    w_shared_down,
    w_expert_gate,
    w_expert_up,
    w_expert_down,
    routes,
    cotangent,
):
    own_rows = inputs.shape[0]
    width = inputs.shape[1]
    tensor_size = lax.axis_size(TENSOR)
    expert_size = lax.axis_size(EXPERT)
    tensor_index = lax.axis_index(TENSOR)
    expert_index = lax.axis_index(EXPERT)
    seq_rows = own_rows * tensor_size
    local_heads = w_query.shape[1] // (NOPE + ROPE)
    experts = w_router.shape[1]
    local_experts = experts // expert_size
    capacity = own_rows * TOPK * 4 // (3 * experts)
    scale = 1.0 / math.sqrt(NOPE + ROPE)

    beside = jnp.pad(routes.astype(jnp.bfloat16), ((0, 0), (0, EXTRA - TOPK)))
    block = jnp.concatenate([cotangent, beside], axis=1)
    from_x, from_y = send_x(block), send_y(block)

    flat_in = inputs.astype(jnp.float32)
    scale_one = lax.rsqrt(jnp.mean(flat_in * flat_in, axis=-1, keepdims=True) + EPS)
    normed_one = flat_in * scale_one
    h_own = (normed_one * norm_attn).astype(jnp.bfloat16)
    compressed = jnp.dot(h_own, w_latent, preferred_element_type=jnp.float32)
    lat_raw = compressed[:, :LATENT]
    scale_lat = lax.rsqrt(jnp.mean(lat_raw * lat_raw, axis=-1, keepdims=True) + EPS)
    normed_lat = lat_raw * scale_lat
    lat_own = (normed_lat * norm_latent).astype(jnp.bfloat16)
    places = jnp.arange(own_rows)
    places_all = jnp.concatenate(
        [tensor_index * own_rows + places, (1 - tensor_index) * own_rows + places]
    )
    cos_own, sin_own = rope_tables(places_all[:own_rows], ROPE)
    rope_own = rotate(compressed[:, LATENT:], cos_own, sin_own).astype(jnp.bfloat16)

    def both(values):
        return jnp.concatenate([values, send_core(values)], axis=0)

    h_all = both(h_own)
    h_all, from_x, from_y = lax.optimization_barrier((h_all, from_x, from_y))
    near = [from_x, from_y, send_y(from_x)]
    lat_rope = both(jnp.concatenate([lat_own, rope_own], axis=1))
    lat_all, rope_all = lat_rope[:, :LATENT], lat_rope[:, LATENT:]
    cos_all, sin_all = rope_tables(places_all, ROPE)
    cos_all = cos_all[:, None, :]
    sin_all = sin_all[:, None, :]
    query_raw = jnp.dot(h_all, w_query, preferred_element_type=jnp.float32).reshape(
        seq_rows, local_heads, NOPE + ROPE
    )
    query = jnp.concatenate(
        [query_raw[..., :NOPE], rotate(query_raw[..., NOPE:], cos_all, sin_all)], axis=-1
    ).astype(jnp.bfloat16)
    expanded = jnp.dot(lat_all, w_expand, preferred_element_type=jnp.float32).astype(jnp.bfloat16)
    expanded = expanded.reshape(seq_rows, local_heads, NOPE + VD)
    key_full = jnp.concatenate(
        [
            expanded[..., :NOPE],
            jnp.broadcast_to(rope_all[:, None, :], (seq_rows, local_heads, ROPE)),
        ],
        axis=-1,
    )
    value = expanded[..., NOPE:]
    allowed = (places_all[:, None] >= places_all[None, :])[None]
    scores = product("qhd,khd->hqk", query, key_full) * scale
    scores = jnp.where(allowed, scores, -1e30)
    weights = jnp.exp(scores - jnp.max(scores, axis=-1, keepdims=True))
    probs = weights / jnp.sum(weights, axis=-1, keepdims=True)
    attended = product("hqk,khd->qhd", probs.astype(jnp.bfloat16), value)
    attended_flat = attended.astype(jnp.bfloat16).reshape(seq_rows, local_heads * VD)
    attended_flat, near = lax.optimization_barrier((attended_flat, near))
    attn_terms = product("sv,dv->sd", attended_flat, w_output)
    after_attn = (
        flat_in
        + attn_terms[:own_rows]
        + send_core(attn_terms[own_rows:].astype(jnp.bfloat16)).astype(jnp.float32)
    )
    scale_two = lax.rsqrt(jnp.mean(after_attn * after_attn, axis=-1, keepdims=True) + EPS)
    normed_two = after_attn * scale_two
    h_moe = (normed_two * norm_moe).astype(jnp.bfloat16)
    logits = jnp.dot(h_moe, w_router, preferred_element_type=jnp.float32)
    expert_ids = jnp.arange(experts, dtype=jnp.int32)
    chosen = jnp.any(routes[:, :, None] == expert_ids[None, None, :], axis=1)
    masked = jnp.where(chosen, logits, -1e30)
    raised = jnp.where(chosen, jnp.exp(masked - jnp.max(masked, axis=-1, keepdims=True)), 0.0)
    gates = raised / jnp.sum(raised, axis=-1, keepdims=True)
    high_gates = lax.reduce_precision(gates, 8, 7)
    beside = [high_gates.astype(jnp.bfloat16), (gates - high_gates).astype(jnp.bfloat16)]
    beside.append(jnp.zeros((own_rows, EXTRA - 2 * experts), jnp.bfloat16))
    own_rows_in = jnp.stack([jnp.concatenate([h_moe, *beside], axis=1), block])

    own_ids = expert_index * local_experts + jnp.arange(local_experts, dtype=jnp.int32)
    lane_ids = jnp.arange(EXTRA, dtype=jnp.int32)[None, :]
    slot_experts = expert_index * local_experts + lane_ids // (2 * capacity)
    gate_lanes = (lane_ids == own_ids[:, None]) | (lane_ids == own_ids[:, None] + experts)
    back_lanes = (own_ids[:, None] * tensor_size + tensor_index) * 2 + jnp.arange(2)[None, :]
    lanes = jnp.concatenate(
        [slot_experts, gate_lanes, lane_ids == back_lanes.reshape(-1, 1)], axis=0
    ).astype(jnp.float32)
    lanes = jnp.pad(lanes, ((0, -lanes.shape[0] % 8), (0, 0)))

    all_weights = tuple(jnp.swapaxes(w, 1, 2) for w in (w_expert_gate, w_expert_up, w_expert_down))
    all_weights += (w_shared_gate, w_shared_up, w_shared_down)
    out_parts, grad_parts, kept = moe_layer(own_rows_in, near, lanes, all_weights)
    shared_grads = kept[5].reshape((PLANES, 2, 2) + kept[5].shape[1:])
    moe_back, moe_out, shared_grads = sum_over_chips(
        1, [(2, grad_parts, 512), (2, out_parts, 512)], shared_grads
    )
    output = (after_attn + moe_out).astype(jnp.bfloat16)

    grad_gates = jnp.sum(moe_back[:, width:].reshape(own_rows, experts, -1), axis=-1)
    grad_gates = jnp.where(chosen, grad_gates, 0.0)
    grad_select = gates * (grad_gates - jnp.sum(gates * grad_gates, axis=-1, keepdims=True))
    grad_logits = grad_select.astype(jnp.bfloat16)
    grad_router = product("td,te->de", h_moe, grad_logits)

    grad_out = cotangent.astype(jnp.float32)
    grad_moe = moe_back[:, :width] + product("te,de->td", grad_logits, w_router)
    grad_mid, grad_norm_moe = norm_back(grad_moe, normed_two, scale_two, norm_moe)
    grad_mid = grad_mid + grad_out
    grad_attn_all = both(grad_mid.astype(jnp.bfloat16))
    grad_output = product("sd,sv->dv", grad_attn_all, attended_flat)
    grad_attended = product("sd,dv->sv", grad_attn_all, w_output)
    grad_attended = grad_attended.astype(jnp.bfloat16).reshape(seq_rows, local_heads, VD)
    grad_probs = product("qhv,khv->hqk", grad_attended, value)
    centre = jnp.sum(probs * grad_probs, axis=-1, keepdims=True)
    grad_scores = (probs * (grad_probs - centre)).astype(jnp.bfloat16)
    grad_query_full = product("hqk,khd->qhd", grad_scores, key_full) * scale
    grad_key_full = product("hqk,qhd->khd", grad_scores, query) * scale
    grad_value = product("hqk,qhv->khv", probs.astype(jnp.bfloat16), grad_attended)
    grad_query_raw = jnp.concatenate(
        [grad_query_full[..., :NOPE], unrotate(grad_query_full[..., NOPE:], cos_all, sin_all)],
        axis=-1,
    )
    grad_query_raw = grad_query_raw.astype(jnp.bfloat16).reshape(
        seq_rows, local_heads * (NOPE + ROPE)
    )
    grad_query = product("sd,sq->dq", h_all, grad_query_raw)
    grad_expanded = jnp.concatenate([grad_key_full[..., :NOPE], grad_value], axis=-1)
    grad_expanded = grad_expanded.astype(jnp.bfloat16).reshape(seq_rows, local_heads * (NOPE + VD))
    grad_expand = product("sl,sk->lk", lat_all, grad_expanded)
    grad_rope_part = jnp.sum(grad_key_full[..., NOPE:], axis=1)
    grad_h_part = product("sq,dq->sd", grad_query_raw, w_query)
    grad_lat_part = product("sk,lk->sl", grad_expanded, w_expand)
    own_side = jnp.concatenate([grad_lat_part, grad_rope_part], axis=1)
    own_side = own_side[:own_rows] + send_core(own_side[own_rows:].astype(jnp.bfloat16)).astype(
        jnp.float32
    )
    grad_h_own = grad_h_part[:own_rows] + send_core(
        grad_h_part[own_rows:].astype(jnp.bfloat16)
    ).astype(jnp.float32)
    grad_lat_raw, grad_norm_latent = norm_back(
        own_side[:, :LATENT], normed_lat, scale_lat, norm_latent
    )
    grad_compressed = jnp.concatenate(
        [grad_lat_raw, unrotate(own_side[:, LATENT:], cos_own, sin_own)], axis=-1
    ).astype(jnp.bfloat16)
    grad_latent = product("td,tc->dc", h_own, grad_compressed)
    grad_h = grad_h_own + product("tc,dc->td", grad_compressed, w_latent)
    grad_in, grad_norm_attn = norm_back(grad_h, normed_one, scale_one, norm_attn)
    grad_inputs = grad_mid + grad_in

    share = width // expert_size
    low_rows = expert_size * share
    own_part = share // tensor_size

    def in_two(values):
        high = lax.reduce_precision(values, 8, 7)
        return jnp.stack([high, values - high], axis=-1)

    gains = in_two(grad_norm_latent).reshape(expert_size * tensor_size, -1, 2)
    gain_rows = gains.shape[1]
    gains = jnp.pad(gains, ((0, 0), (0, own_part - gain_rows), (0, 0))).reshape(low_rows, 2)
    small = jnp.concatenate(
        [grad_router, in_two(grad_norm_attn), in_two(grad_norm_moe), gains], axis=1
    )
    small = jnp.pad(small, ((0, 0), (0, EXTRA - small.shape[1])))
    small, grad_latent = [
        v.astype(jnp.bfloat16).reshape(expert_size, tensor_size, own_part, -1)
        for v in (small, grad_latent)
    ]
    grad_output = grad_output.astype(jnp.bfloat16).reshape(expert_size, share, -1)
    grad_query = grad_query.astype(jnp.bfloat16).reshape(expert_size, share, -1)
    grad_expand = grad_expand.astype(jnp.bfloat16).reshape(expert_size, -1, w_expand.shape[1])
    grad_output, grad_query, grad_expand, grad_latent, small = sum_over_chips(
        2,
        [
            (0, [grad_output], 256),
            (0, [grad_query], 384),
            (0, [grad_expand], 512),
            (1, [grad_latent], 0),
            (1, [small], 0),
        ],
    )
    grad_router = small[:, :experts]
    grad_norm_attn = small[:, experts] + small[:, experts + 1]
    grad_norm_moe = small[:, experts + 2] + small[:, experts + 3]
    grad_norm_latent = (small[:, experts + 4] + small[:, experts + 5])[:gain_rows]

    rows, pair_grads, hidden, grad_gate, grad_up = kept[:5]
    grad_expert_gate, grad_expert_up, grad_expert_down = expert_grads(
        rows, pair_grads, grad_gate, grad_up, hidden
    )
    columns = w_shared_gate.shape[1]
    shared_grads = shared_grads[: columns // EXTRA].reshape(-1, 3, EXTRA, share)
    shared_grads = (
        jnp.transpose(shared_grads, (1, 3, 0, 2)).reshape(3, share, columns).astype(jnp.float32)
    )
    return (
        output,
        grad_inputs,
        grad_norm_attn,
        grad_query,
        grad_latent,
        grad_norm_latent,
        grad_expand,
        grad_output,
        grad_norm_moe,
        grad_router,
        shared_grads[0],
        shared_grads[1],
        shared_grads[2],
        grad_expert_gate,
        grad_expert_up,
        grad_expert_down,
    )


def per_device_for(mesh):
    if mesh.shape[EXPERT] == PLANES * 4 and mesh.shape[TENSOR] == 2:
        return per_device_gathered
    return per_device_exchanged


def solution(mesh):
    return jax.shard_map(
        per_device_for(mesh),
        mesh=mesh,
        in_specs=(
            P((EXPERT, TENSOR), None),
            P(),
            P(None, TENSOR),
            P(),
            P(),
            P(None, TENSOR),
            P(None, TENSOR),
            P(),
            P(),
            P(None, TENSOR),
            P(None, TENSOR),
            P(None, TENSOR),
            P(EXPERT, None, TENSOR),
            P(EXPERT, None, TENSOR),
            P(EXPERT, None, TENSOR),
            P((EXPERT, TENSOR), None),
            P((EXPERT, TENSOR), None),
        ),
        out_specs=(
            P((EXPERT, TENSOR), None),
            P((EXPERT, TENSOR), None),
            P((EXPERT, TENSOR)),
            P(EXPERT, TENSOR),
            P((EXPERT, TENSOR), None),
            P((EXPERT, TENSOR)),
            P(EXPERT, TENSOR),
            P(EXPERT, TENSOR),
            P((EXPERT, TENSOR)),
            P((EXPERT, TENSOR), None),
            P(EXPERT, TENSOR),
            P(EXPERT, TENSOR),
            P(EXPERT, TENSOR),
            P(EXPERT, None, TENSOR),
            P(EXPERT, None, TENSOR),
            P(EXPERT, None, TENSOR),
        ),
        check_vma=False,
    )
```
